32 devices in a mesh: groups: 2 (over y), tensor: 4 (over z), dp: 4 (over x, core).
Axes of the slice: x: 2, y: 2, z: 4, core: 2. Of those that a mesh axis runs over, the one named last changes fastest.
Arguments:
- acts: bfloat16 [32, 256, 8192], P(('groups', 'dp'), None, 'tensor'), parts along dimension 0, may hold values from -30 to 30
- grads: bfloat16 [2, 32, 256, 28672], P(None, ('groups', 'dp'), None, 'tensor'), parts along dimension 1, may hold values from -30 to 30
- proj_in: bfloat16 [2, 64, 8192], P(None, None, 'tensor'), may hold values from -0.0625 to 0.0625
- proj_out: bfloat16 [2, 64, 28672], P(None, None, 'tensor'), may hold values from -0.03125 to 0.03125
- queries: bfloat16 [64, 2, 64, 64], P('dp'), may hold values from -1.1953125 to 1.1953125
Outputs:
- scores: float32 [32, 64], P(('groups', 'dp')), parts along dimension 0
The draws below stay inside these ranges and needn't reach their ends.
There are 2 independent parts, one for each index of `groups`. The reference program is written for one: setup_inputs(seed, part) draws one part's arguments, and reference() takes and returns one part's arrays. A program takes and returns all parts, laid end to end along the dimension named above; an argument that names none is the same for every part. Nothing has to cross between parts.
All inputs are finite; a program needn't handle non-finite values.
Results may differ from the reference program's by a relative error of at most 0.003.
The reference program's roundings to bfloat16 on the way (of `precond` and `sample_b`) count: a program that leaves them out, or rounds other values in their place, can miss the bound.
Values may be sent and summed in bfloat16 or wider, within the bound.
No kernel may reach another device: no remote copies, remote signals or barrier semaphores. Data moves between devices by JAX's collectives and lax.ppermute only.
A program may use at most 128 MiB of HBM per device.

```python
import math
import jax
import jax.numpy as jnp
from jax import lax

D = 8192
FF = 28672
RANK = 64
LEN = 256
SEQS = 16
QUERIES = 64


def shaped(key, shape, width_axis, seq_axis):
    keys = jax.random.split(key, 3)
    base = jax.random.normal(keys[0], shape, jnp.float32)
    col_shape = [1] * len(shape)
    col_shape[width_axis] = shape[width_axis]
    cols = jnp.exp(jax.random.uniform(keys[1], tuple(col_shape), jnp.float32, -1.15, 1.15))
    row_shape = list(shape)
    row_shape[width_axis] = 1
    rows = jnp.exp(jax.random.uniform(keys[2], tuple(row_shape), jnp.float32, -0.7, 0.7))
    seq_shape = [1] * len(shape)
    seq_shape[seq_axis] = shape[seq_axis]
    ramp = jnp.arange(shape[seq_axis], dtype=jnp.float32) / shape[seq_axis]
    seqs = jnp.exp(math.log(3.0) * ramp).reshape(seq_shape) * 0.6
    return jnp.clip(base * cols * rows * seqs, -30.0, 30.0)


def draw_acts(key, part):
    key = jax.random.fold_in(key, 11)
    return shaped(key, (SEQS, LEN, D), 2, 0).astype(jnp.bfloat16)


def draw_grads(key, part):
    key = jax.random.fold_in(key, 23)
    return shaped(key, (2, SEQS, LEN, FF), 3, 1).astype(jnp.bfloat16)


def levels(own_key, dims, cuts, least, high):
    factor_of, own = 1.0, jax.random.fold_in(own_key, 6)
    for position, shards_of in cuts:
        heights = jnp.exp(jax.random.uniform(jax.random.fold_in(own, position), (shards_of,), jnp.float32, least / len(cuts), high / len(cuts)))
        factor_of = factor_of * jnp.repeat(heights, dims[position] // shards_of).reshape([-1 if axis == position else 1 for axis in range(len(dims))])
    return factor_of


def gaussian(key, shape, scale, bound, cuts=(), kind=jnp.bfloat16):
    values = jax.random.normal(key, shape, jnp.float32) * scale
    if len(cuts) > 0:
        values = levels(key, shape, cuts, -0.22, 0.18) * values
    return jnp.clip(values, min=-bound, max=bound).astype(kind)


def setup_inputs(seed: int = 0, part: int = 0) -> dict:
    arg_keys = jax.random.split(jax.random.key(seed), 6)
    own_keys = jax.random.split(jax.random.fold_in(arg_keys[5], part), 6)
    return {
        "acts": draw_acts(jax.random.fold_in(jax.random.fold_in(arg_keys[5], part), 71), part),
        "grads": draw_grads(jax.random.fold_in(jax.random.fold_in(arg_keys[5], part), 71), part),
        "proj_in": gaussian(arg_keys[2], (2, RANK, D), D ** -0.5, 0.0625, ((2, 4),)),
        "proj_out": gaussian(arg_keys[3], (2, RANK, FF), FF ** -0.5, 0.03125, ((2, 4),)),
        "queries": gaussian(arg_keys[4], (QUERIES, 2, RANK, RANK), 0.2, 1.1953125, ((0, 4),)),
    }


def damp(matrix):
    size = matrix.shape[0]
    shift = 0.1 * jnp.trace(matrix) / size
    return matrix + shift * jnp.eye(size, dtype=matrix.dtype)

def precondition(query, left, right):
    count = query.shape[0]
    left_b = jnp.broadcast_to(left, (count,) + left.shape)
    right_b = jnp.broadcast_to(right, (count,) + right.shape)
    middle = jnp.linalg.solve(left_b, query)
    result = jnp.linalg.solve(right_b, jnp.swapaxes(middle, 1, 2))
    return jnp.swapaxes(result, 1, 2)

def reference(acts, grads, proj_in, proj_out, queries):
    flat = acts.reshape(-1, D)
    xin = jnp.dot(flat.astype(jnp.float32), proj_in.reshape(2 * RANK, D).T.astype(jnp.float32), preferred_element_type=jnp.float32)
    gout = jnp.concatenate([jnp.dot(grads[0].reshape(-1, FF).astype(jnp.float32), proj_out[0].T.astype(jnp.float32), preferred_element_type=jnp.float32), jnp.dot(grads[1].reshape(-1, FF).astype(jnp.float32), proj_out[1].T.astype(jnp.float32), preferred_element_type=jnp.float32)], axis=1)
    total = SEQS * LEN
    cov_in = jnp.dot(xin.T, xin, precision=lax.Precision.HIGHEST) / total
    cov_out = jnp.dot(gout.T, gout, precision=lax.Precision.HIGHEST) / total
    whole = jnp.einsum('sto,sti->soi', gout.reshape(SEQS, LEN, 2 * RANK), xin.reshape(SEQS, LEN, 2 * RANK), precision=lax.Precision.HIGHEST) / LEN
    layers = []
    precond = []
    for layer in range(2):
        low = layer * RANK
        layers.append(whole[:, low:low + RANK, low:low + RANK])
        damped_in = damp(cov_in[low:low + RANK, low:low + RANK])
        damped_out = damp(cov_out[low:low + RANK, low:low + RANK])
        precond.append(precondition(queries[:, layer].astype(jnp.float32), damped_out, damped_in))
    sample_b = jnp.stack(layers, axis=1).astype(jnp.bfloat16).reshape(SEQS, -1)
    query_b = jnp.stack(precond, axis=1).astype(jnp.bfloat16).reshape(QUERIES, -1)
    return jnp.dot(sample_b.astype(jnp.float32), query_b.T.astype(jnp.float32), preferred_element_type=jnp.float32)
```

```python
import functools

import jax
import jax.numpy as jnp
from jax import lax
from jax.experimental import pallas as pl
from jax.experimental.pallas import tpu as pltpu
from jax.sharding import PartitionSpec as P

HIGHEST = lax.Precision.HIGHEST
MIB = 1024 * 1024


def nt(a, b, precision=None):
    return lax.dot_general(
        a, b, (((1,), (1,)), ((), ())), precision=precision, preferred_element_type=jnp.float32
    )


def tn(a, b, precision=None):
    return lax.dot_general(
        a, b, (((0,), (0,)), ((), ())), precision=precision, preferred_element_type=jnp.float32
    )


def nn(a, b, precision=None):
    return jnp.dot(a, b, precision=precision, preferred_element_type=jnp.float32)


def vmem():
    return pl.BlockSpec(memory_space=pltpu.VMEM)


def smem():
    return pl.BlockSpec(memory_space=pltpu.SMEM)


def emit(where_ref, outs, acc):
    count = len(outs)
    for k, out in enumerate(outs):
        out[...] = acc[lax.rem(where_ref[0] + k, count)]


def project_in_kernel(where_ref, acts_ref, proj_ref, *rest):
    outs, acc = rest[:-1], rest[-1]
    step = pl.program_id(0)
    seqs, length, width = acts_ref.shape
    both = proj_ref.shape[0] * proj_ref.shape[1]
    part = nt(acts_ref[...].reshape(seqs * length, width), proj_ref[...].reshape(both, width))
    part = part.reshape(seqs, length, both)

    @pl.when(step == 0)
    def _():
        acc[...] = part

    @pl.when(step > 0)
    def _():
        acc[...] += part

    @pl.when(step == pl.num_programs(0) - 1)
    def _():
        emit(where_ref, outs, acc)


def project_out_kernel(where_ref, grads_ref, proj_ref, *rest):
    outs, acc = rest[:-1], rest[-1]
    step = pl.program_id(0)
    _, seqs, length, width = grads_ref.shape
    rank = proj_ref.shape[1]
    none = jnp.zeros((rank, width), proj_ref.dtype)
    first = jnp.concatenate([proj_ref[0], none], axis=0)
    second = jnp.concatenate([none, proj_ref[1]], axis=0)
    part = nt(grads_ref[0].reshape(seqs * length, width), first)
    part = part + nt(grads_ref[1].reshape(seqs * length, width), second)
    part = part.reshape(seqs, length, 2 * rank)

    @pl.when(step == 0)
    def _():
        acc[...] = part

    @pl.when(step > 0)
    def _():
        acc[...] += part

    @pl.when(step == pl.num_programs(0) - 1)
    def _():
        emit(where_ref, outs, acc)


def project_in(where, acts, proj):
    seqs, length, width = acts.shape
    rank = proj.shape[1]
    block = 512
    return pl.pallas_call(
        project_in_kernel,
        grid=(width // block,),
        in_specs=[
            smem(),
            pl.BlockSpec((seqs, length, block), lambda i: (0, 0, i)),
            pl.BlockSpec((2, rank, block), lambda i: (0, 0, i)),
        ],
        out_specs=[pl.BlockSpec((length, 2 * rank), lambda i: (0, 0))] * seqs,
        out_shape=[jax.ShapeDtypeStruct((length, 2 * rank), jnp.float32)] * seqs,
        scratch_shapes=[pltpu.VMEM((seqs, length, 2 * rank), jnp.float32)],
        compiler_params=pltpu.CompilerParams(vmem_limit_bytes=24 * MIB),
        name="project_in",
    )(where, acts, proj)


def project_out(where, grads, proj):
    _, seqs, length, width = grads.shape
    rank = proj.shape[1]
    block = 512
    return pl.pallas_call(
        project_out_kernel,
        grid=(width // block,),
        in_specs=[
            smem(),
            pl.BlockSpec((2, seqs, length, block), lambda i: (0, 0, 0, i)),
            pl.BlockSpec((2, rank, block), lambda i: (0, 0, i)),
        ],
        out_specs=[pl.BlockSpec((length, 2 * rank), lambda i: (0, 0))] * seqs,
        out_shape=[jax.ShapeDtypeStruct((length, 2 * rank), jnp.float32)] * seqs,
        scratch_shapes=[pltpu.VMEM((seqs, length, 2 * rank), jnp.float32)],
        compiler_params=pltpu.CompilerParams(vmem_limit_bytes=24 * MIB),
        name="project_out",
    )(where, grads, proj)


def left_lanes(rows, lanes):
    return lax.broadcasted_iota(jnp.int32, (rows, lanes), 1) < lanes // 2


def side_by_side(whole):
    size = whole.shape[0]
    half = size // 2
    return jnp.where(left_lanes(half, size), whole[:half], whole[half:])


def block_diagonal(pair):
    left = left_lanes(*pair.shape)
    return jnp.concatenate([jnp.where(left, pair, 0.0), jnp.where(left, 0.0, pair)], axis=0)


def total(pieces):
    value = pieces[0][...]
    for piece in pieces[1:]:
        value = value + piece[...]
    return value


def cov_in_kernel(*refs):
    pieces, (x_out, cov_out) = refs[:-2], refs[-2:]
    x = total(pieces)
    x_out[...] = x
    cov_out[...] = side_by_side(tn(x, x, HIGHEST))


def cov_in(pieces):
    length, both = pieces[0].shape
    return pl.pallas_call(
        cov_in_kernel,
        in_specs=[vmem()] * len(pieces),
        out_specs=[vmem()] * 2,
        out_shape=[
            jax.ShapeDtypeStruct((length, both), jnp.float32),
            jax.ShapeDtypeStruct((both // 2, both), jnp.float32),
        ],
        compiler_params=pltpu.CompilerParams(vmem_limit_bytes=8 * MIB),
        name="cov_in",
    )(*pieces)


def cov_out_kernel(length, x_ref, *refs):
    pieces, (cov_out, sample_out) = refs[:-2], refs[-2:]
    x = x_ref[...]
    g = total(pieces)
    cov_out[...] = side_by_side(tn(g, g, HIGHEST))
    sample = tn(x, g, HIGHEST) / length
    sample_out[...] = side_by_side(sample).astype(jnp.bfloat16)


def cov_out(x, pieces):
    length, both = x.shape
    return pl.pallas_call(
        functools.partial(cov_out_kernel, length),
        in_specs=[vmem()] * (1 + len(pieces)),
        out_specs=[vmem()] * 2,
        out_shape=[
            jax.ShapeDtypeStruct((both // 2, both), jnp.float32),
            jax.ShapeDtypeStruct((both // 2, both), jnp.bfloat16),
        ],
        compiler_params=pltpu.CompilerParams(vmem_limit_bytes=8 * MIB),
        name="cov_out",
    )(x, *pieces)


def ordered_sum_kernel(where_ref, *refs):
    pieces, (out, slots) = refs[:-2], refs[-2:]
    count = len(pieces)
    for k, piece in enumerate(pieces):
        slots[lax.rem(where_ref[0] + count - k, count)] = piece[...]
    value = slots[0]
    for k in range(1, count):
        value = value + slots[k]
    out[...] = value


def ordered_sum(where, pieces):
    shape = pieces[0].shape
    return pl.pallas_call(
        ordered_sum_kernel,
        in_specs=[smem()] + [vmem()] * len(pieces),
        out_specs=vmem(),
        out_shape=jax.ShapeDtypeStruct(shape, jnp.float32),
        scratch_shapes=[pltpu.VMEM((len(pieces),) + shape, jnp.float32)],
        compiler_params=pltpu.CompilerParams(vmem_limit_bytes=8 * MIB),
        name="ordered_sum",
    )(where, *pieces)


def scales(steps, spread):
    r = (spread - 1.0) / (spread + 1.0)
    out = []
    for _ in range(steps):
        out.append(2.0 / (2.0 - r * r))
        r = r * r / (2.0 - r * r)
    return out


def damped_inverse(pair, tokens):
    size = pair.shape[0]
    whole = block_diagonal(pair / tokens)
    rows = lax.broadcasted_iota(jnp.int32, whole.shape, 0)
    cols = lax.broadcasted_iota(jnp.int32, whole.shape, 1)
    diagonal = rows == cols
    on_diagonal = jnp.where(diagonal, whole, 0.0)
    first = jnp.sum(on_diagonal[:size]) / size
    second = jnp.sum(on_diagonal[size:]) / size
    unit = jnp.where(rows < size, first, second)
    eye = jnp.where(diagonal, 1.0, 0.0)
    matrix = whole / unit + 0.1 * eye
    low, high = 0.1, size + 0.1
    start = 2.0 / (low + high)
    steps = scales(7, high / low)
    y = matrix * start
    x = (2.0 * start * steps[0]) * eye - (start * steps[0]) * y
    y = steps[0] * (2.0 * y - nn(y, y, HIGHEST))
    for scale in steps[1:-1]:
        both = nn(jnp.concatenate([x, y], axis=0), y, HIGHEST)
        x = scale * (2.0 * x - both[: 2 * size])
        y = scale * (2.0 * y - both[2 * size :])
    x = steps[-1] * (2.0 * x - nn(x, y, HIGHEST))
    x = x + nn(x, eye - nn(matrix, x, HIGHEST), HIGHEST)
    return x / unit


def split(value):
    high = value.astype(jnp.bfloat16)
    rest = value - high.astype(jnp.float32)
    middle = rest.astype(jnp.bfloat16)
    low = (rest - middle.astype(jnp.float32)).astype(jnp.bfloat16)
    return high, middle, low


def right_kernel(tokens, *refs):
    pieces, (queries_ref, out) = refs[:-2], refs[-2:]
    inverse = damped_inverse(total(pieces), tokens)
    size = inverse.shape[0] // 2
    count = queries_ref.shape[0]
    parts = jnp.concatenate(split(inverse), axis=0)
    group = 4
    for layer in range(2):
        low = layer * size
        left = jnp.concatenate(
            [
                parts[2 * size * k + low : 2 * size * k + low + size, low : low + size]
                for k in range(3)
            ],
            axis=0,
        )
        for block in range(count // group):
            first = block * group // 2
            places = [first, first + count // 2, first + 1, first + 1 + count // 2]
            rows = jnp.concatenate([queries_ref[place, layer] for place in places], axis=0)
            result = nt(left, rows)
            result = result[:size] + result[size : 2 * size] + result[2 * size :]
            high, middle, _ = split(result)
            lanes = slice(block * group * size, (block + 1) * group * size)
            out[layer, 0, :, lanes] = high
            out[layer, 1, :, lanes] = middle


def right(pieces, queries, tokens):
    count, layers, rank, _ = queries.shape
    return pl.pallas_call(
        functools.partial(right_kernel, tokens),
        in_specs=[vmem()] * (len(pieces) + 1),
        out_specs=vmem(),
        out_shape=jax.ShapeDtypeStruct((layers, 2, rank, count * rank), jnp.bfloat16),
        compiler_params=pltpu.CompilerParams(vmem_limit_bytes=24 * MIB),
        name="right",
    )(*pieces, queries)


def score_kernel(tokens, seqs, where_ref, half_ref, *refs):
    pieces, samples, (out, slots) = refs[: -2 - seqs], refs[-2 - seqs : -2], refs[-2:]
    inverse = damped_inverse(total(pieces), tokens)
    both = inverse.shape[0]
    size = both // 2
    pairs = half_ref.shape[3] // both
    for k, sample in enumerate(samples):
        slots[lax.rem(where_ref[0] + seqs - k, seqs)] = sample[...].astype(jnp.float32)
    left = left_lanes(size, both)
    sums = [[None] * pairs for _ in range(seqs)]
    for layer in range(2):
        block = inverse[layer * size : (layer + 1) * size]
        other = pltpu.roll(block, size, 1)
        if layer == 0:
            twice = jnp.concatenate([block, other], axis=0)
        else:
            twice = jnp.concatenate([other, block], axis=0)
        high, middle, _ = split(twice)
        once = jnp.concatenate([high, middle], axis=1)
        weights = jnp.concatenate([once, once], axis=0)
        doubled = []
        for s in range(seqs):
            sample = slots[s]
            turned = pltpu.roll(sample, size, 1)
            keep = left if layer == 0 else jnp.logical_not(left)
            doubled.append(jnp.where(keep, sample, turned))
        for pair in range(pairs):
            lanes = slice(pair * both, (pair + 1) * both)
            rows = jnp.concatenate([half_ref[layer, 0, :, lanes], half_ref[layer, 1, :, lanes]], axis=1)
            result = nn(rows, weights)
            result = (result[:, :both] + result[:, both:]).astype(jnp.bfloat16).astype(jnp.float32)
            for s in range(seqs):
                product = jnp.sum((result * doubled[s]).reshape(size // 8, 8, both), axis=0)
                sums[s][pair] = product if layer == 0 else sums[s][pair] + product
    lines = []
    for s in range(seqs):
        for pair in range(pairs):
            lines.append(jnp.sum(sums[s][pair], axis=0, keepdims=True))
    lines = jnp.concatenate(lines, axis=0)
    ends = jnp.where(
        (lax.broadcasted_iota(jnp.int32, (8, both), 1) < size)
        == (lax.broadcasted_iota(jnp.int32, (8, both), 0) == 0),
        1.0,
        0.0,
    )
    result = nt(ends, lines, HIGHEST)
    for s in range(seqs):
        for side in range(2):
            out[s : s + 1, side * pairs : (side + 1) * pairs] = result[
                side : side + 1, s * pairs : (s + 1) * pairs
            ]


def score(where, half, pieces, samples, tokens, queries):
    rank = half.shape[2]
    seqs = len(samples)
    return pl.pallas_call(
        functools.partial(score_kernel, tokens, seqs),
        in_specs=[smem()] + [vmem()] * (1 + len(pieces) + seqs),
        out_specs=vmem(),
        out_shape=jax.ShapeDtypeStruct((seqs, queries), jnp.float32),
        scratch_shapes=[pltpu.VMEM((seqs, rank, 2 * rank), jnp.float32)],
        compiler_params=pltpu.CompilerParams(vmem_limit_bytes=24 * MIB),
        name="score",
    )(where, half, *pieces, *samples)


def shift(value, axis, by):
    size = lax.axis_size(axis)
    return lax.ppermute(value, axis, [(i, (i + by) % size) for i in range(size)])


def everyone(value, axis):
    return [value] + [shift(value, axis, k) for k in range(1, lax.axis_size(axis))]


def scatter(pieces, axis):
    return [pieces[0]] + [shift(piece, axis, k) for k, piece in enumerate(pieces) if k > 0]


def local_owned(acts, grads, proj_in, proj_out, queries):
    seqs, length, _ = acts.shape
    tokens = seqs * length * lax.axis_size("dp")
    where = lax.axis_index("tensor").astype(jnp.int32).reshape(1)
    all_queries = lax.all_gather(queries, "dp", axis=0, tiled=True)
    x_pieces = scatter(project_in(where, acts, proj_in), "tensor")
    g_pieces = scatter(project_out(where, grads, proj_out), "tensor")
    x, in_part = cov_in(x_pieces)
    in_sum = ordered_sum(where, everyone(in_part, "tensor"))
    half = right(everyone(in_sum, "dp"), all_queries, tokens)
    out_part, sample = cov_out(x, g_pieces)
    out_sum = ordered_sum(where, everyone(out_part, "tensor"))
    return score(
        where,
        half,
        everyone(out_sum, "dp"),
        everyone(sample, "tensor"),
        tokens,
        all_queries.shape[0],
    )


def damp(matrix):
    size = matrix.shape[0]
    shift_by = 0.1 * jnp.trace(matrix) / size
    return matrix + shift_by * jnp.eye(size, dtype=matrix.dtype)


def chol_apply(factor, rhs):
    lower_sol = lax.linalg.triangular_solve(factor, rhs, left_side=True, lower=True)
    return lax.linalg.triangular_solve(
        factor, lower_sol, left_side=True, lower=True, transpose_a=True
    )


def precondition(query, left, right_side):
    count, rank = (query.shape[0], query.shape[1])
    left_fac = jnp.linalg.cholesky(left)
    right_fac = jnp.linalg.cholesky(right_side)
    stacked = jnp.transpose(query, (1, 0, 2)).reshape(rank, count * rank)
    middle = chol_apply(left_fac, stacked).reshape(rank, count, rank)
    turned = jnp.transpose(middle, (2, 1, 0)).reshape(rank, count * rank)
    result = chol_apply(right_fac, turned).reshape(rank, count, rank)
    return jnp.transpose(result, (1, 2, 0))


def diagonal_blocks(whole, rank):
    return jnp.stack([whole[:, 0:rank, 0:rank], whole[:, rank : 2 * rank, rank : 2 * rank]], axis=1)


def local_general(acts, grads, proj_in, proj_out, queries):
    seq_count, length, width_loc = acts.shape
    rank = proj_in.shape[1]
    hidden_loc = grads.shape[3]
    flat = acts.reshape(-1, width_loc)
    xpart = nt(flat, proj_in.reshape(2 * rank, width_loc))
    gpart = jnp.concatenate(
        [nt(grads[layer].reshape(-1, hidden_loc), proj_out[layer]) for layer in range(2)], axis=1
    )
    count = seq_count * length * lax.axis_size("dp")
    xin, gout = lax.psum((xpart, gpart), "tensor")
    in_cov, out_cov = lax.psum((tn(xin, xin, HIGHEST), tn(gout, gout, HIGHEST)), "dp")
    whole = (
        jnp.einsum(
            "sto,sti->soi",
            gout.reshape(seq_count, length, 2 * rank),
            xin.reshape(seq_count, length, 2 * rank),
            precision=HIGHEST,
        )
        / length
    )
    samples = diagonal_blocks(whole, rank)
    in_cov = in_cov / count
    out_cov = out_cov / count
    precond = []
    for layer in range(2):
        low = layer * rank
        damped_in = damp(in_cov[low : low + rank, low : low + rank])
        damped_out = damp(out_cov[low : low + rank, low : low + rank])
        precond.append(precondition(queries[:, layer].astype(jnp.float32), damped_out, damped_in))
    query_count = queries.shape[0]
    query_b = jnp.stack(precond, axis=1).astype(jnp.bfloat16).reshape(query_count, -1)
    sample_b = samples.astype(jnp.bfloat16).reshape(seq_count, -1)
    return nt(sample_b, lax.all_gather(query_b, "dp", axis=0, tiled=True))


def local(acts, grads, proj_in, proj_out, queries):
    if acts.shape[0] == lax.axis_size("tensor"):
        return local_owned(acts, grads, proj_in, proj_out, queries)
    return local_general(acts, grads, proj_in, proj_out, queries)


def solution(mesh):
    placed = (
        P(("groups", "dp"), None, "tensor"),
        P(None, ("groups", "dp"), None, "tensor"),
        P(None, None, "tensor"),
        P(None, None, "tensor"),
        P("dp", None, None, None),
    )
    return jax.shard_map(
        local, mesh=mesh, in_specs=placed, out_specs=P(("groups", "dp"), None), check_vma=False
    )
```

```python
import functools

import jax
import jax.numpy as jnp
from jax import lax
from jax.experimental import pallas as pl
from jax.experimental.pallas import tpu as pltpu
from jax.sharding import PartitionSpec as P

HIGHEST = lax.Precision.HIGHEST
MIB = 1024 * 1024


def nt(a, b, precision=None):
    return lax.dot_general(
        a, b, (((1,), (1,)), ((), ())), precision=precision, preferred_element_type=jnp.float32
    )


def tn(a, b, precision=None):
    return lax.dot_general(
        a, b, (((0,), (0,)), ((), ())), precision=precision, preferred_element_type=jnp.float32
    )


def nn(a, b, precision=None):
    return jnp.dot(a, b, precision=precision, preferred_element_type=jnp.float32)


def vmem():
    return pl.BlockSpec(memory_space=pltpu.VMEM)


def smem():
    return pl.BlockSpec(memory_space=pltpu.SMEM)


def params(mib):
    return pltpu.CompilerParams(vmem_limit_bytes=mib * MIB)


def project_kernel(one, side_ref, rows_ref, proj_ref, near_ref, far_ref, acc):
    step = pl.program_id(0)
    rank, width = proj_ref.shape[1:]
    tokens = acc.shape[2]
    if one:
        rows = rows_ref[...].reshape(tokens, width)
        part = nt(proj_ref[...].reshape(2 * rank, width), rows).reshape(2, rank, tokens)
        parts = [part[0], part[1]]
    else:
        parts = [nt(proj_ref[k], rows_ref[k].reshape(tokens, width)) for k in range(2)]

    @pl.when(step == 0)
    def _():
        for k in range(2):
            acc[k] = parts[k]

    @pl.when(step > 0)
    def _():
        for k in range(2):
            acc[k] += parts[k]

    @pl.when(step == pl.num_programs(0) - 1)
    def _():
        near_ref[...] = acc[side_ref[0]]
        far_ref[...] = acc[1 - side_ref[0]]


def project(side, rows, proj, block):
    one = rows.ndim == 3
    seqs, length, width = rows.shape[-3:]
    rank = proj.shape[1]
    if one:
        rows_spec = pl.BlockSpec((seqs, length, block), lambda i: (0, 0, i))
    else:
        rows_spec = pl.BlockSpec((2, seqs, length, block), lambda i: (0, 0, 0, i))
    shape = (rank, seqs * length)
    return pl.pallas_call(
        functools.partial(project_kernel, one),
        grid=(width // block,),
        in_specs=[smem(), rows_spec, pl.BlockSpec((2, rank, block), lambda i: (0, 0, i))],
        out_specs=[pl.BlockSpec(shape, lambda i: (0, 0))] * 2,
        out_shape=[jax.ShapeDtypeStruct(shape, jnp.float32)] * 2,
        scratch_shapes=[pltpu.VMEM((2,) + shape, jnp.float32)],
        compiler_params=params(52),
        name="project_in" if one else "project_out",
    )(side, rows, proj)


def to_owner(near, far):
    return [
        near,
        lax.ppermute(near, "tensor", [(0, 1), (3, 2)]),
        lax.ppermute(far, "tensor", [(1, 2), (2, 1)]),
        lax.ppermute(far, "tensor", [(0, 2), (3, 1)]),
    ]


def total(pieces):
    value = pieces[0][...]
    for piece in pieces[1:]:
        value = value + piece[...]
    return value


def fold(square):
    half = square.shape[0] // 2
    return jnp.concatenate([square[:half], square[half:]], axis=1)


def unfold(folded):
    size = folded.shape[1] // 2
    return jnp.concatenate([folded[:, :size], folded[:, size:]], axis=0)


def cov_in_kernel(*refs):
    pieces, (x_out, cov_out) = refs[:-2], refs[-2:]
    x = total(pieces)
    x_out[...] = x
    folded = fold(nt(x, x, HIGHEST))
    for k in range(cov_out.shape[0]):
        cov_out[k] = folded


def cov_in(pieces, copies):
    rank, tokens = pieces[0].shape
    return pl.pallas_call(
        cov_in_kernel,
        in_specs=[vmem()] * len(pieces),
        out_specs=[vmem()] * 2,
        out_shape=[
            jax.ShapeDtypeStruct((rank, tokens), jnp.float32),
            jax.ShapeDtypeStruct((copies, rank // 2, 2 * rank), jnp.float32),
        ],
        compiler_params=params(16),
        name="cov_in",
    )(*pieces)


def cov_out_kernel(x_ref, *refs):
    pieces, (cov_out, sample_out) = refs[:-2], refs[-2:]
    g = total(pieces)
    folded = fold(nt(g, g, HIGHEST))
    for k in range(cov_out.shape[0]):
        cov_out[k] = folded
    seqs = sample_out.shape[0]
    length = x_ref.shape[1] // seqs
    for s in range(seqs):
        tokens = slice(s * length, (s + 1) * length)
        sample = nt(x_ref[:, tokens], g[:, tokens], HIGHEST) / length
        sample = sample.astype(jnp.bfloat16).astype(jnp.float32)
        sample_out[s] = jnp.concatenate([sample, sample], axis=1)


def cov_out(x, pieces, copies, seqs):
    rank = x.shape[0]
    return pl.pallas_call(
        cov_out_kernel,
        in_specs=[vmem()] * (1 + len(pieces)),
        out_specs=[vmem()] * 2,
        out_shape=[
            jax.ShapeDtypeStruct((copies, rank // 2, 2 * rank), jnp.float32),
            jax.ShapeDtypeStruct((seqs, rank, 2 * rank), jnp.float32),
        ],
        compiler_params=params(16),
        name="cov_out",
    )(x, *pieces)


def scales(steps, spread):
    r = (spread - 1.0) / (spread + 1.0)
    out = []
    for _ in range(steps):
        out.append(2.0 / (2.0 - r * r))
        r = r * r / (2.0 - r * r)
    return out


def damped_inverse(folded_ref, tokens):
    folded = folded_ref[0]
    for k in range(1, folded_ref.shape[0]):
        folded = folded + folded_ref[k]
    whole = unfold(folded / tokens)
    size = whole.shape[0]
    rows = lax.broadcasted_iota(jnp.int32, whole.shape, 0)
    cols = lax.broadcasted_iota(jnp.int32, whole.shape, 1)
    diagonal = rows == cols
    unit = jnp.sum(jnp.where(diagonal, whole, 0.0)) / size
    eye = jnp.where(diagonal, 1.0, 0.0)
    matrix = whole / unit + 0.1 * eye
    low, high = 0.1, size + 0.1
    start = 2.0 / (low + high)
    steps = scales(7, high / low)
    y = matrix * start
    x = (2.0 * start * steps[0]) * eye - (start * steps[0]) * y
    y = steps[0] * (2.0 * y - nn(y, y, HIGHEST))
    for scale in steps[1:-1]:
        both = nn(jnp.concatenate([x, y], axis=0), y, HIGHEST)
        x = scale * (2.0 * x - both[:size])
        y = scale * (2.0 * y - both[size:])
    x = steps[-1] * (2.0 * x - nn(x, y, HIGHEST))
    x = x + nn(x, eye - nn(matrix, x, HIGHEST), HIGHEST)
    return x / unit


def split(value):
    high = value.astype(jnp.bfloat16)
    rest = value - high.astype(jnp.float32)
    middle = rest.astype(jnp.bfloat16)
    low = (rest - middle.astype(jnp.float32)).astype(jnp.bfloat16)
    return high, middle, low


def right_kernel(tokens, side_ref, cov_ref, queries_ref, out, held, sem):
    copy = pltpu.make_async_copy(queries_ref.at[:, side_ref[0]], held, sem)
    copy.start()
    inverse = damped_inverse(cov_ref, tokens)
    size = inverse.shape[0]
    count = held.shape[0]
    left = jnp.concatenate(split(inverse), axis=0)
    copy.wait()
    group = 4
    for block in range(count // group):
        first = block * group // 2
        places = [first, first + count // 2, first + 1, first + 1 + count // 2]
        rows = jnp.concatenate([held[place] for place in places], axis=0)
        result = nt(left, rows)
        result = result[:size] + result[size : 2 * size] + result[2 * size :]
        high, middle, _ = split(result)
        lanes = slice(block * group * size, (block + 1) * group * size)
        out[0, :, lanes] = high
        out[1, :, lanes] = middle


def right(side, cov, queries, tokens):
    count, _, rank, _ = queries.shape
    return pl.pallas_call(
        functools.partial(right_kernel, tokens),
        in_specs=[smem(), vmem(), pl.BlockSpec(memory_space=pl.ANY)],
        out_specs=vmem(),
        out_shape=jax.ShapeDtypeStruct((2, rank, count * rank), jnp.bfloat16),
        scratch_shapes=[pltpu.VMEM((count, rank, rank), queries.dtype), pltpu.SemaphoreType.DMA],
        compiler_params=params(48),
        name="right",
    )(side, cov, queries)


def score_kernel(tokens, cov_ref, half_ref, sample_ref, out):
    inverse = damped_inverse(cov_ref, tokens)
    size = inverse.shape[0]
    both = 2 * size
    pairs = half_ref.shape[2] // both
    seqs = sample_ref.shape[0]
    none = jnp.zeros_like(inverse)
    twice = jnp.concatenate(
        [
            jnp.concatenate([inverse, none], axis=1),
            jnp.concatenate([none, inverse], axis=1),
        ],
        axis=0,
    )
    high, middle, _ = split(twice)
    once = jnp.concatenate([high, middle], axis=1)
    weights = jnp.concatenate([once, once], axis=0)
    samples = [sample_ref[s] for s in range(seqs)]
    lines = [[] for _ in range(seqs)]
    for pair in range(pairs):
        lanes = slice(pair * both, (pair + 1) * both)
        rows = jnp.concatenate([half_ref[0, :, lanes], half_ref[1, :, lanes]], axis=1)
        result = nn(rows, weights)
        result = (result[:, :both] + result[:, both:]).astype(jnp.bfloat16).astype(jnp.float32)
        for s in range(seqs):
            lines[s].append(jnp.sum(result * samples[s], axis=0, keepdims=True))
    lines = jnp.concatenate([line for part in lines for line in part], axis=0)
    shape = (8, both)
    ends = jnp.where(
        (lax.broadcasted_iota(jnp.int32, shape, 1) < size)
        == (lax.broadcasted_iota(jnp.int32, shape, 0) == 0),
        1.0,
        0.0,
    )
    result = nt(ends, lines, HIGHEST)
    result = jnp.concatenate(
        [
            jnp.concatenate(
                [result[k : k + 1, s * pairs : (s + 1) * pairs] for k in range(2)], axis=1
            )
            for s in range(seqs)
        ],
        axis=0,
    )
    for k in range(out.shape[0]):
        out[k] = result


def score(cov, half, sample, tokens, queries, copies):
    return pl.pallas_call(
        functools.partial(score_kernel, tokens),
        in_specs=[vmem()] * 3,
        out_specs=vmem(),
        out_shape=jax.ShapeDtypeStruct((copies, sample.shape[0], queries), jnp.float32),
        compiler_params=params(24),
        name="score",
    )(cov, half, sample)


def exchange(copies, axis):
    return lax.all_to_all(copies, axis, 0, 0, tiled=True)


def local_owned(acts, grads, proj_in, proj_out, queries):
    seqs, length, _ = acts.shape
    parts = lax.axis_size("dp")
    tokens = seqs * length * parts
    side = (lax.axis_index("tensor") // 2).astype(jnp.int32).reshape(1)
    all_queries = lax.all_gather(queries, "dp", axis=0, tiled=True)
    x_pieces = to_owner(*project(side, acts, proj_in, 512))
    g_pieces = to_owner(*project(side, grads, proj_out, 512))
    x, in_cov = cov_in(x_pieces, parts)
    half = right(side, exchange(in_cov, "dp"), all_queries, tokens)
    out_cov, sample = cov_out(x, g_pieces, parts, seqs)
    scores = score(
        exchange(out_cov, "dp"), half, sample, tokens, all_queries.shape[0], lax.axis_size("tensor")
    )
    scores = exchange(scores, "tensor")
    return scores[1] + scores[2]


def damp(matrix):
    size = matrix.shape[0]
    shift_by = 0.1 * jnp.trace(matrix) / size
    return matrix + shift_by * jnp.eye(size, dtype=matrix.dtype)


def chol_apply(factor, rhs):
    lower_sol = lax.linalg.triangular_solve(factor, rhs, left_side=True, lower=True)
    return lax.linalg.triangular_solve(
        factor, lower_sol, left_side=True, lower=True, transpose_a=True
    )


def precondition(query, left, right_side):
    count, rank = (query.shape[0], query.shape[1])
    left_fac = jnp.linalg.cholesky(left)
    right_fac = jnp.linalg.cholesky(right_side)
    stacked = jnp.transpose(query, (1, 0, 2)).reshape(rank, count * rank)
    middle = chol_apply(left_fac, stacked).reshape(rank, count, rank)
    turned = jnp.transpose(middle, (2, 1, 0)).reshape(rank, count * rank)
    result = chol_apply(right_fac, turned).reshape(rank, count, rank)
    return jnp.transpose(result, (1, 2, 0))


def diagonal_blocks(whole, rank):
    return jnp.stack([whole[:, 0:rank, 0:rank], whole[:, rank : 2 * rank, rank : 2 * rank]], axis=1)


def local_general(acts, grads, proj_in, proj_out, queries):
    seq_count, length, width_loc = acts.shape
    rank = proj_in.shape[1]
    hidden_loc = grads.shape[3]
    flat = acts.reshape(-1, width_loc)
    xpart = nt(flat, proj_in.reshape(2 * rank, width_loc))
    gpart = jnp.concatenate(
        [nt(grads[layer].reshape(-1, hidden_loc), proj_out[layer]) for layer in range(2)], axis=1
    )
    count = seq_count * length * lax.axis_size("dp")
    xin, gout = lax.psum((xpart, gpart), "tensor")
    in_cov, out_cov = lax.psum((tn(xin, xin, HIGHEST), tn(gout, gout, HIGHEST)), "dp")
    whole = (
        jnp.einsum(
            "sto,sti->soi",
            gout.reshape(seq_count, length, 2 * rank),
            xin.reshape(seq_count, length, 2 * rank),
            precision=HIGHEST,
        )
        / length
    )
    samples = diagonal_blocks(whole, rank)
    in_cov = in_cov / count
    out_cov = out_cov / count
    precond = []
    for layer in range(2):
        low = layer * rank
        damped_in = damp(in_cov[low : low + rank, low : low + rank])
        damped_out = damp(out_cov[low : low + rank, low : low + rank])
        precond.append(precondition(queries[:, layer].astype(jnp.float32), damped_out, damped_in))
    query_count = queries.shape[0]
    query_b = jnp.stack(precond, axis=1).astype(jnp.bfloat16).reshape(query_count, -1)
    sample_b = samples.astype(jnp.bfloat16).reshape(seq_count, -1)
    return nt(sample_b, lax.all_gather(query_b, "dp", axis=0, tiled=True))


def local(acts, grads, proj_in, proj_out, queries):
    if lax.axis_size("tensor") == 4:
        return local_owned(acts, grads, proj_in, proj_out, queries)
    return local_general(acts, grads, proj_in, proj_out, queries)


def solution(mesh):
    placed = (
        P(("groups", "dp"), None, "tensor"),
        P(None, ("groups", "dp"), None, "tensor"),
        P(None, None, "tensor"),
        P(None, None, "tensor"),
        P("dp", None, None, None),
    )
    return jax.shard_map(
        local, mesh=mesh, in_specs=placed, out_specs=P(("groups", "dp"), None), check_vma=False
    )
```

```python
import functools

import jax
import jax.numpy as jnp
from jax import lax
from jax.experimental import pallas as pl
from jax.experimental.pallas import tpu as pltpu
from jax.sharding import PartitionSpec as P

HIGHEST = lax.Precision.HIGHEST
MIB = 1024 * 1024


def nt(a, b, precision=None):
    return lax.dot_general(
        a, b, (((1,), (1,)), ((), ())), precision=precision, preferred_element_type=jnp.float32
    )


def tn(a, b, precision=None):
    return lax.dot_general(
        a, b, (((0,), (0,)), ((), ())), precision=precision, preferred_element_type=jnp.float32
    )


def nn(a, b, precision=None):
    return jnp.dot(a, b, precision=precision, preferred_element_type=jnp.float32)


def vmem():
    return pl.BlockSpec(memory_space=pltpu.VMEM)


def smem():
    return pl.BlockSpec(memory_space=pltpu.SMEM)


def hbm():
    return pl.BlockSpec(memory_space=pl.ANY)


def in_hbm(value):
    return pltpu.with_memory_space_constraint(value, pltpu.HBM)


def params(mib):
    return pltpu.CompilerParams(vmem_limit_bytes=mib * MIB)


def project_in_kernel(side_ref, rows_hbm, proj_hbm, near_ref, far_ref, rows, proj, acc, sems, proj_sem):
    seqs, length, width = rows.shape
    rank = proj.shape[1]
    proj_copy = pltpu.make_async_copy(proj_hbm, proj, proj_sem)
    proj_copy.start()
    copies = [pltpu.make_async_copy(rows_hbm.at[s], rows.at[s], sems.at[s]) for s in range(seqs)]
    for copy in copies:
        copy.start()
    proj_copy.wait()
    weights = proj[...].reshape(2 * rank, width)
    for s in range(seqs):
        copies[s].wait()
        tokens = slice(s * length, (s + 1) * length)
        part = nt(weights, rows[s])
        acc[0, :, tokens] = part[:rank]
        acc[1, :, tokens] = part[rank:]
    near_ref[...] = acc[side_ref[0]]
    far_ref[...] = acc[1 - side_ref[0]]


def project_out_kernel(side_ref, rows_hbm, proj_hbm, near_ref, far_ref, rows, proj, acc, sems, proj_sem):
    _, seqs, length, width = rows.shape
    half = width // 2
    proj_copy = pltpu.make_async_copy(proj_hbm, proj, proj_sem)
    proj_copy.start()
    copies = {}
    for s in range(seqs):
        for part in range(2):
            lanes = pl.ds(part * half, half)
            for layer in range(2):
                copies[s, part, layer] = pltpu.make_async_copy(
                    rows_hbm.at[layer, s, :, lanes],
                    rows.at[layer, s, :, lanes],
                    sems.at[s, part, layer],
                )
                copies[s, part, layer].start()
    proj_copy.wait()
    for s in range(seqs):
        tokens = slice(s * length, (s + 1) * length)
        for part in range(2):
            lanes = slice(part * half, (part + 1) * half)
            for layer in range(2):
                copies[s, part, layer].wait()
            for layer in range(2):
                value = nt(proj[layer, :, lanes], rows[layer, s, :, lanes])
                if part > 0:
                    value = value + acc[layer, :, tokens]
                acc[layer, :, tokens] = value
    near_ref[...] = acc[side_ref[0]]
    far_ref[...] = acc[1 - side_ref[0]]


def project(side, rows, proj, mib):
    one = rows.ndim == 3
    seqs, length, _ = rows.shape[-3:]
    rank = proj.shape[1]
    shape = (rank, seqs * length)
    return pl.pallas_call(
        project_in_kernel if one else project_out_kernel,
        in_specs=[smem(), hbm(), hbm()],
        out_specs=[vmem()] * 2,
        out_shape=[jax.ShapeDtypeStruct(shape, jnp.float32)] * 2,
        scratch_shapes=[
            pltpu.VMEM(rows.shape, rows.dtype),
            pltpu.VMEM(proj.shape, proj.dtype),
            pltpu.VMEM((2,) + shape, jnp.float32),
            pltpu.SemaphoreType.DMA((seqs,) if one else (seqs, 2, 2)),
            pltpu.SemaphoreType.DMA,
        ],
        compiler_params=params(mib),
        name="project_in" if one else "project_out",
    )(side, in_hbm(rows), in_hbm(proj) if one else proj)


def to_owner(near, far):
    return [
        near,
        lax.ppermute(near, "tensor", [(0, 1), (3, 2)]),
        lax.ppermute(far, "tensor", [(1, 2), (2, 1)]),
        lax.ppermute(far, "tensor", [(0, 2), (3, 1)]),
    ]


def total(pieces):
    value = pieces[0][...]
    for piece in pieces[1:]:
        value = value + piece[...]
    return value


def cov_in_kernel(*refs):
    pieces, (x_out, cov_out) = refs[:-2], refs[-2:]
    x = total(pieces)
    x_out[...] = x
    cov_out[...] = nt(x, jnp.concatenate([x, jnp.zeros_like(x)], axis=0), HIGHEST)


def cov_in(pieces):
    rank, tokens = pieces[0].shape
    return pl.pallas_call(
        cov_in_kernel,
        in_specs=[vmem()] * len(pieces),
        out_specs=[vmem()] * 2,
        out_shape=[
            jax.ShapeDtypeStruct((rank, tokens), jnp.float32),
            jax.ShapeDtypeStruct((rank, 2 * rank), jnp.float32),
        ],
        compiler_params=params(16),
        name="cov_in",
    )(*pieces)


def cov_out_kernel(x_ref, cov_ref, *refs):
    pieces, (cov_out, sample_out) = refs[:-2], refs[-2:]
    g = total(pieces)
    cov_out[...] = cov_ref[...] + nt(g, jnp.concatenate([jnp.zeros_like(g), g], axis=0), HIGHEST)
    seqs = sample_out.shape[0]
    length = x_ref.shape[1] // seqs
    for s in range(seqs):
        tokens = slice(s * length, (s + 1) * length)
        sample = nt(x_ref[:, tokens], g[:, tokens], HIGHEST) / length
        sample = sample.astype(jnp.bfloat16).astype(jnp.float32)
        sample_out[s] = jnp.concatenate([sample, sample], axis=1)


def cov_out(x, cov, pieces, seqs):
    rank = x.shape[0]
    return pl.pallas_call(
        cov_out_kernel,
        in_specs=[vmem()] * (2 + len(pieces)),
        out_specs=[vmem()] * 2,
        out_shape=[
            jax.ShapeDtypeStruct((rank, 2 * rank), jnp.float32),
            jax.ShapeDtypeStruct((seqs, rank, 2 * rank), jnp.float32),
        ],
        compiler_params=params(16),
        name="cov_out",
    )(x, cov, *pieces)


def scales(steps, spread):
    r = (spread - 1.0) / (spread + 1.0)
    out = []
    for _ in range(steps):
        out.append(2.0 / (2.0 - r * r))
        r = r * r / (2.0 - r * r)
    return out


def damped_inverses(pair):
    size, both = pair.shape
    left = lax.broadcasted_iota(jnp.int32, pair.shape, 1) < size
    whole = jnp.concatenate([jnp.where(left, pair, 0.0), jnp.where(left, 0.0, pair)], axis=0)
    rows = lax.broadcasted_iota(jnp.int32, whole.shape, 0)
    cols = lax.broadcasted_iota(jnp.int32, whole.shape, 1)
    diagonal = rows == cols
    on_diagonal = jnp.where(diagonal, whole, 0.0)
    unit = jnp.where(
        rows < size, jnp.sum(on_diagonal[:size]) / size, jnp.sum(on_diagonal[size:]) / size
    )
    eye = jnp.where(diagonal, 1.0, 0.0)
    matrix = whole / unit + 0.1 * eye
    low, high = 0.1, size + 0.1
    start = 2.0 / (low + high)
    steps = scales(7, high / low)
    y = matrix * start
    x = (2.0 * start * steps[0]) * eye - (start * steps[0]) * y
    y = steps[0] * (2.0 * y - nn(y, y, HIGHEST))
    for scale in steps[1:-1]:
        product = nn(jnp.concatenate([x, y], axis=0), y, HIGHEST)
        x = scale * (2.0 * x - product[:both])
        y = scale * (2.0 * y - product[both:])
    x = steps[-1] * (2.0 * x - nn(x, y, HIGHEST))
    x = x + nn(x, eye - nn(matrix, x, HIGHEST), HIGHEST)
    return x / unit


def split(value):
    high = value.astype(jnp.bfloat16)
    rest = value - high.astype(jnp.float32)
    middle = rest.astype(jnp.bfloat16)
    low = (rest - middle.astype(jnp.float32)).astype(jnp.bfloat16)
    return high, middle, low


def score_kernel(tokens, side_ref, own_ref, other_ref, sample_ref, queries_hbm, out, held, half, sem):
    copy = pltpu.make_async_copy(queries_hbm.at[:, side_ref[0]], held, sem)
    copy.start()
    inverses = damped_inverses((own_ref[...] + other_ref[...]) / tokens)
    both = inverses.shape[0]
    size = both // 2
    count = held.shape[0]
    seqs = sample_ref.shape[0]
    pairs = count // 2
    first = jnp.concatenate(split(inverses[:size, :size]), axis=0)
    right = inverses[size:]
    twice = jnp.concatenate([pltpu.roll(right, size, 1), right], axis=0)
    high, middle, _ = split(twice)
    once = jnp.concatenate([high, middle], axis=1)
    second = jnp.concatenate([once, once], axis=0)
    copy.wait()
    group = 4
    for block in range(count // group):
        start = block * group // 2
        places = [start, start + pairs, start + 1, start + 1 + pairs]
        rows = jnp.concatenate([held[place] for place in places], axis=0)
        result = nt(first, rows)
        result = result[:size] + result[size : 2 * size] + result[2 * size :]
        high, middle, _ = split(result)
        lanes = slice(block * group * size, (block + 1) * group * size)
        half[0, :, lanes] = high
        half[1, :, lanes] = middle
    samples = [sample_ref[s] for s in range(seqs)]
    lines = [[] for _ in range(seqs)]
    for pair in range(pairs):
        lanes = slice(pair * both, (pair + 1) * both)
        rows = jnp.concatenate([half[0, :, lanes], half[1, :, lanes]], axis=1)
        result = nn(rows, second)
        result = (result[:, :both] + result[:, both:]).astype(jnp.bfloat16).astype(jnp.float32)
        for s in range(seqs):
            lines[s].append(jnp.sum(result * samples[s], axis=0, keepdims=True))
    lines = jnp.concatenate([line for part in lines for line in part], axis=0)
    shape = (8, both)
    ends = jnp.where(
        (lax.broadcasted_iota(jnp.int32, shape, 1) < size)
        == (lax.broadcasted_iota(jnp.int32, shape, 0) == 0),
        1.0,
        0.0,
    )
    result = nt(ends, lines, HIGHEST)
    for s in range(seqs):
        for k in range(2):
            out[s : s + 1, k * pairs : (k + 1) * pairs] = result[
                k : k + 1, s * pairs : (s + 1) * pairs
            ]


def score(side, own, other, sample, queries, tokens):
    count, _, rank, _ = queries.shape
    return pl.pallas_call(
        functools.partial(score_kernel, tokens),
        in_specs=[smem(), vmem(), vmem(), vmem(), hbm()],
        out_specs=vmem(),
        out_shape=jax.ShapeDtypeStruct((sample.shape[0], count), jnp.float32),
        scratch_shapes=[
            pltpu.VMEM((count, rank, rank), queries.dtype),
            pltpu.VMEM((2, rank, count * rank), jnp.bfloat16),
            pltpu.SemaphoreType.DMA,
        ],
        compiler_params=params(16),
        name="score",
    )(side, own, other, sample, in_hbm(queries))


def swap(value, axis, bit):
    return lax.ppermute(value, axis, [(i, i ^ bit) for i in range(lax.axis_size(axis))])


def local_owned(acts, grads, proj_in, proj_out, queries):
    seqs, length, _ = acts.shape
    parts = lax.axis_size("dp")
    tokens = seqs * length * parts
    place = lax.axis_index("tensor").astype(jnp.int32)
    side = (place >= 2).astype(jnp.int32).reshape(1)
    all_queries = lax.all_gather(queries, "dp", axis=0, tiled=True)
    x_pieces = to_owner(*project(side, acts, proj_in, 16))
    g_pieces = to_owner(*project(side, grads, proj_out, 40))
    x, cov = cov_in(x_pieces)
    cov, sample = cov_out(x, cov, g_pieces, seqs)
    other = jnp.zeros_like(cov)
    bit = 1
    while bit < parts:
        cov = cov if bit == 1 else cov + other
        other = swap(cov, "dp", bit)
        bit *= 2
    scores = score(side, cov, other, sample, all_queries, tokens)
    owner = (place == 1) | (place == 2)
    return (
        jnp.where(owner, scores, 0.0)
        + lax.ppermute(scores, "tensor", [(1, 2), (2, 1)])
        + lax.ppermute(scores, "tensor", [(1, 0), (2, 3)])
        + lax.ppermute(scores, "tensor", [(2, 0), (1, 3)])
    )


def damp(matrix):
    size = matrix.shape[0]
    shift_by = 0.1 * jnp.trace(matrix) / size
    return matrix + shift_by * jnp.eye(size, dtype=matrix.dtype)


def chol_apply(factor, rhs):
    lower_sol = lax.linalg.triangular_solve(factor, rhs, left_side=True, lower=True)
    return lax.linalg.triangular_solve(
        factor, lower_sol, left_side=True, lower=True, transpose_a=True
    )


def precondition(query, left, right_side):
    count, rank = (query.shape[0], query.shape[1])
    left_fac = jnp.linalg.cholesky(left)
    right_fac = jnp.linalg.cholesky(right_side)
    stacked = jnp.transpose(query, (1, 0, 2)).reshape(rank, count * rank)
    middle = chol_apply(left_fac, stacked).reshape(rank, count, rank)
    turned = jnp.transpose(middle, (2, 1, 0)).reshape(rank, count * rank)
    result = chol_apply(right_fac, turned).reshape(rank, count, rank)
    return jnp.transpose(result, (1, 2, 0))


def diagonal_blocks(whole, rank):
    return jnp.stack([whole[:, 0:rank, 0:rank], whole[:, rank : 2 * rank, rank : 2 * rank]], axis=1)


def local_general(acts, grads, proj_in, proj_out, queries):
    seq_count, length, width_loc = acts.shape
    rank = proj_in.shape[1]
    hidden_loc = grads.shape[3]
    flat = acts.reshape(-1, width_loc)
    xpart = nt(flat, proj_in.reshape(2 * rank, width_loc))
    gpart = jnp.concatenate(
        [nt(grads[layer].reshape(-1, hidden_loc), proj_out[layer]) for layer in range(2)], axis=1
    )
    count = seq_count * length * lax.axis_size("dp")
    xin, gout = lax.psum((xpart, gpart), "tensor")
    in_cov, out_cov = lax.psum((tn(xin, xin, HIGHEST), tn(gout, gout, HIGHEST)), "dp")
    whole = (
        jnp.einsum(
            "sto,sti->soi",
            gout.reshape(seq_count, length, 2 * rank),
            xin.reshape(seq_count, length, 2 * rank),
            precision=HIGHEST,
        )
        / length
    )
    samples = diagonal_blocks(whole, rank)
    in_cov = in_cov / count
    out_cov = out_cov / count
    precond = []
    for layer in range(2):
        low = layer * rank
        damped_in = damp(in_cov[low : low + rank, low : low + rank])
        damped_out = damp(out_cov[low : low + rank, low : low + rank])
        precond.append(precondition(queries[:, layer].astype(jnp.float32), damped_out, damped_in))
    query_count = queries.shape[0]
    query_b = jnp.stack(precond, axis=1).astype(jnp.bfloat16).reshape(query_count, -1)
    sample_b = samples.astype(jnp.bfloat16).reshape(seq_count, -1)
    return nt(sample_b, lax.all_gather(query_b, "dp", axis=0, tiled=True))


def local(acts, grads, proj_in, proj_out, queries):
    parts = lax.axis_size("dp")
    if lax.axis_size("tensor") == 4 and parts & (parts - 1) == 0:
        return local_owned(acts, grads, proj_in, proj_out, queries)
    return local_general(acts, grads, proj_in, proj_out, queries)


def solution(mesh):
    placed = (
        P(("groups", "dp"), None, "tensor"),
        P(None, ("groups", "dp"), None, "tensor"),
        P(None, None, "tensor"),
        P(None, None, "tensor"),
        P("dp", None, None, None),
    )
    return jax.shard_map(
        local, mesh=mesh, in_specs=placed, out_specs=P(("groups", "dp"), None), check_vma=False
    )
```

```python
import functools

import jax
import jax.numpy as jnp
from jax import lax
from jax.experimental import pallas as pl
from jax.experimental.pallas import tpu as pltpu
from jax.sharding import PartitionSpec as P

HIGHEST = lax.Precision.HIGHEST
MIB = 1024 * 1024


def nt(a, b, precision=None):
    return lax.dot_general(
        a, b, (((1,), (1,)), ((), ())), precision=precision, preferred_element_type=jnp.float32
    )


def tn(a, b, precision=None):
    return lax.dot_general(
        a, b, (((0,), (0,)), ((), ())), precision=precision, preferred_element_type=jnp.float32
    )


def nn(a, b, precision=None):
    return jnp.dot(a, b, precision=precision, preferred_element_type=jnp.float32)


def vmem():
    return pl.BlockSpec(memory_space=pltpu.VMEM)


def smem():
    return pl.BlockSpec(memory_space=pltpu.SMEM)


def hbm():
    return pl.BlockSpec(memory_space=pl.ANY)


def in_hbm(value):
    return pltpu.with_memory_space_constraint(value, pltpu.HBM)


def params(mib):
    return pltpu.CompilerParams(vmem_limit_bytes=mib * MIB)


def project_in_kernel(side_ref, rows_hbm, proj_hbm, near_ref, far_ref, rows, proj, acc, sems, proj_sem):
    seqs, length, width = rows.shape
    rank = proj.shape[1]
    proj_copy = pltpu.make_async_copy(proj_hbm, proj, proj_sem)
    proj_copy.start()
    copies = [pltpu.make_async_copy(rows_hbm.at[s], rows.at[s], sems.at[s]) for s in range(seqs)]
    for copy in copies:
        copy.start()
    proj_copy.wait()
    weights = proj[...].reshape(2 * rank, width)
    for s in range(seqs):
        copies[s].wait()
        tokens = slice(s * length, (s + 1) * length)
        part = nt(weights, rows[s])
        acc[0, :, tokens] = part[:rank]
        acc[1, :, tokens] = part[rank:]
    near_ref[...] = acc[side_ref[0]]
    far_ref[...] = acc[1 - side_ref[0]]


def project_out_kernel(side_ref, rows_hbm, proj_hbm, near_ref, far_ref, rows, proj, acc, sems, proj_sem):
    _, seqs, length, width = rows.shape
    half = width // 2
    proj_copy = pltpu.make_async_copy(proj_hbm, proj, proj_sem)
    proj_copy.start()
    copies = {}
    for s in range(seqs):
        for part in range(2):
            lanes = pl.ds(part * half, half)
            for layer in range(2):
                copies[s, part, layer] = pltpu.make_async_copy(
                    rows_hbm.at[layer, s, :, lanes],
                    rows.at[layer, s, :, lanes],
                    sems.at[s, part, layer],
                )
                copies[s, part, layer].start()
    proj_copy.wait()
    for s in range(seqs):
        tokens = slice(s * length, (s + 1) * length)
        for part in range(2):
            lanes = slice(part * half, (part + 1) * half)
            for layer in range(2):
                copies[s, part, layer].wait()
            for layer in range(2):
                value = nt(proj[layer, :, lanes], rows[layer, s, :, lanes])
                if part > 0:
                    value = value + acc[layer, :, tokens]
                acc[layer, :, tokens] = value
    near_ref[...] = acc[side_ref[0]]
    far_ref[...] = acc[1 - side_ref[0]]


def project(side, rows, proj, mib):
    one = rows.ndim == 3
    seqs, length, _ = rows.shape[-3:]
    rank = proj.shape[1]
    shape = (rank, seqs * length)
    return pl.pallas_call(
        project_in_kernel if one else project_out_kernel,
        in_specs=[smem(), hbm(), hbm()],
        out_specs=[vmem()] * 2,
        out_shape=[jax.ShapeDtypeStruct(shape, jnp.float32)] * 2,
        scratch_shapes=[
            pltpu.VMEM(rows.shape, rows.dtype),
            pltpu.VMEM(proj.shape, proj.dtype),
            pltpu.VMEM((2,) + shape, jnp.float32),
            pltpu.SemaphoreType.DMA((seqs,) if one else (seqs, 2, 2)),
            pltpu.SemaphoreType.DMA,
        ],
        compiler_params=params(mib),
        name="project_in" if one else "project_out",
    )(side, in_hbm(rows), in_hbm(proj) if one else proj)


def to_owner(near, far):
    return [
        near,
        lax.ppermute(far, "tensor", [(0, 2), (3, 1)]),
        lax.ppermute(far, "tensor", [(1, 2), (2, 1)]),
        lax.ppermute(near, "tensor", [(0, 1), (3, 2)]),
    ]


def total(pieces):
    value = pieces[0][...]
    for piece in pieces[1:]:
        value = value + piece[...]
    return value


def cov_in_kernel(side_ref, queries_hbm, *refs):
    pieces, (x_out, cov_out, packed_out, held, sem) = refs[:-5], refs[-5:]
    copy = pltpu.make_async_copy(queries_hbm.at[:, side_ref[0]], held, sem)
    copy.start()
    x = total(pieces)
    x_out[...] = x
    cov_out[...] = nt(x, jnp.concatenate([x, jnp.zeros_like(x)], axis=0), HIGHEST)
    copy.wait()
    half = held.shape[0] // 2
    for k in range(half):
        pair = [held[k].astype(jnp.float32), held[k + half].astype(jnp.float32)]
        packed_out[k] = jnp.concatenate(pair, axis=1).astype(packed_out.dtype)


def cov_in(side, queries, pieces):
    rank, tokens = pieces[0].shape
    count = queries.shape[0]
    return pl.pallas_call(
        cov_in_kernel,
        in_specs=[smem(), hbm()] + [vmem()] * len(pieces),
        out_specs=[vmem()] * 3,
        out_shape=[
            jax.ShapeDtypeStruct((rank, tokens), jnp.float32),
            jax.ShapeDtypeStruct((rank, 2 * rank), jnp.float32),
            jax.ShapeDtypeStruct((count // 2, rank, 2 * rank), queries.dtype),
        ],
        scratch_shapes=[
            pltpu.VMEM((count, rank, rank), queries.dtype),
            pltpu.SemaphoreType.DMA,
        ],
        compiler_params=params(16),
        name="cov_in",
    )(side, in_hbm(queries), *pieces)


def cov_out_kernel(x_ref, cov_ref, *refs):
    pieces, (cov_out, sample_out) = refs[:-2], refs[-2:]
    g = total(pieces)
    cov_out[...] = cov_ref[...] + nt(g, jnp.concatenate([jnp.zeros_like(g), g], axis=0), HIGHEST)
    seqs = sample_out.shape[0]
    length = x_ref.shape[1] // seqs
    for s in range(seqs):
        tokens = slice(s * length, (s + 1) * length)
        sample = nt(x_ref[:, tokens], g[:, tokens], HIGHEST) / length
        sample = sample.astype(jnp.bfloat16).astype(jnp.float32)
        sample_out[s] = jnp.concatenate([sample, sample], axis=1)


def cov_out(x, cov, pieces, seqs):
    rank = x.shape[0]
    return pl.pallas_call(
        cov_out_kernel,
        in_specs=[vmem()] * (2 + len(pieces)),
        out_specs=[vmem()] * 2,
        out_shape=[
            jax.ShapeDtypeStruct((rank, 2 * rank), jnp.float32),
            jax.ShapeDtypeStruct((seqs, rank, 2 * rank), jnp.float32),
        ],
        compiler_params=params(16),
        name="cov_out",
    )(x, cov, *pieces)


def scales(steps, spread):
    r = (spread - 1.0) / (spread + 1.0)
    out = []
    for _ in range(steps):
        out.append(2.0 / (2.0 - r * r))
        r = r * r / (2.0 - r * r)
    return out


def damped_inverses(pair):
    size, both = pair.shape
    left = lax.broadcasted_iota(jnp.int32, pair.shape, 1) < size
    whole = jnp.concatenate([jnp.where(left, pair, 0.0), jnp.where(left, 0.0, pair)], axis=0)
    rows = lax.broadcasted_iota(jnp.int32, whole.shape, 0)
    cols = lax.broadcasted_iota(jnp.int32, whole.shape, 1)
    diagonal = rows == cols
    on_diagonal = jnp.where(diagonal, whole, 0.0)
    unit = jnp.where(
        rows < size, jnp.sum(on_diagonal[:size]) / size, jnp.sum(on_diagonal[size:]) / size
    )
    eye = jnp.where(diagonal, 1.0, 0.0)
    matrix = whole / unit + 0.1 * eye
    low, high = 0.1, size + 0.1
    start = 2.0 / (low + high)
    steps = scales(7, high / low)
    y = matrix * start
    x = (2.0 * start * steps[0]) * eye - (start * steps[0]) * y
    y = steps[0] * (2.0 * y - nn(y, y, HIGHEST))
    for scale in steps[1:-1]:
        product = nn(jnp.concatenate([x, y], axis=0), y, HIGHEST)
        x = scale * (2.0 * x - product[:both])
        y = scale * (2.0 * y - product[both:])
    x = steps[-1] * (2.0 * x - nn(x, y, HIGHEST))
    x = x + nn(x, eye - nn(matrix, x, HIGHEST), HIGHEST)
    return x / unit


def split(value):
    high = value.astype(jnp.bfloat16)
    rest = value - high.astype(jnp.float32)
    middle = rest.astype(jnp.bfloat16)
    low = (rest - middle.astype(jnp.float32)).astype(jnp.bfloat16)
    return high, middle, low


def score_kernel(tokens, place_ref, own_ref, other_ref, sample_ref, *refs):
    pieces, (out, held, half) = refs[:-3], refs[-3:]
    parts = len(pieces)
    for k, piece in enumerate(pieces):
        held[place_ref[0] ^ k] = piece[...]
    inverses = damped_inverses((own_ref[...] + other_ref[...]) / tokens)
    both = inverses.shape[0]
    size = both // 2
    seqs = sample_ref.shape[0]
    blocks = held.shape[1]
    pairs = parts * blocks
    first = jnp.concatenate(split(inverses[:size, :size]), axis=0)
    none = jnp.zeros_like(first)
    first = jnp.concatenate(
        [jnp.concatenate([first, none], axis=1), jnp.concatenate([none, first], axis=1)], axis=0
    )
    right = inverses[size:]
    twice = jnp.concatenate([pltpu.roll(right, size, 1), right], axis=0)
    high, middle, _ = split(twice)
    once = jnp.concatenate([high, middle], axis=1)
    second = jnp.concatenate([once, once], axis=0)
    for part in range(parts // 2):
        for block in range(0, blocks, 2):
            rows = jnp.concatenate(
                [
                    held[part, block],
                    held[part + parts // 2, block],
                    held[part, block + 1],
                    held[part + parts // 2, block + 1],
                ],
                axis=0,
            )
            result = nt(first, rows)
            for k in range(2):
                three = result[3 * size * k : 3 * size * (k + 1)]
                value = three[:size] + three[size : 2 * size] + three[2 * size :]
                high, middle, _ = split(value)
                pair = (2 * part + k) * blocks + block
                lanes = slice(pair * both, (pair + 2) * both)
                half[0, :, lanes] = high
                half[1, :, lanes] = middle
    samples = [sample_ref[s] for s in range(seqs)]
    lines = [[] for _ in range(seqs)]
    for pair in range(pairs):
        lanes = slice(pair * both, (pair + 1) * both)
        rows = jnp.concatenate([half[0, :, lanes], half[1, :, lanes]], axis=1)
        result = nn(rows, second)
        result = (result[:, :both] + result[:, both:]).astype(jnp.bfloat16).astype(jnp.float32)
        for s in range(seqs):
            lines[s].append(jnp.sum(result * samples[s], axis=0, keepdims=True))
    lines = jnp.concatenate([line for part in lines for line in part], axis=0)
    shape = (8, both)
    ends = jnp.where(
        (lax.broadcasted_iota(jnp.int32, shape, 1) < size)
        == (lax.broadcasted_iota(jnp.int32, shape, 0) == 0),
        1.0,
        0.0,
    )
    result = nt(ends, lines, HIGHEST)
    for s in range(seqs):
        for k in range(2):
            out[s : s + 1, k * pairs : (k + 1) * pairs] = result[
                k : k + 1, s * pairs : (s + 1) * pairs
            ]


def score(place, own, other, sample, pieces, tokens):
    blocks, rank, both = pieces[0].shape
    parts = len(pieces)
    count = 2 * parts * blocks
    return pl.pallas_call(
        functools.partial(score_kernel, tokens),
        in_specs=[smem()] + [vmem()] * (3 + parts),
        out_specs=vmem(),
        out_shape=jax.ShapeDtypeStruct((sample.shape[0], count), jnp.float32),
        scratch_shapes=[
            pltpu.VMEM((parts, blocks, rank, both), pieces[0].dtype),
            pltpu.VMEM((2, rank, count * rank), jnp.bfloat16),
        ],
        compiler_params=params(16),
        name="score",
    )(place, own, other, sample, *pieces)


def swap(value, axis, bit):
    return lax.ppermute(value, axis, [(i, i ^ bit) for i in range(lax.axis_size(axis))])


def local_owned(acts, grads, proj_in, proj_out, queries):
    seqs, length, _ = acts.shape
    parts = lax.axis_size("dp")
    tokens = seqs * length * parts
    across = lax.axis_index("tensor").astype(jnp.int32)
    side = (across >= 2).astype(jnp.int32)
    side = side.reshape(1)
    place = lax.axis_index("dp").astype(jnp.int32).reshape(1)
    x_pieces = to_owner(*project(side, acts, proj_in, 16))
    g_pieces = to_owner(*project(side, grads, proj_out, 40))
    x, cov, packed = cov_in(side, queries, x_pieces)
    query_pieces = [packed] + [swap(packed, "dp", bits) for bits in range(1, parts)]
    cov, sample = cov_out(x, cov, g_pieces, seqs)
    other = jnp.zeros_like(cov)
    bit = 1
    while bit < parts:
        cov = cov if bit == 1 else cov + other
        other = swap(cov, "dp", bit)
        bit *= 2
    scores = score(place, cov, other, sample, query_pieces, tokens)
    scores = scores + lax.ppermute(scores, "tensor", [(1, 2), (2, 1)])
    outer = lax.ppermute(scores, "tensor", [(1, 0), (2, 3)])
    return jnp.where((across == 1) | (across == 2), scores, outer)


def damp(matrix):
    size = matrix.shape[0]
    shift_by = 0.1 * jnp.trace(matrix) / size
    return matrix + shift_by * jnp.eye(size, dtype=matrix.dtype)


def chol_apply(factor, rhs):
    lower_sol = lax.linalg.triangular_solve(factor, rhs, left_side=True, lower=True)
    return lax.linalg.triangular_solve(
        factor, lower_sol, left_side=True, lower=True, transpose_a=True
    )


def precondition(query, left, right_side):
    count, rank = (query.shape[0], query.shape[1])
    left_fac = jnp.linalg.cholesky(left)
    right_fac = jnp.linalg.cholesky(right_side)
    stacked = jnp.transpose(query, (1, 0, 2)).reshape(rank, count * rank)
    middle = chol_apply(left_fac, stacked).reshape(rank, count, rank)
    turned = jnp.transpose(middle, (2, 1, 0)).reshape(rank, count * rank)
    result = chol_apply(right_fac, turned).reshape(rank, count, rank)
    return jnp.transpose(result, (1, 2, 0))


def diagonal_blocks(whole, rank):
    return jnp.stack([whole[:, 0:rank, 0:rank], whole[:, rank : 2 * rank, rank : 2 * rank]], axis=1)


def local_general(acts, grads, proj_in, proj_out, queries):
    seq_count, length, width_loc = acts.shape
    rank = proj_in.shape[1]
    hidden_loc = grads.shape[3]
    flat = acts.reshape(-1, width_loc)
    xpart = nt(flat, proj_in.reshape(2 * rank, width_loc))
    gpart = jnp.concatenate(
        [nt(grads[layer].reshape(-1, hidden_loc), proj_out[layer]) for layer in range(2)], axis=1
    )
    count = seq_count * length * lax.axis_size("dp")
    xin, gout = lax.psum((xpart, gpart), "tensor")
    in_cov, out_cov = lax.psum((tn(xin, xin, HIGHEST), tn(gout, gout, HIGHEST)), "dp")
    whole = (
        jnp.einsum(
            "sto,sti->soi",
            gout.reshape(seq_count, length, 2 * rank),
            xin.reshape(seq_count, length, 2 * rank),
            precision=HIGHEST,
        )
        / length
    )
    samples = diagonal_blocks(whole, rank)
    in_cov = in_cov / count
    out_cov = out_cov / count
    precond = []
    for layer in range(2):
        low = layer * rank
        damped_in = damp(in_cov[low : low + rank, low : low + rank])
        damped_out = damp(out_cov[low : low + rank, low : low + rank])
        precond.append(precondition(queries[:, layer].astype(jnp.float32), damped_out, damped_in))
    query_count = queries.shape[0]
    query_b = jnp.stack(precond, axis=1).astype(jnp.bfloat16).reshape(query_count, -1)
    sample_b = samples.astype(jnp.bfloat16).reshape(seq_count, -1)
    return nt(sample_b, lax.all_gather(query_b, "dp", axis=0, tiled=True))


def local(acts, grads, proj_in, proj_out, queries):
    parts = lax.axis_size("dp")
    blocks = queries.shape[0]
    if lax.axis_size("tensor") == 4 and parts > 1 and parts & (parts - 1) == 0 and blocks % 4 == 0:
        return local_owned(acts, grads, proj_in, proj_out, queries)
    return local_general(acts, grads, proj_in, proj_out, queries)


def solution(mesh):
    placed = (
        P(("groups", "dp"), None, "tensor"),
        P(None, ("groups", "dp"), None, "tensor"),
        P(None, None, "tensor"),
        P(None, None, "tensor"),
        P("dp", None, None, None),
    )
    return jax.shard_map(
        local, mesh=mesh, in_specs=placed, out_specs=P(("groups", "dp"), None), check_vma=False
    )
```

```python
import functools

import jax
import jax.numpy as jnp
from jax import lax
from jax.experimental import pallas as pl
from jax.experimental.pallas import tpu as pltpu
from jax.sharding import PartitionSpec as P

HIGHEST = lax.Precision.HIGHEST
MIB = 1024 * 1024


def nt(a, b, precision=None):
    return lax.dot_general(
        a, b, (((1,), (1,)), ((), ())), precision=precision, preferred_element_type=jnp.float32
    )


def tn(a, b, precision=None):
    return lax.dot_general(
        a, b, (((0,), (0,)), ((), ())), precision=precision, preferred_element_type=jnp.float32
    )


def nn(a, b, precision=None):
    return jnp.dot(a, b, precision=precision, preferred_element_type=jnp.float32)


def vmem():
    return pl.BlockSpec(memory_space=pltpu.VMEM)


def smem():
    return pl.BlockSpec(memory_space=pltpu.SMEM)


def hbm():
    return pl.BlockSpec(memory_space=pl.ANY)


def in_hbm(value):
    return pltpu.with_memory_space_constraint(value, pltpu.HBM)


def params(mib):
    return pltpu.CompilerParams(vmem_limit_bytes=mib * MIB)


def project_in_kernel(side_ref, rows_hbm, proj_hbm, out, rows, proj, sems, proj_sem):
    seqs, length, width = rows.shape
    rank = proj.shape[1]
    proj_copy = pltpu.make_async_copy(proj_hbm, proj, proj_sem)
    proj_copy.start()

    def copy(s):
        return pltpu.make_async_copy(rows_hbm.at[s], rows.at[s], sems.at[s])

    for s in range(seqs):
        copy(s).start()
    proj_copy.wait()

    @pl.loop(0, seqs)
    def _(s):
        copy(s).wait()
        part = nt(proj[...].reshape(2 * rank, width), rows[s])
        tokens = pl.ds(pl.multiple_of(s * length, length), length)
        out[side_ref[0], :, tokens] = part[:rank]
        out[1 - side_ref[0], :, tokens] = part[rank:]


def project_in(side, rows, proj):
    seqs, length, _ = rows.shape
    rank = proj.shape[1]
    return pl.pallas_call(
        project_in_kernel,
        in_specs=[smem(), hbm(), hbm()],
        out_specs=vmem(),
        out_shape=jax.ShapeDtypeStruct((2, rank, seqs * length), jnp.float32),
        scratch_shapes=[
            pltpu.VMEM(rows.shape, rows.dtype),
            pltpu.VMEM(proj.shape, proj.dtype),
            pltpu.SemaphoreType.DMA((seqs,)),
            pltpu.SemaphoreType.DMA,
        ],
        compiler_params=params(16),
        name="project_in",
    )(side, in_hbm(rows), in_hbm(proj))


def project_out_kernel(first, side_ref, rows_hbm, proj_ref, after, out, rows, sems):
    del after
    _, seqs, length, width = rows.shape
    half = width // 2

    def copy(layer, s, part):
        lanes = pl.ds(part * half, half)
        return pltpu.make_async_copy(
            rows_hbm.at[layer, first + s, :, lanes],
            rows.at[layer, s, :, lanes],
            sems.at[layer, s, part],
        )

    for s in range(seqs):
        for part in range(2):
            for layer in range(2):
                copy(layer, s, part).start()

    @pl.loop(0, seqs)
    def _(s):
        values = [None, None]
        for part in range(2):
            lanes = slice(part * half, (part + 1) * half)
            for layer in range(2):
                copy(layer, s, part).wait()
            for layer in range(2):
                value = nt(proj_ref[layer, :, lanes], rows[layer, s, :, lanes])
                values[layer] = value if part == 0 else values[layer] + value
        tokens = pl.ds(pl.multiple_of(s * length, length), length)
        out[side_ref[0], :, tokens] = values[0]
        out[1 - side_ref[0], :, tokens] = values[1]


def project_out(side, rows, proj, first, seqs, after):
    _, _, length, width = rows.shape
    rank = proj.shape[1]
    return pl.pallas_call(
        functools.partial(project_out_kernel, first),
        in_specs=[smem(), hbm(), vmem(), hbm()],
        out_specs=vmem(),
        out_shape=jax.ShapeDtypeStruct((2, rank, seqs * length), jnp.float32),
        scratch_shapes=[
            pltpu.VMEM((2, seqs, length, width), rows.dtype),
            pltpu.SemaphoreType.DMA((2, seqs, 2)),
        ],
        compiler_params=params(20),
        name="project_out",
    )(side, in_hbm(rows), proj, after)


def inwards(value):
    return lax.ppermute(value, "tensor", [(0, 1), (3, 2)])


def across(value):
    return lax.ppermute(value, "tensor", [(1, 2), (2, 1)])


def gathered(own_ref, outer_ref, other_ref):
    return own_ref[0] + outer_ref[0] + other_ref[...]


def cov_in_kernel(own_ref, outer_ref, other_ref, after, x_out, cov_out):
    del after
    x = gathered(own_ref, outer_ref, other_ref)
    x_out[...] = x
    cov_out[...] = nt(x, jnp.concatenate([x, jnp.zeros_like(x)], axis=0), HIGHEST)


def cov_in(own, outer, other, after):
    rank, tokens = other.shape
    return pl.pallas_call(
        cov_in_kernel,
        in_specs=[vmem()] * 3 + [hbm()],
        out_specs=[vmem()] * 2,
        out_shape=[
            jax.ShapeDtypeStruct((rank, tokens), jnp.float32),
            jax.ShapeDtypeStruct((rank, 2 * rank), jnp.float32),
        ],
        compiler_params=params(16),
        name="cov_in",
    )(own, outer, other, after)


def cov_out_kernel(first, x_ref, cov_ref, own_ref, outer_ref, other_ref, cov_out, sample_out):
    g = gathered(own_ref, outer_ref, other_ref)
    cov_out[...] = cov_ref[...] + nt(g, jnp.concatenate([jnp.zeros_like(g), g], axis=0), HIGHEST)
    seqs = sample_out.shape[0]
    length = g.shape[1] // seqs
    for s in range(seqs):
        x = x_ref[:, (first + s) * length : (first + s + 1) * length]
        sample = nt(x, g[:, s * length : (s + 1) * length], HIGHEST) / length
        sample = sample.astype(jnp.bfloat16).astype(jnp.float32)
        sample_out[s] = jnp.concatenate([sample, sample], axis=1)


def cov_out(x, cov, own, outer, other, first, seqs):
    rank = x.shape[0]
    return pl.pallas_call(
        functools.partial(cov_out_kernel, first),
        in_specs=[vmem()] * 5,
        out_specs=[vmem()] * 2,
        out_shape=[
            jax.ShapeDtypeStruct((rank, 2 * rank), jnp.float32),
            jax.ShapeDtypeStruct((seqs, rank, 2 * rank), jnp.float32),
        ],
        compiler_params=params(16),
        name="cov_out",
    )(x, cov, own, outer, other)


def pack_kernel(side_ref, queries_hbm, after, out, held, sem):
    del after
    copy = pltpu.make_async_copy(queries_hbm.at[:, side_ref[0]], held, sem)
    copy.start()
    copy.wait()
    half = held.shape[0] // 2
    for k in range(half):
        pair = [held[k].astype(jnp.float32), held[k + half].astype(jnp.float32)]
        out[k] = jnp.concatenate(pair, axis=1).astype(out.dtype)


def pack(side, queries, after):
    count, _, rank, _ = queries.shape
    return pl.pallas_call(
        pack_kernel,
        in_specs=[smem(), hbm(), hbm()],
        out_specs=vmem(),
        out_shape=jax.ShapeDtypeStruct((count // 2, rank, 2 * rank), queries.dtype),
        scratch_shapes=[
            pltpu.VMEM((count, rank, rank), queries.dtype),
            pltpu.SemaphoreType.DMA,
        ],
        compiler_params=params(16),
        name="pack",
    )(side, in_hbm(queries), after)


def scales(steps, spread):
    r = (spread - 1.0) / (spread + 1.0)
    out = []
    for _ in range(steps):
        out.append(2.0 / (2.0 - r * r))
        r = r * r / (2.0 - r * r)
    return out


def damped_inverses(pair):
    size, both = pair.shape
    left = lax.broadcasted_iota(jnp.int32, pair.shape, 1) < size
    whole = jnp.concatenate([jnp.where(left, pair, 0.0), jnp.where(left, 0.0, pair)], axis=0)
    rows = lax.broadcasted_iota(jnp.int32, whole.shape, 0)
    cols = lax.broadcasted_iota(jnp.int32, whole.shape, 1)
    diagonal = rows == cols
    on_diagonal = jnp.where(diagonal, whole, 0.0)
    unit = jnp.where(
        rows < size, jnp.sum(on_diagonal[:size]) / size, jnp.sum(on_diagonal[size:]) / size
    )
    eye = jnp.where(diagonal, 1.0, 0.0)
    matrix = whole / unit + 0.1 * eye
    low, high = 0.1, size + 0.1
    start = 2.0 / (low + high)
    steps = scales(7, high / low)
    y = matrix * start
    x = (2.0 * start * steps[0]) * eye - (start * steps[0]) * y
    y = steps[0] * (2.0 * y - nn(y, y, HIGHEST))
    for scale in steps[1:-1]:
        product = nn(jnp.concatenate([x, y], axis=0), y, HIGHEST)
        x = scale * (2.0 * x - product[:both])
        y = scale * (2.0 * y - product[both:])
    x = steps[-1] * (2.0 * x - nn(x, y, HIGHEST))
    x = x + nn(x, eye - nn(matrix, x, HIGHEST), HIGHEST)
    return x / unit


def split(value):
    high = value.astype(jnp.bfloat16)
    rest = value - high.astype(jnp.float32)
    middle = rest.astype(jnp.bfloat16)
    low = (rest - middle.astype(jnp.float32)).astype(jnp.bfloat16)
    return high, middle, low


def score_kernel(tokens, place_ref, own_ref, other_ref, first_ref, second_ref, *refs):
    pieces, (out, held, half) = refs[:-3], refs[-3:]
    parts = len(pieces)
    for k, piece in enumerate(pieces):
        held[place_ref[0] ^ k] = piece[...]
    inverses = damped_inverses((own_ref[...] + other_ref[...]) / tokens)
    both = inverses.shape[0]
    size = both // 2
    samples = [ref[s] for ref in (first_ref, second_ref) for s in range(ref.shape[0])]
    seqs = len(samples)
    blocks = held.shape[1]
    pairs = parts * blocks
    first = jnp.concatenate(split(inverses[:size, :size]), axis=0)
    none = jnp.zeros_like(first)
    first = jnp.concatenate(
        [jnp.concatenate([first, none], axis=1), jnp.concatenate([none, first], axis=1)], axis=0
    )
    right = inverses[size:]
    twice = jnp.concatenate([pltpu.roll(right, size, 1), right], axis=0)
    high, middle, _ = split(twice)
    once = jnp.concatenate([high, middle], axis=1)
    second = jnp.concatenate([once, once], axis=0)
    for part in range(parts // 2):
        for block in range(0, blocks, 2):
            rows = jnp.concatenate(
                [
                    held[part, block],
                    held[part + parts // 2, block],
                    held[part, block + 1],
                    held[part + parts // 2, block + 1],
                ],
                axis=0,
            )
            result = nt(first, rows)
            for k in range(2):
                three = result[3 * size * k : 3 * size * (k + 1)]
                value = three[:size] + three[size : 2 * size] + three[2 * size :]
                high, middle, _ = split(value)
                pair = (2 * part + k) * blocks + block
                lanes = slice(pair * both, (pair + 2) * both)
                half[0, :, lanes] = high
                half[1, :, lanes] = middle
    lines = [[] for _ in range(seqs)]
    for pair in range(pairs):
        lanes = slice(pair * both, (pair + 1) * both)
        rows = jnp.concatenate([half[0, :, lanes], half[1, :, lanes]], axis=1)
        result = nn(rows, second)
        result = (result[:, :both] + result[:, both:]).astype(jnp.bfloat16).astype(jnp.float32)
        for s in range(seqs):
            lines[s].append(jnp.sum(result * samples[s], axis=0, keepdims=True))
    lines = jnp.concatenate([line for part in lines for line in part], axis=0)
    shape = (8, both)
    ends = jnp.where(
        (lax.broadcasted_iota(jnp.int32, shape, 1) < size)
        == (lax.broadcasted_iota(jnp.int32, shape, 0) == 0),
        1.0,
        0.0,
    )
    result = nt(ends, lines, HIGHEST)
    for s in range(seqs):
        for k in range(2):
            out[s : s + 1, k * pairs : (k + 1) * pairs] = result[
                k : k + 1, s * pairs : (s + 1) * pairs
            ]


def score(place, own, other, samples, pieces, tokens):
    blocks, rank, both = pieces[0].shape
    parts = len(pieces)
    count = 2 * parts * blocks
    seqs = sum(sample.shape[0] for sample in samples)
    return pl.pallas_call(
        functools.partial(score_kernel, tokens),
        in_specs=[smem()] + [vmem()] * (4 + parts),
        out_specs=vmem(),
        out_shape=jax.ShapeDtypeStruct((seqs, count), jnp.float32),
        scratch_shapes=[
            pltpu.VMEM((parts, blocks, rank, both), pieces[0].dtype),
            pltpu.VMEM((2, rank, count * rank), jnp.bfloat16),
        ],
        compiler_params=params(16),
        name="score",
    )(place, own, other, *samples, *pieces)


def swap(value, axis, bit):
    return lax.ppermute(value, axis, [(i, i ^ bit) for i in range(lax.axis_size(axis))])


def after(value, earlier):
    return lax.optimization_barrier((value, earlier))[0]


def local_owned(acts, grads, proj_in, proj_out, queries):
    seqs, length, _ = acts.shape
    parts = lax.axis_size("dp")
    tokens = seqs * length * parts
    column = lax.axis_index("tensor").astype(jnp.int32)
    side = (column >= 2).astype(jnp.int32).reshape(1)
    place = lax.axis_index("dp").astype(jnp.int32).reshape(1)
    half = seqs // 2
    x = project_in(side, acts, proj_in)
    x_outer = inwards(x)
    g = project_out(side, grads, proj_out, 0, half, x)
    g_outer = inwards(g)
    h = project_out(side, grads, proj_out, half, seqs - half, g)
    h_outer = inwards(h)
    x_far = x[1] + after(x_outer, h)[1]
    x_other = across(x_far)
    g_far = g[1] + after(g_outer, x_far)[1]
    g_other = across(g_far)
    packed = pack(side, queries, g_far)
    query_pieces = [packed] + [swap(packed, "dp", bits) for bits in range(1, parts)]
    h_far = h[1] + after(h_outer, packed)[1]
    h_other = across(h_far)
    x_sum, cov = cov_in(x, x_outer, x_other, h_far)
    cov, sample = cov_out(x_sum, cov, g, g_outer, g_other, 0, half)
    cov, last = cov_out(x_sum, cov, h, h_outer, h_other, half, seqs - half)
    other = jnp.zeros_like(cov)
    bit = 1
    while bit < parts:
        cov = cov if bit == 1 else cov + other
        other = swap(cov, "dp", bit)
        bit *= 2
    scores = score(place, cov, other, [sample, last], query_pieces, tokens)
    scores = scores + across(scores)
    outer = lax.ppermute(scores, "tensor", [(1, 0), (2, 3)])
    return jnp.where((column == 1) | (column == 2), scores, outer)


def damp(matrix):
    size = matrix.shape[0]
    shift_by = 0.1 * jnp.trace(matrix) / size
    return matrix + shift_by * jnp.eye(size, dtype=matrix.dtype)


def chol_apply(factor, rhs):
    lower_sol = lax.linalg.triangular_solve(factor, rhs, left_side=True, lower=True)
    return lax.linalg.triangular_solve(
        factor, lower_sol, left_side=True, lower=True, transpose_a=True
    )


def precondition(query, left, right_side):
    count, rank = (query.shape[0], query.shape[1])
    left_fac = jnp.linalg.cholesky(left)
    right_fac = jnp.linalg.cholesky(right_side)
    stacked = jnp.transpose(query, (1, 0, 2)).reshape(rank, count * rank)
    middle = chol_apply(left_fac, stacked).reshape(rank, count, rank)
    turned = jnp.transpose(middle, (2, 1, 0)).reshape(rank, count * rank)
    result = chol_apply(right_fac, turned).reshape(rank, count, rank)
    return jnp.transpose(result, (1, 2, 0))


def diagonal_blocks(whole, rank):
    return jnp.stack([whole[:, 0:rank, 0:rank], whole[:, rank : 2 * rank, rank : 2 * rank]], axis=1)


def local_general(acts, grads, proj_in, proj_out, queries):
    seq_count, length, width_loc = acts.shape
    rank = proj_in.shape[1]
    hidden_loc = grads.shape[3]
    flat = acts.reshape(-1, width_loc)
    xpart = nt(flat, proj_in.reshape(2 * rank, width_loc))
    gpart = jnp.concatenate(
        [nt(grads[layer].reshape(-1, hidden_loc), proj_out[layer]) for layer in range(2)], axis=1
    )
    count = seq_count * length * lax.axis_size("dp")
    xin, gout = lax.psum((xpart, gpart), "tensor")
    in_cov, out_cov = lax.psum((tn(xin, xin, HIGHEST), tn(gout, gout, HIGHEST)), "dp")
    whole = (
        jnp.einsum(
            "sto,sti->soi",
            gout.reshape(seq_count, length, 2 * rank),
            xin.reshape(seq_count, length, 2 * rank),
            precision=HIGHEST,
        )
        / length
    )
    samples = diagonal_blocks(whole, rank)
    in_cov = in_cov / count
    out_cov = out_cov / count
    precond = []
    for layer in range(2):
        low = layer * rank
        damped_in = damp(in_cov[low : low + rank, low : low + rank])
        damped_out = damp(out_cov[low : low + rank, low : low + rank])
        precond.append(precondition(queries[:, layer].astype(jnp.float32), damped_out, damped_in))
    query_count = queries.shape[0]
    query_b = jnp.stack(precond, axis=1).astype(jnp.bfloat16).reshape(query_count, -1)
    sample_b = samples.astype(jnp.bfloat16).reshape(seq_count, -1)
    return nt(sample_b, lax.all_gather(query_b, "dp", axis=0, tiled=True))


def local(acts, grads, proj_in, proj_out, queries):
    parts = lax.axis_size("dp")
    even = parts > 1 and parts & (parts - 1) == 0
    if lax.axis_size("tensor") == 4 and even and acts.shape[0] > 1 and queries.shape[0] % 4 == 0:
        return local_owned(acts, grads, proj_in, proj_out, queries)
    return local_general(acts, grads, proj_in, proj_out, queries)


def solution(mesh):
    placed = (
        P(("groups", "dp"), None, "tensor"),
        P(None, ("groups", "dp"), None, "tensor"),
        P(None, None, "tensor"),
        P(None, None, "tensor"),
        P("dp", None, None, None),
    )
    return jax.shard_map(
        local, mesh=mesh, in_specs=placed, out_specs=P(("groups", "dp"), None), check_vma=False
    )
```

```python
import functools

import jax
import jax.numpy as jnp
from jax import lax
from jax.experimental import pallas as pl
from jax.experimental.pallas import tpu as pltpu
from jax.sharding import PartitionSpec as P

HIGHEST = lax.Precision.HIGHEST
MIB = 1024 * 1024


def nt(a, b, precision=None):
    return lax.dot_general(
        a, b, (((1,), (1,)), ((), ())), precision=precision, preferred_element_type=jnp.float32
    )


def tn(a, b, precision=None):
    return lax.dot_general(
        a, b, (((0,), (0,)), ((), ())), precision=precision, preferred_element_type=jnp.float32
    )


def nn(a, b, precision=None):
    return jnp.dot(a, b, precision=precision, preferred_element_type=jnp.float32)


def vmem():
    return pl.BlockSpec(memory_space=pltpu.VMEM)


def smem():
    return pl.BlockSpec(memory_space=pltpu.SMEM)


def hbm():
    return pl.BlockSpec(memory_space=pl.ANY)


def in_hbm(value):
    return pltpu.with_memory_space_constraint(value, pltpu.HBM)


def params(mib):
    return pltpu.CompilerParams(vmem_limit_bytes=mib * MIB)


def project_in_kernel(side_ref, rows_hbm, proj_hbm, out, rows, proj, sems, proj_sem):
    seqs, length, width = rows.shape
    rank = proj.shape[1]
    proj_copy = pltpu.make_async_copy(proj_hbm, proj, proj_sem)
    proj_copy.start()

    def copy(s):
        return pltpu.make_async_copy(rows_hbm.at[s], rows.at[s], sems.at[s])

    for s in range(seqs):
        copy(s).start()
    proj_copy.wait()

    @pl.loop(0, seqs)
    def _(s):
        copy(s).wait()
        part = nt(proj[...].reshape(2 * rank, width), rows[s])
        tokens = pl.ds(pl.multiple_of(s * length, length), length)
        out[side_ref[0], :, tokens] = part[:rank]
        out[1 - side_ref[0], :, tokens] = part[rank:]


def project_in(side, rows, proj):
    seqs, length, _ = rows.shape
    rank = proj.shape[1]
    return pl.pallas_call(
        project_in_kernel,
        in_specs=[smem(), hbm(), hbm()],
        out_specs=vmem(),
        out_shape=jax.ShapeDtypeStruct((2, rank, seqs * length), jnp.float32),
        scratch_shapes=[
            pltpu.VMEM(rows.shape, rows.dtype),
            pltpu.VMEM(proj.shape, proj.dtype),
            pltpu.SemaphoreType.DMA((seqs,)),
            pltpu.SemaphoreType.DMA,
        ],
        compiler_params=params(16),
        name="project_in",
    )(side, in_hbm(rows), in_hbm(proj))


def project_out_kernel(first, side_ref, rows_hbm, proj_ref, queries_hbm, after, out, *refs):
    del after
    packed, (rows, held, sems, sem) = refs[:-4], refs[-4:]
    _, seqs, length, width = rows.shape
    half = width // 2
    copies = {}
    for s in range(seqs):
        for part in range(2):
            lanes = pl.ds(part * half, half)
            for layer in range(2):
                copies[s, part, layer] = pltpu.make_async_copy(
                    rows_hbm.at[layer, first + s, :, lanes],
                    rows.at[layer, s, :, lanes],
                    sems.at[layer, s, part],
                )
                copies[s, part, layer].start()
    if packed:
        copy = pltpu.make_async_copy(queries_hbm.at[:, side_ref[0]], held, sem)
        copy.start()
    for s in range(seqs):
        values = [None, None]
        for part in range(2):
            lanes = slice(part * half, (part + 1) * half)
            for layer in range(2):
                copies[s, part, layer].wait()
                value = nt(proj_ref[layer, :, lanes], rows[layer, s, :, lanes])
                values[layer] = value if part == 0 else values[layer] + value
        tokens = slice(s * length, (s + 1) * length)
        out[side_ref[0], :, tokens] = values[0]
        out[1 - side_ref[0], :, tokens] = values[1]
    if packed:
        copy.wait()
        blocks = held.shape[0] // 2
        for k in range(blocks):
            pair = [held[k].astype(jnp.float32), held[k + blocks].astype(jnp.float32)]
            packed[0][k] = jnp.concatenate(pair, axis=1).astype(held.dtype)


def project_out(side, rows, proj, queries, first, seqs, after, packs):
    _, _, length, width = rows.shape
    rank = proj.shape[1]
    count = queries.shape[0]
    out_shape = [jax.ShapeDtypeStruct((2, rank, seqs * length), jnp.float32)]
    if packs:
        out_shape.append(jax.ShapeDtypeStruct((count // 2, rank, 2 * rank), queries.dtype))
    return pl.pallas_call(
        functools.partial(project_out_kernel, first),
        in_specs=[smem(), hbm(), vmem(), hbm(), hbm()],
        out_specs=[vmem()] * len(out_shape),
        out_shape=out_shape,
        scratch_shapes=[
            pltpu.VMEM((2, seqs, length, width), rows.dtype),
            pltpu.VMEM((count, rank, rank), queries.dtype),
            pltpu.SemaphoreType.DMA((2, seqs, 2)),
            pltpu.SemaphoreType.DMA,
        ],
        compiler_params=params(24),
        name="project_out",
    )(side, in_hbm(rows), proj, in_hbm(queries), after)


def inwards(value):
    return lax.ppermute(value, "tensor", [(0, 1), (3, 2)])


def across(value):
    return lax.ppermute(value, "tensor", [(1, 2), (2, 1)])


def covariance(value, right):
    none = jnp.zeros_like(value)
    both = [none, value] if right else [value, none]
    return nt(value, jnp.concatenate(both, axis=0), HIGHEST)


def samples_of(x, g, sample_out):
    seqs = sample_out.shape[0]
    length = g.shape[1] // seqs
    for s in range(seqs):
        tokens = slice(s * length, (s + 1) * length)
        sample = nt(x[:, tokens], g[:, tokens], HIGHEST) / length
        sample = sample.astype(jnp.bfloat16).astype(jnp.float32)
        sample_out[s] = jnp.concatenate([sample, sample], axis=1)


def first_kernel(x_ref, x_outer, g_ref, g_outer, other, after, x_out, cov_out, sample_out):
    del after
    tokens = x_ref.shape[2]
    here = g_ref.shape[2]
    x = x_ref[0] + x_outer[0] + other[:, :tokens]
    x_out[...] = x[:, here:]
    g = g_ref[0] + g_outer[0] + other[:, tokens:]
    cov_out[...] = covariance(x, False) + covariance(g, True)
    samples_of(x[:, :here], g, sample_out)


def second_kernel(x_ref, cov_ref, h_ref, h_outer, other, cov_out, sample_out):
    h = h_ref[0] + h_outer[0] + other[...]
    cov_out[...] = cov_ref[...] + covariance(h, True)
    samples_of(x_ref[...], h, sample_out)


def first_half(x, x_outer, g, g_outer, other, after, seqs):
    _, rank, tokens = x.shape
    here = g.shape[2]
    return pl.pallas_call(
        first_kernel,
        in_specs=[vmem()] * 5 + [hbm()],
        out_specs=[vmem()] * 3,
        out_shape=[
            jax.ShapeDtypeStruct((rank, tokens - here), jnp.float32),
            jax.ShapeDtypeStruct((rank, 2 * rank), jnp.float32),
            jax.ShapeDtypeStruct((seqs, rank, 2 * rank), jnp.float32),
        ],
        compiler_params=params(16),
        name="first_half",
    )(x, x_outer, g, g_outer, other, after)


def second_half(x, cov, h, h_outer, other, seqs):
    rank = x.shape[0]
    return pl.pallas_call(
        second_kernel,
        in_specs=[vmem()] * 5,
        out_specs=[vmem()] * 2,
        out_shape=[
            jax.ShapeDtypeStruct((rank, 2 * rank), jnp.float32),
            jax.ShapeDtypeStruct((seqs, rank, 2 * rank), jnp.float32),
        ],
        compiler_params=params(16),
        name="second_half",
    )(x, cov, h, h_outer, other)


def scales(steps, spread):
    r = (spread - 1.0) / (spread + 1.0)
    out = []
    for _ in range(steps):
        out.append(2.0 / (2.0 - r * r))
        r = r * r / (2.0 - r * r)
    return out


def damped_inverses(pair):
    size, both = pair.shape
    left = lax.broadcasted_iota(jnp.int32, pair.shape, 1) < size
    whole = jnp.concatenate([jnp.where(left, pair, 0.0), jnp.where(left, 0.0, pair)], axis=0)
    rows = lax.broadcasted_iota(jnp.int32, whole.shape, 0)
    cols = lax.broadcasted_iota(jnp.int32, whole.shape, 1)
    diagonal = rows == cols
    on_diagonal = jnp.where(diagonal, whole, 0.0)
    unit = jnp.where(
        rows < size, jnp.sum(on_diagonal[:size]) / size, jnp.sum(on_diagonal[size:]) / size
    )
    eye = jnp.where(diagonal, 1.0, 0.0)
    matrix = whole / unit + 0.1 * eye
    low, high = 0.1, size + 0.1
    start = 2.0 / (low + high)
    steps = scales(7, high / low)
    y = matrix * start
    x = (2.0 * start * steps[0]) * eye - (start * steps[0]) * y
    y = steps[0] * (2.0 * y - nn(y, y, HIGHEST))

    def step(k, pair):
        x, y = pair
        scale = jnp.float32(steps[1])
        for place in range(2, len(steps) - 1):
            scale = jnp.where(k == place, jnp.float32(steps[place]), scale)
        product = nn(jnp.concatenate([x, y], axis=0), y, HIGHEST)
        return scale * (2.0 * x - product[:both]), scale * (2.0 * y - product[both:])

    x, y = lax.fori_loop(1, len(steps) - 1, step, (x, y))
    x = steps[-1] * (2.0 * x - nn(x, y, HIGHEST))
    x = x + nn(x, eye - nn(matrix, x, HIGHEST), HIGHEST)
    return x / unit


def split(value):
    high = value.astype(jnp.bfloat16)
    rest = value - high.astype(jnp.float32)
    middle = rest.astype(jnp.bfloat16)
    low = (rest - middle.astype(jnp.float32)).astype(jnp.bfloat16)
    return high, middle, low


def score_kernel(tokens, place_ref, own_ref, other_ref, first_ref, second_ref, *refs):
    pieces, (out, held, half, lines) = refs[:-4], refs[-4:]
    parts = held.shape[0]
    k = 0
    for piece in pieces:
        for place in range(piece.shape[0]):
            held[place_ref[0] ^ k] = piece[place]
            k += 1
    inverses = damped_inverses((own_ref[...] + other_ref[...]) / tokens)
    both = inverses.shape[0]
    size = both // 2
    samples = [ref[s] for ref in (first_ref, second_ref) for s in range(ref.shape[0])]
    seqs = len(samples)
    blocks = held.shape[1]
    pairs = parts * blocks
    first = jnp.concatenate(split(inverses[:size, :size]), axis=0)
    none = jnp.zeros_like(first)
    first = jnp.concatenate(
        [jnp.concatenate([first, none], axis=1), jnp.concatenate([none, first], axis=1)], axis=0
    )
    right = inverses[size:]
    twice = jnp.concatenate([pltpu.roll(right, size, 1), right], axis=0)
    high, middle, _ = split(twice)
    once = jnp.concatenate([high, middle], axis=1)
    second = jnp.concatenate([once, once], axis=0)

    @pl.loop(0, parts // 2)
    def _(part):
        @pl.loop(0, blocks // 2)
        def _(step):
            block = 2 * step
            rows = [
                held[part + place, block + offset]
                for offset in range(2)
                for place in (0, parts // 2)
            ]
            result = nt(first, jnp.concatenate(rows, axis=0))
            for k in range(2):
                three = result[3 * size * k : 3 * size * (k + 1)]
                value = three[:size] + three[size : 2 * size] + three[2 * size :]
                high, middle, _ = split(value)
                pair = (2 * part + k) * blocks + block
                for offset in range(2):
                    lanes = slice(offset * both, (offset + 1) * both)
                    half[pair + offset] = jnp.concatenate([high[:, lanes], middle[:, lanes]], axis=1)

    group = 8

    @pl.loop(0, pairs // group)
    def _(step):
        start = pl.multiple_of(step * group, group)
        rows = half[pl.ds(start, group)].reshape(group * size, 2 * both)
        result = nn(rows, second)
        result = (result[:, :both] + result[:, both:]).astype(jnp.bfloat16).astype(jnp.float32)
        result = result.reshape(group, size, both)
        for s in range(seqs):
            lines[s, pl.ds(start, group)] = jnp.sum(result * samples[s][None], axis=1)

    shape = (8, both)
    ends = jnp.where(
        (lax.broadcasted_iota(jnp.int32, shape, 1) < size)
        == (lax.broadcasted_iota(jnp.int32, shape, 0) == 0),
        1.0,
        0.0,
    )
    result = nt(ends, lines[...].reshape(seqs * pairs, both), HIGHEST)
    for s in range(seqs):
        for k in range(2):
            out[s : s + 1, k * pairs : (k + 1) * pairs] = result[
                k : k + 1, s * pairs : (s + 1) * pairs
            ]


def score(place, own, other, samples, pieces, tokens):
    _, blocks, rank, both = pieces[0].shape
    parts = sum(piece.shape[0] for piece in pieces)
    pairs = parts * blocks
    seqs = sum(sample.shape[0] for sample in samples)
    return pl.pallas_call(
        functools.partial(score_kernel, tokens),
        in_specs=[smem()] + [vmem()] * (4 + len(pieces)),
        out_specs=vmem(),
        out_shape=jax.ShapeDtypeStruct((seqs, 2 * pairs), jnp.float32),
        scratch_shapes=[
            pltpu.VMEM((parts, blocks, rank, both), pieces[0].dtype),
            pltpu.VMEM((pairs, rank, 2 * both), jnp.bfloat16),
            pltpu.VMEM((seqs, pairs, both), jnp.float32),
        ],
        compiler_params=params(16),
        name="score",
    )(place, own, other, *samples, *pieces)


def swap(value, axis, bit):
    return lax.ppermute(value, axis, [(i, i ^ bit) for i in range(lax.axis_size(axis))])


def after(value, earlier):
    return lax.optimization_barrier((value, earlier))[0]


def local_owned(acts, grads, proj_in, proj_out, queries):
    seqs, length, _ = acts.shape
    parts = lax.axis_size("dp")
    tokens = seqs * length * parts
    column = lax.axis_index("tensor").astype(jnp.int32)
    side = (column >= 2).astype(jnp.int32).reshape(1)
    place = lax.axis_index("dp").astype(jnp.int32).reshape(1)
    half = seqs // 2
    x = project_in(side, acts, proj_in)
    x_outer = inwards(x)
    (g,) = project_out(side, grads, proj_out, queries, 0, half, x, False)
    g_outer = inwards(g)
    h, packed = project_out(side, grads, proj_out, queries, half, seqs - half, g, True)
    h_outer = inwards(h)
    far = jnp.concatenate([x[1] + after(x_outer, h)[1], g[1] + after(g_outer, h)[1]], axis=1)
    other = across(far)
    pieces = [after(packed, far)[None]]
    bit = 1
    while bit < parts:
        mine = pieces[0] if bit == 1 else jnp.concatenate(pieces, axis=0)
        pieces = [mine, swap(mine, "dp", bit)]
        bit *= 2
    h_far = h[1] + after(h_outer, pieces[0])[1]
    h_other = across(h_far)
    x_rest, cov, sample = first_half(x, x_outer, g, g_outer, other, h_far, half)
    cov, last = second_half(x_rest, cov, h, h_outer, h_other, seqs - half)
    other = jnp.zeros_like(cov)
    bit = 1
    while bit < parts:
        cov = cov if bit == 1 else cov + other
        other = swap(cov, "dp", bit)
        bit *= 2
    scores = score(place, cov, other, [sample, last], pieces, tokens)
    scores = scores + across(scores)
    outer = lax.ppermute(scores, "tensor", [(1, 0), (2, 3)])
    return jnp.where((column == 1) | (column == 2), scores, outer)


def damp(matrix):
    size = matrix.shape[0]
    shift_by = 0.1 * jnp.trace(matrix) / size
    return matrix + shift_by * jnp.eye(size, dtype=matrix.dtype)


def chol_apply(factor, rhs):
    lower_sol = lax.linalg.triangular_solve(factor, rhs, left_side=True, lower=True)
    return lax.linalg.triangular_solve(
        factor, lower_sol, left_side=True, lower=True, transpose_a=True
    )


def precondition(query, left, right_side):
    count, rank = (query.shape[0], query.shape[1])
    left_fac = jnp.linalg.cholesky(left)
    right_fac = jnp.linalg.cholesky(right_side)
    stacked = jnp.transpose(query, (1, 0, 2)).reshape(rank, count * rank)
    middle = chol_apply(left_fac, stacked).reshape(rank, count, rank)
    turned = jnp.transpose(middle, (2, 1, 0)).reshape(rank, count * rank)
    result = chol_apply(right_fac, turned).reshape(rank, count, rank)
    return jnp.transpose(result, (1, 2, 0))


def diagonal_blocks(whole, rank):
    return jnp.stack([whole[:, 0:rank, 0:rank], whole[:, rank : 2 * rank, rank : 2 * rank]], axis=1)


def local_general(acts, grads, proj_in, proj_out, queries):
    seq_count, length, width_loc = acts.shape
    rank = proj_in.shape[1]
    hidden_loc = grads.shape[3]
    flat = acts.reshape(-1, width_loc)
    xpart = nt(flat, proj_in.reshape(2 * rank, width_loc))
    gpart = jnp.concatenate(
        [nt(grads[layer].reshape(-1, hidden_loc), proj_out[layer]) for layer in range(2)], axis=1
    )
    count = seq_count * length * lax.axis_size("dp")
    xin, gout = lax.psum((xpart, gpart), "tensor")
    in_cov, out_cov = lax.psum((tn(xin, xin, HIGHEST), tn(gout, gout, HIGHEST)), "dp")
    whole = (
        jnp.einsum(
            "sto,sti->soi",
            gout.reshape(seq_count, length, 2 * rank),
            xin.reshape(seq_count, length, 2 * rank),
            precision=HIGHEST,
        )
        / length
    )
    samples = diagonal_blocks(whole, rank)
    in_cov = in_cov / count
    out_cov = out_cov / count
    precond = []
    for layer in range(2):
        low = layer * rank
        damped_in = damp(in_cov[low : low + rank, low : low + rank])
        damped_out = damp(out_cov[low : low + rank, low : low + rank])
        precond.append(precondition(queries[:, layer].astype(jnp.float32), damped_out, damped_in))
    query_count = queries.shape[0]
    query_b = jnp.stack(precond, axis=1).astype(jnp.bfloat16).reshape(query_count, -1)
    sample_b = samples.astype(jnp.bfloat16).reshape(seq_count, -1)
    return nt(sample_b, lax.all_gather(query_b, "dp", axis=0, tiled=True))


def local(acts, grads, proj_in, proj_out, queries):
    parts = lax.axis_size("dp")
    even = parts > 1 and parts & (parts - 1) == 0
    if lax.axis_size("tensor") == 4 and even and acts.shape[0] > 1 and queries.shape[0] % 8 == 0:
        return local_owned(acts, grads, proj_in, proj_out, queries)
    return local_general(acts, grads, proj_in, proj_out, queries)


def solution(mesh):
    placed = (
        P(("groups", "dp"), None, "tensor"),
        P(None, ("groups", "dp"), None, "tensor"),
        P(None, None, "tensor"),
        P(None, None, "tensor"),
        P("dp", None, None, None),
    )
    return jax.shard_map(
        local, mesh=mesh, in_specs=placed, out_specs=P(("groups", "dp"), None), check_vma=False
    )
```

```python
import functools

import jax
import jax.numpy as jnp
from jax import lax
from jax.experimental import pallas as pl
from jax.experimental.pallas import tpu as pltpu
from jax.sharding import PartitionSpec as P

HIGHEST = lax.Precision.HIGHEST
MIB = 1024 * 1024


def nt(a, b, precision=None):
    return lax.dot_general(
        a, b, (((1,), (1,)), ((), ())), precision=precision, preferred_element_type=jnp.float32
    )


def tn(a, b, precision=None):
    return lax.dot_general(
        a, b, (((0,), (0,)), ((), ())), precision=precision, preferred_element_type=jnp.float32
    )


def nn(a, b, precision=None):
    return jnp.dot(a, b, precision=precision, preferred_element_type=jnp.float32)


def vmem():
    return pl.BlockSpec(memory_space=pltpu.VMEM)


def smem():
    return pl.BlockSpec(memory_space=pltpu.SMEM)


def hbm():
    return pl.BlockSpec(memory_space=pl.ANY)


def in_hbm(value):
    return pltpu.with_memory_space_constraint(value, pltpu.HBM)


def params(mib):
    return pltpu.CompilerParams(vmem_limit_bytes=mib * MIB)


def project_in_kernel(side_ref, rows_hbm, proj_hbm, out, rows, proj, sems, proj_sem):
    seqs, length, width = rows.shape
    rank = proj.shape[1]
    proj_copy = pltpu.make_async_copy(proj_hbm, proj, proj_sem)
    proj_copy.start()

    def copy(s):
        return pltpu.make_async_copy(rows_hbm.at[s], rows.at[s], sems.at[s])

    for s in range(seqs):
        copy(s).start()
    proj_copy.wait()

    @pl.loop(0, seqs)
    def _(s):
        copy(s).wait()
        part = nt(rows[s], proj[...].reshape(2 * rank, width)).T
        tokens = pl.ds(pl.multiple_of(s * length, length), length)
        out[side_ref[0], :, tokens] = part[:rank]
        out[1 - side_ref[0], :, tokens] = part[rank:]


def project_in(side, rows, proj):
    seqs, length, _ = rows.shape
    rank = proj.shape[1]
    return pl.pallas_call(
        project_in_kernel,
        in_specs=[smem(), hbm(), hbm()],
        out_specs=vmem(),
        out_shape=jax.ShapeDtypeStruct((2, rank, seqs * length), jnp.float32),
        scratch_shapes=[
            pltpu.VMEM(rows.shape, rows.dtype),
            pltpu.VMEM(proj.shape, proj.dtype),
            pltpu.SemaphoreType.DMA((seqs,)),
            pltpu.SemaphoreType.DMA,
        ],
        compiler_params=params(16),
        name="project_in",
    )(side, in_hbm(rows), in_hbm(proj))


def project_out_kernel(first, side_ref, rows_hbm, proj_ref, queries_hbm, after, out, *refs):
    del after
    packed, (rows, held, sems, sem) = refs[:-4], refs[-4:]
    _, seqs, length, width = rows.shape
    half = width // 2

    def chunk(layer, s, part):
        lanes = pl.ds(part * half, half)
        return pltpu.make_async_copy(
            rows_hbm.at[layer, first + s, :, lanes],
            rows.at[layer, s, :, lanes],
            sems.at[layer, s, part],
        )

    for s in range(seqs):
        for part in range(2):
            for layer in range(2):
                chunk(layer, s, part).start()
    if packed:
        copy = pltpu.make_async_copy(queries_hbm.at[:, side_ref[0]], held, sem)
        copy.start()

    @pl.loop(0, seqs)
    def _(s):
        values = [None, None]
        for part in range(2):
            lanes = slice(part * half, (part + 1) * half)
            for layer in range(2):
                chunk(layer, s, part).wait()
            for layer in range(2):
                value = nt(rows[layer, s, :, lanes], proj_ref[layer, :, lanes])
                values[layer] = value if part == 0 else values[layer] + value
        tokens = pl.ds(pl.multiple_of(s * length, length), length)
        turned = jnp.concatenate(values, axis=1).T
        rank = turned.shape[0] // 2
        out[side_ref[0], :, tokens] = turned[:rank]
        out[1 - side_ref[0], :, tokens] = turned[rank:]

    if packed:
        copy.wait()
        blocks = held.shape[0] // 2
        for k in range(blocks):
            pair = [held[k].astype(jnp.float32), held[k + blocks].astype(jnp.float32)]
            packed[0][k] = jnp.concatenate(pair, axis=1).astype(held.dtype)


def project_out(side, rows, proj, queries, first, seqs, after, packs):
    _, _, length, width = rows.shape
    rank = proj.shape[1]
    count = queries.shape[0]
    out_shape = [jax.ShapeDtypeStruct((2, rank, seqs * length), jnp.float32)]
    if packs:
        out_shape.append(jax.ShapeDtypeStruct((count // 2, rank, 2 * rank), queries.dtype))
    return pl.pallas_call(
        functools.partial(project_out_kernel, first),
        in_specs=[smem(), hbm(), vmem(), hbm(), hbm()],
        out_specs=[vmem()] * len(out_shape),
        out_shape=out_shape,
        scratch_shapes=[
            pltpu.VMEM((2, seqs, length, width), rows.dtype),
            pltpu.VMEM((count, rank, rank), queries.dtype),
            pltpu.SemaphoreType.DMA((2, seqs, 2)),
            pltpu.SemaphoreType.DMA,
        ],
        compiler_params=params(24),
        name="project_out",
    )(side, in_hbm(rows), proj, in_hbm(queries), after)


def inwards(value):
    return lax.ppermute(value, "tensor", [(0, 1), (3, 2)])


def across(value):
    return lax.ppermute(value, "tensor", [(1, 2), (2, 1)])


def covariance(value, right):
    none = jnp.zeros_like(value)
    both = [none, value] if right else [value, none]
    return nt(value, jnp.concatenate(both, axis=0), HIGHEST)


def samples_of(x, g, sample_out):
    seqs = sample_out.shape[0]
    length = g.shape[1] // seqs
    for s in range(seqs):
        tokens = slice(s * length, (s + 1) * length)
        sample = nt(x[:, tokens], g[:, tokens], HIGHEST) / length
        sample = sample.astype(jnp.bfloat16).astype(jnp.float32)
        sample_out[s] = jnp.concatenate([sample, sample], axis=1)


def first_kernel(x_ref, x_outer, g_ref, g_outer, other, after, x_out, cov_out, sample_out):
    del after
    tokens = x_ref.shape[2]
    here = g_ref.shape[2]
    x = x_ref[0] + x_outer[0] + other[:, :tokens]
    x_out[...] = x[:, here:]
    g = g_ref[0] + g_outer[0] + other[:, tokens:]
    cov_out[...] = covariance(x, False) + covariance(g, True)
    samples_of(x[:, :here], g, sample_out)


def second_kernel(x_ref, cov_ref, h_ref, h_outer, other, cov_out, sample_out):
    h = h_ref[0] + h_outer[0] + other[...]
    cov_out[...] = cov_ref[...] + covariance(h, True)
    samples_of(x_ref[...], h, sample_out)


def first_half(x, x_outer, g, g_outer, other, after, seqs):
    _, rank, tokens = x.shape
    here = g.shape[2]
    return pl.pallas_call(
        first_kernel,
        in_specs=[vmem()] * 5 + [hbm()],
        out_specs=[vmem()] * 3,
        out_shape=[
            jax.ShapeDtypeStruct((rank, tokens - here), jnp.float32),
            jax.ShapeDtypeStruct((rank, 2 * rank), jnp.float32),
            jax.ShapeDtypeStruct((seqs, rank, 2 * rank), jnp.float32),
        ],
        compiler_params=params(16),
        name="first_half",
    )(x, x_outer, g, g_outer, other, after)


def second_half(x, cov, h, h_outer, other, seqs):
    rank = x.shape[0]
    return pl.pallas_call(
        second_kernel,
        in_specs=[vmem()] * 5,
        out_specs=[vmem()] * 2,
        out_shape=[
            jax.ShapeDtypeStruct((rank, 2 * rank), jnp.float32),
            jax.ShapeDtypeStruct((seqs, rank, 2 * rank), jnp.float32),
        ],
        compiler_params=params(16),
        name="second_half",
    )(x, cov, h, h_outer, other)


def scales(steps, spread):
    r = (spread - 1.0) / (spread + 1.0)
    out = []
    for _ in range(steps):
        out.append(2.0 / (2.0 - r * r))
        r = r * r / (2.0 - r * r)
    return out


def damped_inverses(pair):
    size, both = pair.shape
    left = lax.broadcasted_iota(jnp.int32, pair.shape, 1) < size
    whole = jnp.concatenate([jnp.where(left, pair, 0.0), jnp.where(left, 0.0, pair)], axis=0)
    rows = lax.broadcasted_iota(jnp.int32, whole.shape, 0)
    cols = lax.broadcasted_iota(jnp.int32, whole.shape, 1)
    diagonal = rows == cols
    on_diagonal = jnp.where(diagonal, whole, 0.0)
    unit = jnp.where(
        rows < size, jnp.sum(on_diagonal[:size]) / size, jnp.sum(on_diagonal[size:]) / size
    )
    eye = jnp.where(diagonal, 1.0, 0.0)
    matrix = whole / unit + 0.1 * eye
    low, high = 0.1, size + 0.1
    start = 2.0 / (low + high)
    steps = scales(7, high / low)
    y = matrix * start
    x = (2.0 * start * steps[0]) * eye - (start * steps[0]) * y
    y = steps[0] * (2.0 * y - nn(y, y, HIGHEST))

    for scale in steps[1:-1]:
        product = nn(jnp.concatenate([x, y], axis=0), y, HIGHEST)
        x = scale * (2.0 * x - product[:both])
        y = scale * (2.0 * y - product[both:])
    x = steps[-1] * (2.0 * x - nn(x, y, HIGHEST))
    x = x + nn(x, eye - nn(matrix, x, HIGHEST), HIGHEST)
    return x / unit


def split(value):
    high = value.astype(jnp.bfloat16)
    rest = value - high.astype(jnp.float32)
    middle = rest.astype(jnp.bfloat16)
    low = (rest - middle.astype(jnp.float32)).astype(jnp.bfloat16)
    return high, middle, low


def score_kernel(tokens, place_ref, own_ref, other_ref, first_ref, second_ref, *refs):
    pieces, (out, held, half) = refs[:-3], refs[-3:]
    parts = held.shape[0]
    k = 0
    for piece in pieces:
        for place in range(piece.shape[0]):
            held[place_ref[0] ^ k] = piece[place]
            k += 1
    inverses = damped_inverses((own_ref[...] + other_ref[...]) / tokens)
    both = inverses.shape[0]
    size = both // 2
    samples = [ref[s] for ref in (first_ref, second_ref) for s in range(ref.shape[0])]
    seqs = len(samples)
    blocks = held.shape[1]
    pairs = parts * blocks
    first = jnp.concatenate(split(inverses[:size, :size]), axis=0)
    none = jnp.zeros_like(first)
    first = jnp.concatenate(
        [jnp.concatenate([first, none], axis=1), jnp.concatenate([none, first], axis=1)], axis=0
    )
    right = inverses[size:]
    twice = jnp.concatenate([pltpu.roll(right, size, 1), right], axis=0)
    high, middle, _ = split(twice)
    once = jnp.concatenate([high, middle], axis=1)
    second = jnp.concatenate([once, once], axis=0)

    for part in range(parts // 2):
        for block in range(0, blocks, 2):
            rows = jnp.concatenate(
                [
                    held[part, block],
                    held[part + parts // 2, block],
                    held[part, block + 1],
                    held[part + parts // 2, block + 1],
                ],
                axis=0,
            )
            result = nt(first, rows)
            for k in range(2):
                three = result[3 * size * k : 3 * size * (k + 1)]
                value = three[:size] + three[size : 2 * size] + three[2 * size :]
                high, middle, _ = split(value)
                pair = (2 * part + k) * blocks + block
                lanes = slice(pair * both, (pair + 2) * both)
                half[0, :, lanes] = high
                half[1, :, lanes] = middle
    lines = [[] for _ in range(seqs)]
    for pair in range(pairs):
        lanes = slice(pair * both, (pair + 1) * both)
        rows = jnp.concatenate([half[0, :, lanes], half[1, :, lanes]], axis=1)
        result = nn(rows, second)
        result = (result[:, :both] + result[:, both:]).astype(jnp.bfloat16).astype(jnp.float32)
        for s in range(seqs):
            lines[s].append(jnp.sum(result * samples[s], axis=0, keepdims=True))
    lines = jnp.concatenate([line for part in lines for line in part], axis=0)
    shape = (8, both)
    ends = jnp.where(
        (lax.broadcasted_iota(jnp.int32, shape, 1) < size)
        == (lax.broadcasted_iota(jnp.int32, shape, 0) == 0),
        1.0,
        0.0,
    )
    result = nt(ends, lines, HIGHEST)
    for s in range(seqs):
        for k in range(2):
            out[s : s + 1, k * pairs : (k + 1) * pairs] = result[
                k : k + 1, s * pairs : (s + 1) * pairs
            ]


def score(place, own, other, samples, pieces, tokens):
    _, blocks, rank, both = pieces[0].shape
    parts = sum(piece.shape[0] for piece in pieces)
    pairs = parts * blocks
    seqs = sum(sample.shape[0] for sample in samples)
    return pl.pallas_call(
        functools.partial(score_kernel, tokens),
        in_specs=[smem()] + [vmem()] * (4 + len(pieces)),
        out_specs=vmem(),
        out_shape=jax.ShapeDtypeStruct((seqs, 2 * pairs), jnp.float32),
        scratch_shapes=[
            pltpu.VMEM((parts, blocks, rank, both), pieces[0].dtype),
            pltpu.VMEM((2, rank, pairs * both), jnp.bfloat16),
        ],
        compiler_params=params(16),
        name="score",
    )(place, own, other, *samples, *pieces)


def swap(value, axis, bit):
    return lax.ppermute(value, axis, [(i, i ^ bit) for i in range(lax.axis_size(axis))])


def after(value, earlier):
    return lax.optimization_barrier((value, earlier))[0]


def local_owned(acts, grads, proj_in, proj_out, queries):
    seqs, length, _ = acts.shape
    parts = lax.axis_size("dp")
    tokens = seqs * length * parts
    column = lax.axis_index("tensor").astype(jnp.int32)
    side = (column >= 2).astype(jnp.int32).reshape(1)
    place = lax.axis_index("dp").astype(jnp.int32).reshape(1)
    half = seqs // 2
    x = project_in(side, acts, proj_in)
    x_outer = inwards(x)
    (g,) = project_out(side, grads, proj_out, queries, 0, half, x, False)
    g_outer = inwards(g)
    h, packed = project_out(side, grads, proj_out, queries, half, seqs - half, g, True)
    h_outer = inwards(h)
    far = jnp.concatenate([x[1] + after(x_outer, h)[1], g[1] + after(g_outer, h)[1]], axis=1)
    other = across(far)
    pieces = [after(packed, far)[None]]
    bit = 1
    while bit < parts:
        mine = pieces[0] if bit == 1 else jnp.concatenate(pieces, axis=0)
        pieces = [mine, swap(mine, "dp", bit)]
        bit *= 2
    h_far = h[1] + after(h_outer, pieces[0])[1]
    h_other = across(h_far)
    x_rest, cov, sample = first_half(x, x_outer, g, g_outer, other, h_far, half)
    cov, last = second_half(x_rest, cov, h, h_outer, h_other, seqs - half)
    other = jnp.zeros_like(cov)
    bit = 1
    while bit < parts:
        cov = cov if bit == 1 else cov + other
        other = swap(cov, "dp", bit)
        bit *= 2
    scores = score(place, cov, other, [sample, last], pieces, tokens)
    scores = scores + across(scores)
    outer = lax.ppermute(scores, "tensor", [(1, 0), (2, 3)])
    return jnp.where((column == 1) | (column == 2), scores, outer)


def damp(matrix):
    size = matrix.shape[0]
    shift_by = 0.1 * jnp.trace(matrix) / size
    return matrix + shift_by * jnp.eye(size, dtype=matrix.dtype)


def chol_apply(factor, rhs):
    lower_sol = lax.linalg.triangular_solve(factor, rhs, left_side=True, lower=True)
    return lax.linalg.triangular_solve(
        factor, lower_sol, left_side=True, lower=True, transpose_a=True
    )


def precondition(query, left, right_side):
    count, rank = (query.shape[0], query.shape[1])
    left_fac = jnp.linalg.cholesky(left)
    right_fac = jnp.linalg.cholesky(right_side)
    stacked = jnp.transpose(query, (1, 0, 2)).reshape(rank, count * rank)
    middle = chol_apply(left_fac, stacked).reshape(rank, count, rank)
    turned = jnp.transpose(middle, (2, 1, 0)).reshape(rank, count * rank)
    result = chol_apply(right_fac, turned).reshape(rank, count, rank)
    return jnp.transpose(result, (1, 2, 0))


def diagonal_blocks(whole, rank):
    return jnp.stack([whole[:, 0:rank, 0:rank], whole[:, rank : 2 * rank, rank : 2 * rank]], axis=1)


def local_general(acts, grads, proj_in, proj_out, queries):
    seq_count, length, width_loc = acts.shape
    rank = proj_in.shape[1]
    hidden_loc = grads.shape[3]
    flat = acts.reshape(-1, width_loc)
    xpart = nt(flat, proj_in.reshape(2 * rank, width_loc))
    gpart = jnp.concatenate(
        [nt(grads[layer].reshape(-1, hidden_loc), proj_out[layer]) for layer in range(2)], axis=1
    )
    count = seq_count * length * lax.axis_size("dp")
    xin, gout = lax.psum((xpart, gpart), "tensor")
    in_cov, out_cov = lax.psum((tn(xin, xin, HIGHEST), tn(gout, gout, HIGHEST)), "dp")
    whole = (
        jnp.einsum(
            "sto,sti->soi",
            gout.reshape(seq_count, length, 2 * rank),
            xin.reshape(seq_count, length, 2 * rank),
            precision=HIGHEST,
        )
        / length
    )
    samples = diagonal_blocks(whole, rank)
    in_cov = in_cov / count
    out_cov = out_cov / count
    precond = []
    for layer in range(2):
        low = layer * rank
        damped_in = damp(in_cov[low : low + rank, low : low + rank])
        damped_out = damp(out_cov[low : low + rank, low : low + rank])
        precond.append(precondition(queries[:, layer].astype(jnp.float32), damped_out, damped_in))
    query_count = queries.shape[0]
    query_b = jnp.stack(precond, axis=1).astype(jnp.bfloat16).reshape(query_count, -1)
    sample_b = samples.astype(jnp.bfloat16).reshape(seq_count, -1)
    return nt(sample_b, lax.all_gather(query_b, "dp", axis=0, tiled=True))


def local(acts, grads, proj_in, proj_out, queries):
    parts = lax.axis_size("dp")
    even = parts > 1 and parts & (parts - 1) == 0
    if lax.axis_size("tensor") == 4 and even and acts.shape[0] > 1 and queries.shape[0] % 8 == 0:
        return local_owned(acts, grads, proj_in, proj_out, queries)
    return local_general(acts, grads, proj_in, proj_out, queries)


def solution(mesh):
    placed = (
        P(("groups", "dp"), None, "tensor"),
        P(None, ("groups", "dp"), None, "tensor"),
        P(None, None, "tensor"),
        P(None, None, "tensor"),
        P("dp", None, None, None),
    )
    return jax.shard_map(
        local, mesh=mesh, in_specs=placed, out_specs=P(("groups", "dp"), None), check_vma=False
    )
```

```python
import functools

import jax
import jax.numpy as jnp
from jax import lax
from jax.experimental import pallas as pl
from jax.experimental.pallas import tpu as pltpu
from jax.sharding import PartitionSpec as P

HIGHEST = lax.Precision.HIGHEST
MIB = 1024 * 1024


def nt(a, b, precision=None):
    return lax.dot_general(
        a, b, (((1,), (1,)), ((), ())), precision=precision, preferred_element_type=jnp.float32
    )


def tn(a, b, precision=None):
    return lax.dot_general(
        a, b, (((0,), (0,)), ((), ())), precision=precision, preferred_element_type=jnp.float32
    )


def nn(a, b, precision=None):
    return jnp.dot(a, b, precision=precision, preferred_element_type=jnp.float32)


def vmem():
    return pl.BlockSpec(memory_space=pltpu.VMEM)


def smem():
    return pl.BlockSpec(memory_space=pltpu.SMEM)


def hbm():
    return pl.BlockSpec(memory_space=pl.ANY)


def in_hbm(value):
    return pltpu.with_memory_space_constraint(value, pltpu.HBM)


def params(mib):
    return pltpu.CompilerParams(vmem_limit_bytes=mib * MIB)


def project_in_kernel(side_ref, rows_hbm, proj_hbm, out, rows, proj, sems, proj_sem):
    seqs, length, width = rows.shape
    rank = proj.shape[1]
    proj_copy = pltpu.make_async_copy(proj_hbm, proj, proj_sem)
    proj_copy.start()

    def copy(s):
        return pltpu.make_async_copy(rows_hbm.at[s], rows.at[s], sems.at[s])

    for s in range(seqs):
        copy(s).start()
    proj_copy.wait()

    group = 2 - seqs % 2

    @pl.loop(0, seqs // group)
    def _(step):
        for k in range(group):
            copy(step * group + k).wait()
        for k in range(group):
            s = step * group + k
            part = nt(proj[...].reshape(2 * rank, width), rows[s])
            tokens = pl.ds(pl.multiple_of(s * length, length), length)
            out[side_ref[0], :, tokens] = part[:rank]
            out[1 - side_ref[0], :, tokens] = part[rank:]


def project_in(side, rows, proj):
    seqs, length, _ = rows.shape
    rank = proj.shape[1]
    return pl.pallas_call(
        project_in_kernel,
        in_specs=[smem(), hbm(), hbm()],
        out_specs=vmem(),
        out_shape=jax.ShapeDtypeStruct((2, rank, seqs * length), jnp.float32),
        scratch_shapes=[
            pltpu.VMEM(rows.shape, rows.dtype),
            pltpu.VMEM(proj.shape, proj.dtype),
            pltpu.SemaphoreType.DMA((seqs,)),
            pltpu.SemaphoreType.DMA,
        ],
        compiler_params=params(16),
        name="project_in",
    )(side, in_hbm(rows), in_hbm(proj))


def project_out_kernel(side_ref, rows_hbm, proj_ref, queries_hbm, after, *refs):
    del after
    (near, far, packed), (rows, held, acc, sems, sem) = refs[:3], refs[3:]
    _, seqs, length, width = rows.shape
    parts = sems.shape[2]
    piece = width // parts
    copies = {}
    for s in range(seqs):
        for part in range(parts):
            lanes = pl.ds(part * piece, piece)
            for layer in range(2):
                copies[s, part, layer] = pltpu.make_async_copy(
                    rows_hbm.at[layer, s, :, lanes],
                    rows.at[layer, s, :, lanes],
                    sems.at[layer, s, part],
                )
                copies[s, part, layer].start()
    copy = pltpu.make_async_copy(queries_hbm.at[:, side_ref[0]], held, sem)
    copy.start()
    for s in range(seqs):
        tokens = slice(s * length, (s + 1) * length)
        for part in range(parts):
            lanes = slice(part * piece, (part + 1) * piece)
            for layer in range(2):
                copies[s, part, layer].wait()
            for layer in range(2):
                value = nt(proj_ref[layer, :, lanes], rows[layer, s, :, lanes])
                if part > 0:
                    value = value + acc[layer, :, tokens]
                acc[layer, :, tokens] = value
    far[...] = acc[1 - side_ref[0]]
    near[...] = acc[side_ref[0]]
    copy.wait()
    blocks = held.shape[0] // 2
    for k in range(blocks):
        pair = [held[k].astype(jnp.float32), held[k + blocks].astype(jnp.float32)]
        packed[k] = jnp.concatenate(pair, axis=1).astype(held.dtype)


def project_out(side, rows, proj, queries, after):
    _, seqs, length, width = rows.shape
    rank = proj.shape[1]
    count = queries.shape[0]
    parts = 4 if width % 512 == 0 else 1
    return pl.pallas_call(
        project_out_kernel,
        in_specs=[smem(), hbm(), vmem(), hbm(), hbm()],
        out_specs=[vmem()] * 3,
        out_shape=[
            jax.ShapeDtypeStruct((rank, seqs * length), jnp.float32),
            jax.ShapeDtypeStruct((rank, seqs * length), jnp.float32),
            jax.ShapeDtypeStruct((count // 2, rank, 2 * rank), queries.dtype),
        ],
        scratch_shapes=[
            pltpu.VMEM(rows.shape, rows.dtype),
            pltpu.VMEM((count, rank, rank), queries.dtype),
            pltpu.VMEM((2, rank, seqs * length), jnp.float32),
            pltpu.SemaphoreType.DMA((2, seqs, parts)),
            pltpu.SemaphoreType.DMA,
        ],
        compiler_params=params(40),
        name="project_out",
    )(side, in_hbm(rows), proj, in_hbm(queries), after)


def inwards(value):
    return lax.ppermute(value, "tensor", [(0, 1), (3, 2)])


def across(value):
    return lax.ppermute(value, "tensor", [(1, 2), (2, 1)])


def covariance(value, right):
    none = jnp.zeros_like(value)
    both = [none, value] if right else [value, none]
    return nt(value, jnp.concatenate(both, axis=0), HIGHEST)


def samples_of(x, g, sample_out):
    seqs = sample_out.shape[0]
    length = g.shape[1] // seqs
    for s in range(seqs):
        tokens = slice(s * length, (s + 1) * length)
        sample = nt(x[:, tokens], g[:, tokens], HIGHEST) / length
        sample = sample.astype(jnp.bfloat16).astype(jnp.float32)
        sample_out[s] = jnp.concatenate([sample, sample], axis=1)


def covariances_kernel(x_ref, x_outer, near, near_outer, far_outer, other, cov_out, sample_out):
    tokens = near.shape[1]
    x = x_ref[0] + x_outer[0] + other[:, :tokens]
    g = (near[...] + near_outer[...]) + (far_outer[...] + other[:, tokens:])
    cov_out[...] = covariance(x, False) + covariance(g, True)
    samples_of(x, g, sample_out)


def covariances(x, x_outer, near, near_outer, far_outer, other, seqs):
    rank = near.shape[0]
    return pl.pallas_call(
        covariances_kernel,
        in_specs=[vmem()] * 6,
        out_specs=[vmem()] * 2,
        out_shape=[
            jax.ShapeDtypeStruct((rank, 2 * rank), jnp.float32),
            jax.ShapeDtypeStruct((seqs, rank, 2 * rank), jnp.float32),
        ],
        compiler_params=params(16),
        name="covariances",
    )(x, x_outer, near, near_outer, far_outer, other)


def scales(steps, spread):
    r = (spread - 1.0) / (spread + 1.0)
    out = []
    for _ in range(steps):
        out.append(2.0 / (2.0 - r * r))
        r = r * r / (2.0 - r * r)
    return out


def damped_inverses(pair):
    size, both = pair.shape
    left = lax.broadcasted_iota(jnp.int32, pair.shape, 1) < size
    whole = jnp.concatenate([jnp.where(left, pair, 0.0), jnp.where(left, 0.0, pair)], axis=0)
    rows = lax.broadcasted_iota(jnp.int32, whole.shape, 0)
    cols = lax.broadcasted_iota(jnp.int32, whole.shape, 1)
    diagonal = rows == cols
    on_diagonal = jnp.where(diagonal, whole, 0.0)
    unit = jnp.where(
        rows < size, jnp.sum(on_diagonal[:size]) / size, jnp.sum(on_diagonal[size:]) / size
    )
    eye = jnp.where(diagonal, 1.0, 0.0)
    matrix = whole / unit + 0.1 * eye
    low, high = 0.1, size + 0.1
    start = 2.0 / (low + high)
    steps = scales(7, high / low)
    y = matrix * start
    x = (2.0 * start * steps[0]) * eye - (start * steps[0]) * y
    y = steps[0] * (2.0 * y - nn(y, y, HIGHEST))

    for scale in steps[1:-1]:
        product = nn(jnp.concatenate([x, y], axis=0), y, HIGHEST)
        x = scale * (2.0 * x - product[:both])
        y = scale * (2.0 * y - product[both:])
    x = steps[-1] * (2.0 * x - nn(x, y, HIGHEST))
    x = x + nn(x, eye - nn(matrix, x, HIGHEST), HIGHEST)
    return x / unit


def split(value):
    high = value.astype(jnp.bfloat16)
    rest = value - high.astype(jnp.float32)
    middle = rest.astype(jnp.bfloat16)
    low = (rest - middle.astype(jnp.float32)).astype(jnp.bfloat16)
    return high, middle, low


def score_kernel(tokens, place_ref, own_ref, other_ref, sample_ref, *refs):
    pieces, (out, held, half) = refs[:-3], refs[-3:]
    parts = held.shape[0]
    k = 0
    for piece in pieces:
        for place in range(piece.shape[0]):
            held[place_ref[0] ^ k] = piece[place]
            k += 1
    inverses = damped_inverses((own_ref[...] + other_ref[...]) / tokens)
    both = inverses.shape[0]
    size = both // 2
    samples = [sample_ref[s] for s in range(sample_ref.shape[0])]
    seqs = len(samples)
    blocks = held.shape[1]
    pairs = parts * blocks
    first = jnp.concatenate(split(inverses[:size, :size]), axis=0)
    none = jnp.zeros_like(first)
    first = jnp.concatenate(
        [jnp.concatenate([first, none], axis=1), jnp.concatenate([none, first], axis=1)], axis=0
    )
    right = inverses[size:]
    twice = jnp.concatenate([pltpu.roll(right, size, 1), right], axis=0)
    high, middle, _ = split(twice)
    once = jnp.concatenate([high, middle], axis=1)
    second = jnp.concatenate([once, once], axis=0)

    for part in range(parts // 2):
        for block in range(0, blocks, 2):
            rows = jnp.concatenate(
                [
                    held[part, block],
                    held[part + parts // 2, block],
                    held[part, block + 1],
                    held[part + parts // 2, block + 1],
                ],
                axis=0,
            )
            result = nt(first, rows)
            for k in range(2):
                three = result[3 * size * k : 3 * size * (k + 1)]
                value = three[:size] + three[size : 2 * size] + three[2 * size :]
                high, middle, _ = split(value)
                pair = (2 * part + k) * blocks + block
                lanes = slice(pair * both, (pair + 2) * both)
                half[0, :, lanes] = high
                half[1, :, lanes] = middle
    lines = [[] for _ in range(seqs)]
    for pair in range(pairs):
        lanes = slice(pair * both, (pair + 1) * both)
        rows = jnp.concatenate([half[0, :, lanes], half[1, :, lanes]], axis=1)
        result = nn(rows, second)
        result = (result[:, :both] + result[:, both:]).astype(jnp.bfloat16).astype(jnp.float32)
        for s in range(seqs):
            lines[s].append(jnp.sum(result * samples[s], axis=0, keepdims=True))
    lines = jnp.concatenate([line for part in lines for line in part], axis=0)
    shape = (8, both)
    ends = jnp.where(
        (lax.broadcasted_iota(jnp.int32, shape, 1) < size)
        == (lax.broadcasted_iota(jnp.int32, shape, 0) == 0),
        1.0,
        0.0,
    )
    result = nt(ends, lines, HIGHEST)
    for s in range(seqs):
        for k in range(2):
            out[s : s + 1, k * pairs : (k + 1) * pairs] = result[
                k : k + 1, s * pairs : (s + 1) * pairs
            ]


def score(place, own, other, sample, pieces, tokens):
    _, blocks, rank, both = pieces[0].shape
    parts = sum(piece.shape[0] for piece in pieces)
    pairs = parts * blocks
    seqs = sample.shape[0]
    return pl.pallas_call(
        functools.partial(score_kernel, tokens),
        in_specs=[smem()] + [vmem()] * (3 + len(pieces)),
        out_specs=vmem(),
        out_shape=jax.ShapeDtypeStruct((seqs, 2 * pairs), jnp.float32),
        scratch_shapes=[
            pltpu.VMEM((parts, blocks, rank, both), pieces[0].dtype),
            pltpu.VMEM((2, rank, pairs * both), jnp.bfloat16),
        ],
        compiler_params=params(16),
        name="score",
    )(place, own, other, sample, *pieces)


def swap(value, axis, bit):
    return lax.ppermute(value, axis, [(i, i ^ bit) for i in range(lax.axis_size(axis))])


def after(value, earlier):
    return lax.optimization_barrier((value, earlier))[0]


def local_owned(acts, grads, proj_in, proj_out, queries):
    seqs, length, _ = acts.shape
    parts = lax.axis_size("dp")
    tokens = seqs * length * parts
    column = lax.axis_index("tensor").astype(jnp.int32)
    side = (column >= 2).astype(jnp.int32).reshape(1)
    place = lax.axis_index("dp").astype(jnp.int32).reshape(1)
    x = project_in(side, acts, proj_in)
    x_outer = inwards(x)
    near, far, packed = project_out(side, grads, proj_out, queries, x)
    far_outer = lax.ppermute(far, "tensor", [(0, 2), (3, 1)])
    crossing = jnp.concatenate([x[1] + after(x_outer, far)[1], far], axis=1)
    other = across(crossing)
    near_outer = inwards(near)
    pieces = [after(packed, crossing)[None]]
    bit = 1
    while bit < parts:
        mine = pieces[0] if bit == 1 else jnp.concatenate(pieces, axis=0)
        pieces = [mine, swap(mine, "dp", bit)]
        bit *= 2
    cov, sample = covariances(x, x_outer, near, near_outer, far_outer, other, seqs)
    other = jnp.zeros_like(cov)
    bit = 1
    while bit < parts:
        cov = cov if bit == 1 else cov + other
        other = swap(cov, "dp", bit)
        bit *= 2
    scores = score(place, cov, other, sample, pieces, tokens)
    owner = (column == 1) | (column == 2)
    return (
        jnp.where(owner, scores, 0.0)
        + lax.ppermute(scores, "tensor", [(1, 0), (2, 3)])
        + lax.ppermute(scores, "tensor", [(2, 0), (1, 3)])
        + across(scores)
    )


def damp(matrix):
    size = matrix.shape[0]
    shift_by = 0.1 * jnp.trace(matrix) / size
    return matrix + shift_by * jnp.eye(size, dtype=matrix.dtype)


def chol_apply(factor, rhs):
    lower_sol = lax.linalg.triangular_solve(factor, rhs, left_side=True, lower=True)
    return lax.linalg.triangular_solve(
        factor, lower_sol, left_side=True, lower=True, transpose_a=True
    )


def precondition(query, left, right_side):
    count, rank = (query.shape[0], query.shape[1])
    left_fac = jnp.linalg.cholesky(left)
    right_fac = jnp.linalg.cholesky(right_side)
    stacked = jnp.transpose(query, (1, 0, 2)).reshape(rank, count * rank)
    middle = chol_apply(left_fac, stacked).reshape(rank, count, rank)
    turned = jnp.transpose(middle, (2, 1, 0)).reshape(rank, count * rank)
    result = chol_apply(right_fac, turned).reshape(rank, count, rank)
    return jnp.transpose(result, (1, 2, 0))


def diagonal_blocks(whole, rank):
    return jnp.stack([whole[:, 0:rank, 0:rank], whole[:, rank : 2 * rank, rank : 2 * rank]], axis=1)


def local_general(acts, grads, proj_in, proj_out, queries):
    seq_count, length, width_loc = acts.shape
    rank = proj_in.shape[1]
    hidden_loc = grads.shape[3]
    flat = acts.reshape(-1, width_loc)
    xpart = nt(flat, proj_in.reshape(2 * rank, width_loc))
    gpart = jnp.concatenate(
        [nt(grads[layer].reshape(-1, hidden_loc), proj_out[layer]) for layer in range(2)], axis=1
    )
    count = seq_count * length * lax.axis_size("dp")
    xin, gout = lax.psum((xpart, gpart), "tensor")
    in_cov, out_cov = lax.psum((tn(xin, xin, HIGHEST), tn(gout, gout, HIGHEST)), "dp")
    whole = (
        jnp.einsum(
            "sto,sti->soi",
            gout.reshape(seq_count, length, 2 * rank),
            xin.reshape(seq_count, length, 2 * rank),
            precision=HIGHEST,
        )
        / length
    )
    samples = diagonal_blocks(whole, rank)
    in_cov = in_cov / count
    out_cov = out_cov / count
    precond = []
    for layer in range(2):
        low = layer * rank
        damped_in = damp(in_cov[low : low + rank, low : low + rank])
        damped_out = damp(out_cov[low : low + rank, low : low + rank])
        precond.append(precondition(queries[:, layer].astype(jnp.float32), damped_out, damped_in))
    query_count = queries.shape[0]
    query_b = jnp.stack(precond, axis=1).astype(jnp.bfloat16).reshape(query_count, -1)
    sample_b = samples.astype(jnp.bfloat16).reshape(seq_count, -1)
    return nt(sample_b, lax.all_gather(query_b, "dp", axis=0, tiled=True))


def local(acts, grads, proj_in, proj_out, queries):
    parts = lax.axis_size("dp")
    even = parts > 1 and parts & (parts - 1) == 0
    if lax.axis_size("tensor") == 4 and even and queries.shape[0] % 4 == 0:
        return local_owned(acts, grads, proj_in, proj_out, queries)
    return local_general(acts, grads, proj_in, proj_out, queries)


def solution(mesh):
    placed = (
        P(("groups", "dp"), None, "tensor"),
        P(None, ("groups", "dp"), None, "tensor"),
        P(None, None, "tensor"),
        P(None, None, "tensor"),
        P("dp", None, None, None),
    )
    return jax.shard_map(
        local, mesh=mesh, in_specs=placed, out_specs=P(("groups", "dp"), None), check_vma=False
    )
```

```python
import functools

import jax
import jax.numpy as jnp
from jax import lax
from jax.experimental import pallas as pl
from jax.experimental.pallas import tpu as pltpu
from jax.sharding import PartitionSpec as P

HIGHEST = lax.Precision.HIGHEST
MIB = 1024 * 1024


def nt(a, b, precision=None):
    return lax.dot_general(
        a, b, (((1,), (1,)), ((), ())), precision=precision, preferred_element_type=jnp.float32
    )


def tn(a, b, precision=None):
    return lax.dot_general(
        a, b, (((0,), (0,)), ((), ())), precision=precision, preferred_element_type=jnp.float32
    )


def nn(a, b, precision=None):
    return jnp.dot(a, b, precision=precision, preferred_element_type=jnp.float32)


def vmem():
    return pl.BlockSpec(memory_space=pltpu.VMEM)


def smem():
    return pl.BlockSpec(memory_space=pltpu.SMEM)


def hbm():
    return pl.BlockSpec(memory_space=pl.ANY)


def in_hbm(value):
    return pltpu.with_memory_space_constraint(value, pltpu.HBM)


def params(mib):
    return pltpu.CompilerParams(vmem_limit_bytes=mib * MIB)


def project_in_kernel(side_ref, rows_hbm, proj_hbm, near, far, rows, proj, acc, sems, proj_sem):
    seqs, length, width = rows.shape
    rank = proj.shape[1]
    proj_copy = pltpu.make_async_copy(proj_hbm, proj, proj_sem)
    proj_copy.start()

    def copy(s):
        return pltpu.make_async_copy(rows_hbm.at[s], rows.at[s], sems.at[s])

    for s in range(seqs):
        copy(s).start()
    proj_copy.wait()

    group = 2 - seqs % 2

    @pl.loop(0, seqs // group)
    def _(step):
        for k in range(group):
            copy(step * group + k).wait()
        for k in range(group):
            s = step * group + k
            part = nt(proj[...].reshape(2 * rank, width), rows[s])
            tokens = pl.ds(pl.multiple_of(s * length, length), length)
            acc[0, :, tokens] = part[:rank]
            acc[1, :, tokens] = part[rank:]

    far[...] = acc[1 - side_ref[0]]
    near[...] = acc[side_ref[0]]


def project_in(side, rows, proj):
    seqs, length, _ = rows.shape
    rank = proj.shape[1]
    return pl.pallas_call(
        project_in_kernel,
        in_specs=[smem(), hbm(), hbm()],
        out_specs=[vmem()] * 2,
        out_shape=[jax.ShapeDtypeStruct((rank, seqs * length), jnp.float32)] * 2,
        scratch_shapes=[
            pltpu.VMEM(rows.shape, rows.dtype),
            pltpu.VMEM(proj.shape, proj.dtype),
            pltpu.VMEM((2, rank, seqs * length), jnp.float32),
            pltpu.SemaphoreType.DMA((seqs,)),
            pltpu.SemaphoreType.DMA,
        ],
        compiler_params=params(16),
        name="project_in",
    )(side, in_hbm(rows), in_hbm(proj))


def project_out_kernel(side_ref, rows_hbm, proj_ref, queries_hbm, after, *refs):
    del after
    (near, far, packed), (rows, held, acc, sems, sem) = refs[:3], refs[3:]
    _, seqs, length, width = rows.shape
    parts = sems.shape[2]
    piece = width // parts
    copies = {}
    for s in range(seqs):
        for part in range(parts):
            lanes = pl.ds(part * piece, piece)
            for layer in range(2):
                copies[s, part, layer] = pltpu.make_async_copy(
                    rows_hbm.at[layer, s, :, lanes],
                    rows.at[layer, s, :, lanes],
                    sems.at[layer, s, part],
                )
                copies[s, part, layer].start()
    copy = pltpu.make_async_copy(queries_hbm.at[:, side_ref[0]], held, sem)
    copy.start()
    for s in range(seqs):
        tokens = slice(s * length, (s + 1) * length)
        for part in range(parts):
            lanes = slice(part * piece, (part + 1) * piece)
            for layer in range(2):
                copies[s, part, layer].wait()
            for layer in range(2):
                value = nt(proj_ref[layer, :, lanes], rows[layer, s, :, lanes])
                if part > 0:
                    value = value + acc[layer, :, tokens]
                acc[layer, :, tokens] = value
    far[...] = acc[1 - side_ref[0]]
    near[...] = acc[side_ref[0]]
    copy.wait()
    blocks = held.shape[0] // 2
    for k in range(blocks):
        pair = [held[k].astype(jnp.float32), held[k + blocks].astype(jnp.float32)]
        packed[k] = jnp.concatenate(pair, axis=1).astype(held.dtype)


def project_out(side, rows, proj, queries, after):
    _, seqs, length, width = rows.shape
    rank = proj.shape[1]
    count = queries.shape[0]
    parts = 4 if width % 512 == 0 else 1
    return pl.pallas_call(
        project_out_kernel,
        in_specs=[smem(), hbm(), vmem(), hbm(), hbm()],
        out_specs=[vmem()] * 3,
        out_shape=[
            jax.ShapeDtypeStruct((rank, seqs * length), jnp.float32),
            jax.ShapeDtypeStruct((rank, seqs * length), jnp.float32),
            jax.ShapeDtypeStruct((count // 2, rank, 2 * rank), queries.dtype),
        ],
        scratch_shapes=[
            pltpu.VMEM(rows.shape, rows.dtype),
            pltpu.VMEM((count, rank, rank), queries.dtype),
            pltpu.VMEM((2, rank, seqs * length), jnp.float32),
            pltpu.SemaphoreType.DMA((2, seqs, parts)),
            pltpu.SemaphoreType.DMA,
        ],
        compiler_params=params(40),
        name="project_out",
    )(side, in_hbm(rows), proj, in_hbm(queries), after)


def across(value):
    return lax.ppermute(value, "tensor", [(1, 2), (2, 1), (0, 0), (3, 3)])


def to_owner(near, far):
    return [
        near,
        lax.ppermute(far, "tensor", [(0, 2), (3, 1)]),
        across(far),
        lax.ppermute(near, "tensor", [(0, 1), (3, 2)]),
    ]


def total(pieces):
    value = pieces[0][...]
    for piece in pieces[1:]:
        value = value + piece[...]
    return value


def covariance(value, right):
    none = jnp.zeros_like(value)
    both = [none, value] if right else [value, none]
    return nt(value, jnp.concatenate(both, axis=0), HIGHEST)


def samples_of(x, g, sample_out):
    seqs = sample_out.shape[0]
    length = g.shape[1] // seqs
    for s in range(seqs):
        tokens = slice(s * length, (s + 1) * length)
        sample = nt(x[:, tokens], g[:, tokens], HIGHEST) / length
        sample = sample.astype(jnp.bfloat16).astype(jnp.float32)
        sample_out[s] = jnp.concatenate([sample, sample], axis=1)


def cov_in_kernel(*refs):
    pieces, (x_out, cov_out) = refs[:-2], refs[-2:]
    x = total(pieces)
    x_out[...] = x
    cov_out[...] = covariance(x, False)


def cov_in(pieces):
    rank, tokens = pieces[0].shape
    return pl.pallas_call(
        cov_in_kernel,
        in_specs=[vmem()] * len(pieces),
        out_specs=[vmem()] * 2,
        out_shape=[
            jax.ShapeDtypeStruct((rank, tokens), jnp.float32),
            jax.ShapeDtypeStruct((rank, 2 * rank), jnp.float32),
        ],
        compiler_params=params(16),
        name="cov_in",
    )(*pieces)


def cov_out_kernel(x_ref, cov_ref, *refs):
    pieces, (cov_out, sample_out) = refs[:-2], refs[-2:]
    g = total(pieces)
    cov_out[...] = cov_ref[...] + covariance(g, True)
    samples_of(x_ref[...], g, sample_out)


def cov_out(x, cov, pieces, seqs):
    rank = x.shape[0]
    return pl.pallas_call(
        cov_out_kernel,
        in_specs=[vmem()] * (2 + len(pieces)),
        out_specs=[vmem()] * 2,
        out_shape=[
            jax.ShapeDtypeStruct((rank, 2 * rank), jnp.float32),
            jax.ShapeDtypeStruct((seqs, rank, 2 * rank), jnp.float32),
        ],
        compiler_params=params(16),
        name="cov_out",
    )(x, cov, *pieces)


def scales(steps, spread):
    r = (spread - 1.0) / (spread + 1.0)
    out = []
    for _ in range(steps):
        out.append(2.0 / (2.0 - r * r))
        r = r * r / (2.0 - r * r)
    return out


def damped_inverses(pair):
    size, both = pair.shape
    left = lax.broadcasted_iota(jnp.int32, pair.shape, 1) < size
    whole = jnp.concatenate([jnp.where(left, pair, 0.0), jnp.where(left, 0.0, pair)], axis=0)
    rows = lax.broadcasted_iota(jnp.int32, whole.shape, 0)
    cols = lax.broadcasted_iota(jnp.int32, whole.shape, 1)
    diagonal = rows == cols
    on_diagonal = jnp.where(diagonal, whole, 0.0)
    unit = jnp.where(
        rows < size, jnp.sum(on_diagonal[:size]) / size, jnp.sum(on_diagonal[size:]) / size
    )
    eye = jnp.where(diagonal, 1.0, 0.0)
    matrix = whole / unit + 0.1 * eye
    low, high = 0.1, size + 0.1
    start = 2.0 / (low + high)
    steps = scales(7, high / low)
    y = matrix * start
    x = (2.0 * start * steps[0]) * eye - (start * steps[0]) * y
    y = steps[0] * (2.0 * y - nn(y, y, HIGHEST))

    for scale in steps[1:-1]:
        product = nn(jnp.concatenate([x, y], axis=0), y, HIGHEST)
        x = scale * (2.0 * x - product[:both])
        y = scale * (2.0 * y - product[both:])
    x = steps[-1] * (2.0 * x - nn(x, y, HIGHEST))
    x = x + nn(x, eye - nn(matrix, x, HIGHEST), HIGHEST)
    return x / unit


def split(value):
    high = value.astype(jnp.bfloat16)
    rest = value - high.astype(jnp.float32)
    middle = rest.astype(jnp.bfloat16)
    low = (rest - middle.astype(jnp.float32)).astype(jnp.bfloat16)
    return high, middle, low


def score_kernel(tokens, place_ref, own_ref, other_ref, sample_ref, *refs):
    pieces, (out, held, half) = refs[:-3], refs[-3:]
    parts = held.shape[0]
    k = 0
    for piece in pieces:
        for place in range(piece.shape[0]):
            held[place_ref[0] ^ k] = piece[place]
            k += 1
    inverses = damped_inverses((own_ref[...] + other_ref[...]) / tokens)
    both = inverses.shape[0]
    size = both // 2
    samples = [sample_ref[s] for s in range(sample_ref.shape[0])]
    seqs = len(samples)
    blocks = held.shape[1]
    pairs = parts * blocks
    first = jnp.concatenate(split(inverses[:size, :size]), axis=0)
    none = jnp.zeros_like(first)
    first = jnp.concatenate(
        [jnp.concatenate([first, none], axis=1), jnp.concatenate([none, first], axis=1)], axis=0
    )
    right = inverses[size:]
    twice = jnp.concatenate([pltpu.roll(right, size, 1), right], axis=0)
    high, middle, _ = split(twice)
    once = jnp.concatenate([high, middle], axis=1)
    second = jnp.concatenate([once, once], axis=0)

    for part in range(parts // 2):
        for block in range(0, blocks, 2):
            rows = jnp.concatenate(
                [
                    held[part, block],
                    held[part + parts // 2, block],
                    held[part, block + 1],
                    held[part + parts // 2, block + 1],
                ],
                axis=0,
            )
            result = nt(first, rows)
            for k in range(2):
                three = result[3 * size * k : 3 * size * (k + 1)]
                value = three[:size] + three[size : 2 * size] + three[2 * size :]
                high, middle, _ = split(value)
                pair = (2 * part + k) * blocks + block
                lanes = slice(pair * both, (pair + 2) * both)
                half[0, :, lanes] = high
                half[1, :, lanes] = middle
    lines = [[] for _ in range(seqs)]
    for pair in range(pairs):
        lanes = slice(pair * both, (pair + 1) * both)
        rows = jnp.concatenate([half[0, :, lanes], half[1, :, lanes]], axis=1)
        result = nn(rows, second)
        result = (result[:, :both] + result[:, both:]).astype(jnp.bfloat16).astype(jnp.float32)
        for s in range(seqs):
            lines[s].append(jnp.sum(result * samples[s], axis=0, keepdims=True))
    lines = jnp.concatenate([line for part in lines for line in part], axis=0)
    shape = (8, both)
    ends = jnp.where(
        (lax.broadcasted_iota(jnp.int32, shape, 1) < size)
        == (lax.broadcasted_iota(jnp.int32, shape, 0) == 0),
        1.0,
        0.0,
    )
    result = nt(ends, lines, HIGHEST)
    for s in range(seqs):
        for k in range(2):
            out[s : s + 1, k * pairs : (k + 1) * pairs] = result[
                k : k + 1, s * pairs : (s + 1) * pairs
            ]


def score(place, own, other, sample, pieces, tokens):
    _, blocks, rank, both = pieces[0].shape
    parts = sum(piece.shape[0] for piece in pieces)
    pairs = parts * blocks
    seqs = sample.shape[0]
    return pl.pallas_call(
        functools.partial(score_kernel, tokens),
        in_specs=[smem()] + [vmem()] * (3 + len(pieces)),
        out_specs=vmem(),
        out_shape=jax.ShapeDtypeStruct((seqs, 2 * pairs), jnp.float32),
        scratch_shapes=[
            pltpu.VMEM((parts, blocks, rank, both), pieces[0].dtype),
            pltpu.VMEM((2, rank, pairs * both), jnp.bfloat16),
        ],
        compiler_params=params(16),
        name="score",
    )(place, own, other, sample, *pieces)


def swap(value, axis, bit):
    return lax.ppermute(value, axis, [(i, i ^ bit) for i in range(lax.axis_size(axis))])


def after(value, earlier):
    return lax.optimization_barrier((value, earlier))[0]


def local_owned(acts, grads, proj_in, proj_out, queries):
    seqs, length, _ = acts.shape
    parts = lax.axis_size("dp")
    tokens = seqs * length * parts
    column = lax.axis_index("tensor").astype(jnp.int32)
    side = (column >= 2).astype(jnp.int32).reshape(1)
    place = lax.axis_index("dp").astype(jnp.int32).reshape(1)
    x_near, x_far = project_in(side, acts, proj_in)
    x_pieces = to_owner(x_near, x_far)
    near, far, packed = project_out(side, grads, proj_out, queries, x_near)
    pieces = to_owner(near, far)
    x, cov = cov_in(x_pieces[:3] + [after(x_pieces[3], pieces[1])])
    query_pieces = [after(packed, cov)[None]]
    bit = 1
    while bit < parts:
        mine = query_pieces[0] if bit == 1 else jnp.concatenate(query_pieces, axis=0)
        query_pieces = [mine, swap(mine, "dp", bit)]
        bit *= 2
    cov, sample = cov_out(x, cov, pieces, seqs)
    other = jnp.zeros_like(cov)
    bit = 1
    while bit < parts:
        cov = cov if bit == 1 else cov + other
        other = swap(cov, "dp", bit)
        bit *= 2
    scores = score(place, cov, other, sample, query_pieces, tokens)
    owner = (column == 1) | (column == 2)
    return (
        jnp.where(owner, scores, 0.0)
        + lax.ppermute(scores, "tensor", [(1, 0), (2, 3)])
        + lax.ppermute(scores, "tensor", [(2, 0), (1, 3)])
        + jnp.where(owner, across(scores), 0.0)
    )


def damp(matrix):
    size = matrix.shape[0]
    shift_by = 0.1 * jnp.trace(matrix) / size
    return matrix + shift_by * jnp.eye(size, dtype=matrix.dtype)


def chol_apply(factor, rhs):
    lower_sol = lax.linalg.triangular_solve(factor, rhs, left_side=True, lower=True)
    return lax.linalg.triangular_solve(
        factor, lower_sol, left_side=True, lower=True, transpose_a=True
    )


def precondition(query, left, right_side):
    count, rank = (query.shape[0], query.shape[1])
    left_fac = jnp.linalg.cholesky(left)
    right_fac = jnp.linalg.cholesky(right_side)
    stacked = jnp.transpose(query, (1, 0, 2)).reshape(rank, count * rank)
    middle = chol_apply(left_fac, stacked).reshape(rank, count, rank)
    turned = jnp.transpose(middle, (2, 1, 0)).reshape(rank, count * rank)
    result = chol_apply(right_fac, turned).reshape(rank, count, rank)
    return jnp.transpose(result, (1, 2, 0))


def diagonal_blocks(whole, rank):
    return jnp.stack([whole[:, 0:rank, 0:rank], whole[:, rank : 2 * rank, rank : 2 * rank]], axis=1)


def local_general(acts, grads, proj_in, proj_out, queries):
    seq_count, length, width_loc = acts.shape
    rank = proj_in.shape[1]
    hidden_loc = grads.shape[3]
    flat = acts.reshape(-1, width_loc)
    xpart = nt(flat, proj_in.reshape(2 * rank, width_loc))
    gpart = jnp.concatenate(
        [nt(grads[layer].reshape(-1, hidden_loc), proj_out[layer]) for layer in range(2)], axis=1
    )
    count = seq_count * length * lax.axis_size("dp")
    xin, gout = lax.psum((xpart, gpart), "tensor")
    in_cov, out_cov = lax.psum((tn(xin, xin, HIGHEST), tn(gout, gout, HIGHEST)), "dp")
    whole = (
        jnp.einsum(
            "sto,sti->soi",
            gout.reshape(seq_count, length, 2 * rank),
            xin.reshape(seq_count, length, 2 * rank),
            precision=HIGHEST,
        )
        / length
    )
    samples = diagonal_blocks(whole, rank)
    in_cov = in_cov / count
    out_cov = out_cov / count
    precond = []
    for layer in range(2):
        low = layer * rank
        damped_in = damp(in_cov[low : low + rank, low : low + rank])
        damped_out = damp(out_cov[low : low + rank, low : low + rank])
        precond.append(precondition(queries[:, layer].astype(jnp.float32), damped_out, damped_in))
    query_count = queries.shape[0]
    query_b = jnp.stack(precond, axis=1).astype(jnp.bfloat16).reshape(query_count, -1)
    sample_b = samples.astype(jnp.bfloat16).reshape(seq_count, -1)
    return nt(sample_b, lax.all_gather(query_b, "dp", axis=0, tiled=True))


def local(acts, grads, proj_in, proj_out, queries):
    parts = lax.axis_size("dp")
    even = parts > 1 and parts & (parts - 1) == 0
    if lax.axis_size("tensor") == 4 and even and queries.shape[0] % 4 == 0:
        return local_owned(acts, grads, proj_in, proj_out, queries)
    return local_general(acts, grads, proj_in, proj_out, queries)


def solution(mesh):
    placed = (
        P(("groups", "dp"), None, "tensor"),
        P(None, ("groups", "dp"), None, "tensor"),
        P(None, None, "tensor"),
        P(None, None, "tensor"),
        P("dp", None, None, None),
    )
    return jax.shard_map(
        local, mesh=mesh, in_specs=placed, out_specs=P(("groups", "dp"), None), check_vma=False
    )
```

```python
import functools

import jax
import jax.numpy as jnp
from jax import lax
from jax.experimental import pallas as pl
from jax.experimental.pallas import tpu as pltpu
from jax.sharding import PartitionSpec as P

HIGHEST = lax.Precision.HIGHEST
MIB = 1024 * 1024


def nt(a, b, precision=None):
    return lax.dot_general(
        a, b, (((1,), (1,)), ((), ())), precision=precision, preferred_element_type=jnp.float32
    )


def tn(a, b, precision=None):
    return lax.dot_general(
        a, b, (((0,), (0,)), ((), ())), precision=precision, preferred_element_type=jnp.float32
    )


def nn(a, b, precision=None):
    return jnp.dot(a, b, precision=precision, preferred_element_type=jnp.float32)


def vmem():
    return pl.BlockSpec(memory_space=pltpu.VMEM)


def smem():
    return pl.BlockSpec(memory_space=pltpu.SMEM)


def hbm():
    return pl.BlockSpec(memory_space=pl.ANY)


def in_hbm(value):
    return pltpu.with_memory_space_constraint(value, pltpu.HBM)


def params(mib):
    return pltpu.CompilerParams(vmem_limit_bytes=mib * MIB)


def project_in_kernel(side_ref, rows_hbm, proj_hbm, near, far, rows, proj, acc, sems, proj_sem):
    seqs, length, width = rows.shape
    rank = proj.shape[1]
    proj_copy = pltpu.make_async_copy(proj_hbm, proj, proj_sem)
    proj_copy.start()

    def copy(s):
        return pltpu.make_async_copy(rows_hbm.at[s], rows.at[s], sems.at[s])

    for s in range(seqs):
        copy(s).start()
    proj_copy.wait()

    group = 2 - seqs % 2

    @pl.loop(0, seqs // group)
    def _(step):
        for k in range(group):
            copy(step * group + k).wait()
        for k in range(group):
            s = step * group + k
            part = nt(proj[...].reshape(2 * rank, width), rows[s])
            tokens = pl.ds(pl.multiple_of(s * length, length), length)
            acc[0, :, tokens] = part[:rank]
            acc[1, :, tokens] = part[rank:]

    far[...] = acc[1 - side_ref[0]]
    near[...] = acc[side_ref[0]]


def project_in(side, rows, proj):
    seqs, length, _ = rows.shape
    rank = proj.shape[1]
    return pl.pallas_call(
        project_in_kernel,
        in_specs=[smem(), hbm(), hbm()],
        out_specs=[vmem()] * 2,
        out_shape=[jax.ShapeDtypeStruct((rank, seqs * length), jnp.float32)] * 2,
        scratch_shapes=[
            pltpu.VMEM(rows.shape, rows.dtype),
            pltpu.VMEM(proj.shape, proj.dtype),
            pltpu.VMEM((2, rank, seqs * length), jnp.float32),
            pltpu.SemaphoreType.DMA((seqs,)),
            pltpu.SemaphoreType.DMA,
        ],
        compiler_params=params(16),
        name="project_in",
    )(side, in_hbm(rows), in_hbm(proj))


def project_out_kernel(side_ref, rows_hbm, proj_ref, queries_hbm, after, *refs):
    del after
    (near, far, packed), (rows, held, acc, sems, sem) = refs[:3], refs[3:]
    _, seqs, length, width = rows.shape
    parts = sems.shape[2]
    piece = width // parts
    copies = {}
    for s in range(seqs):
        for part in range(parts):
            lanes = pl.ds(part * piece, piece)
            for layer in range(2):
                copies[s, part, layer] = pltpu.make_async_copy(
                    rows_hbm.at[layer, s, :, lanes],
                    rows.at[layer, s, :, lanes],
                    sems.at[layer, s, part],
                )
                copies[s, part, layer].start()
    copy = pltpu.make_async_copy(queries_hbm.at[:, side_ref[0]], held, sem)
    copy.start()
    for s in range(seqs):
        tokens = slice(s * length, (s + 1) * length)
        for part in range(parts):
            lanes = slice(part * piece, (part + 1) * piece)
            for layer in range(2):
                copies[s, part, layer].wait()
            for layer in range(2):
                value = nt(proj_ref[layer, :, lanes], rows[layer, s, :, lanes])
                if part > 0:
                    value = value + acc[layer, :, tokens]
                acc[layer, :, tokens] = value
    far[...] = acc[1 - side_ref[0]]
    near[...] = acc[side_ref[0]]
    copy.wait()
    blocks = held.shape[0] // 2
    for k in range(blocks):
        pair = [held[k].astype(jnp.float32), held[k + blocks].astype(jnp.float32)]
        packed[k] = jnp.concatenate(pair, axis=1).astype(held.dtype)


def project_out(side, rows, proj, queries, after):
    _, seqs, length, width = rows.shape
    rank = proj.shape[1]
    count = queries.shape[0]
    parts = 4 if width % 512 == 0 else 1
    return pl.pallas_call(
        project_out_kernel,
        in_specs=[smem(), hbm(), vmem(), hbm(), hbm()],
        out_specs=[vmem()] * 3,
        out_shape=[
            jax.ShapeDtypeStruct((rank, seqs * length), jnp.float32),
            jax.ShapeDtypeStruct((rank, seqs * length), jnp.float32),
            jax.ShapeDtypeStruct((count // 2, rank, 2 * rank), queries.dtype),
        ],
        scratch_shapes=[
            pltpu.VMEM(rows.shape, rows.dtype),
            pltpu.VMEM((count, rank, rank), queries.dtype),
            pltpu.VMEM((2, rank, seqs * length), jnp.float32),
            pltpu.SemaphoreType.DMA((2, seqs, parts)),
            pltpu.SemaphoreType.DMA,
        ],
        compiler_params=params(40),
        name="project_out",
    )(side, in_hbm(rows), proj, in_hbm(queries), after)


def across(value):
    return lax.ppermute(value, "tensor", [(1, 2), (2, 1)])


def to_owner(near, far):
    return [
        near,
        lax.ppermute(far, "tensor", [(0, 2), (3, 1)]),
        across(far),
        lax.ppermute(near, "tensor", [(0, 1), (3, 2)]),
    ]


def total(pieces):
    value = pieces[0][...]
    for piece in pieces[1:]:
        value = value + piece[...]
    return value


def covariance(value, right):
    none = jnp.zeros_like(value)
    both = [none, value] if right else [value, none]
    return nt(value, jnp.concatenate(both, axis=0), HIGHEST)


def samples_of(x, g, sample_out):
    seqs = sample_out.shape[0]
    length = g.shape[1] // seqs
    for s in range(seqs):
        tokens = slice(s * length, (s + 1) * length)
        sample = nt(x[:, tokens], g[:, tokens], HIGHEST) / length
        sample = sample.astype(jnp.bfloat16).astype(jnp.float32)
        sample_out[s] = jnp.concatenate([sample, sample], axis=1)


def cov_in_kernel(packed_ref, *refs):
    pieces, (packed, x_out, cov_out) = refs[:-3], refs[-3:]
    packed[...] = packed_ref[...]
    x = total(pieces)
    x_out[...] = x
    cov_out[...] = covariance(x, False)


def cov_in(packed, pieces):
    rank, tokens = pieces[0].shape
    return pl.pallas_call(
        cov_in_kernel,
        in_specs=[vmem()] * (1 + len(pieces)),
        out_specs=[vmem()] * 3,
        out_shape=[
            jax.ShapeDtypeStruct(packed.shape, packed.dtype),
            jax.ShapeDtypeStruct((rank, tokens), jnp.float32),
            jax.ShapeDtypeStruct((rank, 2 * rank), jnp.float32),
        ],
        compiler_params=params(16),
        name="cov_in",
    )(packed, *pieces)


def cov_out_kernel(x_ref, cov_ref, *refs):
    pieces, (cov_out, sample_out) = refs[:-2], refs[-2:]
    g = total(pieces)
    cov_out[...] = cov_ref[...] + covariance(g, True)
    samples_of(x_ref[...], g, sample_out)


def cov_out(x, cov, pieces, seqs):
    rank = x.shape[0]
    return pl.pallas_call(
        cov_out_kernel,
        in_specs=[vmem()] * (2 + len(pieces)),
        out_specs=[vmem()] * 2,
        out_shape=[
            jax.ShapeDtypeStruct((rank, 2 * rank), jnp.float32),
            jax.ShapeDtypeStruct((seqs, rank, 2 * rank), jnp.float32),
        ],
        compiler_params=params(16),
        name="cov_out",
    )(x, cov, *pieces)


def scales(steps, spread):
    r = (spread - 1.0) / (spread + 1.0)
    out = []
    for _ in range(steps):
        out.append(2.0 / (2.0 - r * r))
        r = r * r / (2.0 - r * r)
    return out


def damped_inverses(pair):
    size, both = pair.shape
    left = lax.broadcasted_iota(jnp.int32, pair.shape, 1) < size
    whole = jnp.concatenate([jnp.where(left, pair, 0.0), jnp.where(left, 0.0, pair)], axis=0)
    rows = lax.broadcasted_iota(jnp.int32, whole.shape, 0)
    cols = lax.broadcasted_iota(jnp.int32, whole.shape, 1)
    diagonal = rows == cols
    on_diagonal = jnp.where(diagonal, whole, 0.0)
    unit = jnp.where(
        rows < size, jnp.sum(on_diagonal[:size]) / size, jnp.sum(on_diagonal[size:]) / size
    )
    eye = jnp.where(diagonal, 1.0, 0.0)
    matrix = whole / unit + 0.1 * eye
    low, high = 0.1, size + 0.1
    start = 2.0 / (low + high)
    steps = scales(7, high / low)
    y = matrix * start
    x = (2.0 * start * steps[0]) * eye - (start * steps[0]) * y
    y = steps[0] * (2.0 * y - nn(y, y, HIGHEST))

    for scale in steps[1:-1]:
        product = nn(jnp.concatenate([x, y], axis=0), y, HIGHEST)
        x = scale * (2.0 * x - product[:both])
        y = scale * (2.0 * y - product[both:])
    x = steps[-1] * (2.0 * x - nn(x, y, HIGHEST))
    x = x + nn(x, eye - nn(matrix, x, HIGHEST), HIGHEST)
    return x / unit


def split(value):
    high = value.astype(jnp.bfloat16)
    rest = value - high.astype(jnp.float32)
    middle = rest.astype(jnp.bfloat16)
    low = (rest - middle.astype(jnp.float32)).astype(jnp.bfloat16)
    return high, middle, low


def score_kernel(tokens, place_ref, own_ref, other_ref, sample_ref, *refs):
    pieces, (out, held, half) = refs[:-3], refs[-3:]
    parts = held.shape[0]
    for k, piece in enumerate(pieces):
        held[place_ref[0] ^ k] = piece[...]
    inverses = damped_inverses((own_ref[...] + other_ref[...]) / tokens)
    both = inverses.shape[0]
    size = both // 2
    samples = [sample_ref[s] for s in range(sample_ref.shape[0])]
    seqs = len(samples)
    blocks = held.shape[1]
    pairs = parts * blocks
    first = jnp.concatenate(split(inverses[:size, :size]), axis=0)
    none = jnp.zeros_like(first)
    first = jnp.concatenate(
        [jnp.concatenate([first, none], axis=1), jnp.concatenate([none, first], axis=1)], axis=0
    )
    right = inverses[size:]
    twice = jnp.concatenate([pltpu.roll(right, size, 1), right], axis=0)
    high, middle, _ = split(twice)
    once = jnp.concatenate([high, middle], axis=1)
    second = jnp.concatenate([once, once], axis=0)

    for part in range(parts // 2):
        for block in range(0, blocks, 2):
            rows = jnp.concatenate(
                [
                    held[part, block],
                    held[part + parts // 2, block],
                    held[part, block + 1],
                    held[part + parts // 2, block + 1],
                ],
                axis=0,
            )
            result = nt(first, rows)
            for k in range(2):
                three = result[3 * size * k : 3 * size * (k + 1)]
                value = three[:size] + three[size : 2 * size] + three[2 * size :]
                high, middle, _ = split(value)
                pair = (2 * part + k) * blocks + block
                lanes = slice(pair * both, (pair + 2) * both)
                half[0, :, lanes] = high
                half[1, :, lanes] = middle
    lines = [[] for _ in range(seqs)]
    for pair in range(pairs):
        lanes = slice(pair * both, (pair + 1) * both)
        rows = jnp.concatenate([half[0, :, lanes], half[1, :, lanes]], axis=1)
        result = nn(rows, second)
        result = (result[:, :both] + result[:, both:]).astype(jnp.bfloat16).astype(jnp.float32)
        for s in range(seqs):
            lines[s].append(jnp.sum(result * samples[s], axis=0, keepdims=True))
    lines = jnp.concatenate([line for part in lines for line in part], axis=0)
    shape = (8, both)
    ends = jnp.where(
        (lax.broadcasted_iota(jnp.int32, shape, 1) < size)
        == (lax.broadcasted_iota(jnp.int32, shape, 0) == 0),
        1.0,
        0.0,
    )
    result = nt(ends, lines, HIGHEST)
    for s in range(seqs):
        for k in range(2):
            out[s : s + 1, k * pairs : (k + 1) * pairs] = result[
                k : k + 1, s * pairs : (s + 1) * pairs
            ]


def score(place, own, other, sample, pieces, tokens):
    blocks, rank, both = pieces[0].shape
    parts = len(pieces)
    pairs = parts * blocks
    seqs = sample.shape[0]
    return pl.pallas_call(
        functools.partial(score_kernel, tokens),
        in_specs=[smem()] + [vmem()] * (3 + len(pieces)),
        out_specs=vmem(),
        out_shape=jax.ShapeDtypeStruct((seqs, 2 * pairs), jnp.float32),
        scratch_shapes=[
            pltpu.VMEM((parts, blocks, rank, both), pieces[0].dtype),
            pltpu.VMEM((2, rank, pairs * both), jnp.bfloat16),
        ],
        compiler_params=params(16),
        name="score",
    )(place, own, other, sample, *pieces)


def swap(value, axis, bit):
    return lax.ppermute(value, axis, [(i, i ^ bit) for i in range(lax.axis_size(axis))])


def local_owned(acts, grads, proj_in, proj_out, queries):
    seqs, length, _ = acts.shape
    parts = lax.axis_size("dp")
    tokens = seqs * length * parts
    column = lax.axis_index("tensor").astype(jnp.int32)
    side = (column >= 2).astype(jnp.int32).reshape(1)
    place = lax.axis_index("dp").astype(jnp.int32).reshape(1)
    x_near, x_far = project_in(side, acts, proj_in)
    x_pieces = to_owner(x_near, x_far)
    near, far, packed = project_out(side, grads, proj_out, queries, x_near)
    pieces = to_owner(near, far)
    packed, x, cov = cov_in(packed, x_pieces)
    query_pieces = [packed] + [swap(packed, "dp", bits) for bits in range(1, parts)]
    cov, sample = cov_out(x, cov, pieces, seqs)
    other = jnp.zeros_like(cov)
    bit = 1
    while bit < parts:
        cov = cov if bit == 1 else cov + other
        other = swap(cov, "dp", bit)
        bit *= 2
    scores = score(place, cov, other, sample, query_pieces, tokens)
    owner = (column == 1) | (column == 2)
    pieces = [
        lax.ppermute(scores, "tensor", [(2, 0), (1, 3)]),
        lax.ppermute(scores, "tensor", [(1, 0), (2, 3)]),
        across(scores),
    ]
    return jnp.where(owner, scores, 0.0) + pieces[0] + pieces[1] + pieces[2]


def damp(matrix):
    size = matrix.shape[0]
    shift_by = 0.1 * jnp.trace(matrix) / size
    return matrix + shift_by * jnp.eye(size, dtype=matrix.dtype)


def chol_apply(factor, rhs):
    lower_sol = lax.linalg.triangular_solve(factor, rhs, left_side=True, lower=True)
    return lax.linalg.triangular_solve(
        factor, lower_sol, left_side=True, lower=True, transpose_a=True
    )


def precondition(query, left, right_side):
    count, rank = (query.shape[0], query.shape[1])
    left_fac = jnp.linalg.cholesky(left)
    right_fac = jnp.linalg.cholesky(right_side)
    stacked = jnp.transpose(query, (1, 0, 2)).reshape(rank, count * rank)
    middle = chol_apply(left_fac, stacked).reshape(rank, count, rank)
    turned = jnp.transpose(middle, (2, 1, 0)).reshape(rank, count * rank)
    result = chol_apply(right_fac, turned).reshape(rank, count, rank)
    return jnp.transpose(result, (1, 2, 0))


def diagonal_blocks(whole, rank):
    return jnp.stack([whole[:, 0:rank, 0:rank], whole[:, rank : 2 * rank, rank : 2 * rank]], axis=1)


def local_general(acts, grads, proj_in, proj_out, queries):
    seq_count, length, width_loc = acts.shape
    rank = proj_in.shape[1]
    hidden_loc = grads.shape[3]
    flat = acts.reshape(-1, width_loc)
    xpart = nt(flat, proj_in.reshape(2 * rank, width_loc))
    gpart = jnp.concatenate(
        [nt(grads[layer].reshape(-1, hidden_loc), proj_out[layer]) for layer in range(2)], axis=1
    )
    count = seq_count * length * lax.axis_size("dp")
    xin, gout = lax.psum((xpart, gpart), "tensor")
    in_cov, out_cov = lax.psum((tn(xin, xin, HIGHEST), tn(gout, gout, HIGHEST)), "dp")
    whole = (
        jnp.einsum(
            "sto,sti->soi",
            gout.reshape(seq_count, length, 2 * rank),
            xin.reshape(seq_count, length, 2 * rank),
            precision=HIGHEST,
        )
        / length
    )
    samples = diagonal_blocks(whole, rank)
    in_cov = in_cov / count
    out_cov = out_cov / count
    precond = []
    for layer in range(2):
        low = layer * rank
        damped_in = damp(in_cov[low : low + rank, low : low + rank])
        damped_out = damp(out_cov[low : low + rank, low : low + rank])
        precond.append(precondition(queries[:, layer].astype(jnp.float32), damped_out, damped_in))
    query_count = queries.shape[0]
    query_b = jnp.stack(precond, axis=1).astype(jnp.bfloat16).reshape(query_count, -1)
    sample_b = samples.astype(jnp.bfloat16).reshape(seq_count, -1)
    return nt(sample_b, lax.all_gather(query_b, "dp", axis=0, tiled=True))


def local(acts, grads, proj_in, proj_out, queries):
    parts = lax.axis_size("dp")
    even = parts > 1 and parts & (parts - 1) == 0
    if lax.axis_size("tensor") == 4 and even and queries.shape[0] % 4 == 0:
        return local_owned(acts, grads, proj_in, proj_out, queries)
    return local_general(acts, grads, proj_in, proj_out, queries)


def solution(mesh):
    placed = (
        P(("groups", "dp"), None, "tensor"),
        P(None, ("groups", "dp"), None, "tensor"),
        P(None, None, "tensor"),
        P(None, None, "tensor"),
        P("dp", None, None, None),
    )
    return jax.shard_map(
        local, mesh=mesh, in_specs=placed, out_specs=P(("groups", "dp"), None), check_vma=False
    )
```

```python
import functools

import jax
import jax.numpy as jnp
from jax import lax
from jax.experimental import pallas as pl
from jax.experimental.pallas import tpu as pltpu
from jax.sharding import PartitionSpec as P

HIGHEST = lax.Precision.HIGHEST
MIB = 1024 * 1024


def nt(a, b, precision=None):
    return lax.dot_general(
        a, b, (((1,), (1,)), ((), ())), precision=precision, preferred_element_type=jnp.float32
    )


def tn(a, b, precision=None):
    return lax.dot_general(
        a, b, (((0,), (0,)), ((), ())), precision=precision, preferred_element_type=jnp.float32
    )


def nn(a, b, precision=None):
    return jnp.dot(a, b, precision=precision, preferred_element_type=jnp.float32)


def vmem():
    return pl.BlockSpec(memory_space=pltpu.VMEM)


def smem():
    return pl.BlockSpec(memory_space=pltpu.SMEM)


def hbm():
    return pl.BlockSpec(memory_space=pl.ANY)


def in_hbm(value):
    return pltpu.with_memory_space_constraint(value, pltpu.HBM)


def params(mib):
    return pltpu.CompilerParams(vmem_limit_bytes=mib * MIB)


def project_in_kernel(
    side_ref, rows_hbm, proj_hbm, grads_hbm, near, far, early, rows, proj, acc, sems, proj_sem, early_sem
):
    seqs, length, width = rows.shape
    rank = proj.shape[1]
    proj_copy = pltpu.make_async_copy(proj_hbm, proj, proj_sem)
    proj_copy.start()

    def copy(s):
        return pltpu.make_async_copy(rows_hbm.at[s], rows.at[s], sems.at[s])

    for s in range(seqs):
        copy(s).start()
    early_copy = pltpu.make_async_copy(
        grads_hbm.at[:, 0, :, pl.ds(0, early.shape[2])], early, early_sem
    )
    early_copy.start()
    proj_copy.wait()

    group = 2 - seqs % 2

    @pl.loop(0, seqs // group)
    def _(step):
        for k in range(group):
            copy(step * group + k).wait()
        for k in range(group):
            s = step * group + k
            part = nt(proj[...].reshape(2 * rank, width), rows[s])
            tokens = pl.ds(pl.multiple_of(s * length, length), length)
            acc[0, :, tokens] = part[:rank]
            acc[1, :, tokens] = part[rank:]

    far[...] = acc[1 - side_ref[0]]
    near[...] = acc[side_ref[0]]
    early_copy.wait()


def project_in(side, rows, proj, grads):
    seqs, length, _ = rows.shape
    early = (2, length, grads.shape[3] // 2)
    rank = proj.shape[1]
    return pl.pallas_call(
        project_in_kernel,
        in_specs=[smem(), hbm(), hbm(), hbm()],
        out_specs=[vmem()] * 3,
        out_shape=[
            jax.ShapeDtypeStruct((rank, seqs * length), jnp.float32),
            jax.ShapeDtypeStruct((rank, seqs * length), jnp.float32),
            jax.ShapeDtypeStruct(early, grads.dtype),
        ],
        scratch_shapes=[
            pltpu.VMEM(rows.shape, rows.dtype),
            pltpu.VMEM(proj.shape, proj.dtype),
            pltpu.VMEM((2, rank, seqs * length), jnp.float32),
            pltpu.SemaphoreType.DMA((seqs,)),
            pltpu.SemaphoreType.DMA,
            pltpu.SemaphoreType.DMA,
        ],
        compiler_params=params(16),
        name="project_in",
    )(side, in_hbm(rows), in_hbm(proj), in_hbm(grads))


def project_out_kernel(side_ref, rows_hbm, proj_ref, queries_hbm, early, *refs):
    (near, far, packed), (rows, held, acc, sems, sem) = refs[:3], refs[3:]
    _, seqs, length, width = rows.shape
    parts = sems.shape[2]
    piece = width // parts
    copies = {}
    for s in range(seqs):
        for part in range(parts):
            if s == 0 and part < parts // 2:
                continue
            lanes = pl.ds(part * piece, piece)
            for layer in range(2):
                copies[s, part, layer] = pltpu.make_async_copy(
                    rows_hbm.at[layer, s, :, lanes],
                    rows.at[layer, s, :, lanes],
                    sems.at[layer, s, part],
                )
                copies[s, part, layer].start()
    copy = pltpu.make_async_copy(queries_hbm.at[:, side_ref[0]], held, sem)
    copy.start()
    for s in range(seqs):
        tokens = slice(s * length, (s + 1) * length)
        for part in range(parts):
            lanes = slice(part * piece, (part + 1) * piece)
            ready = s == 0 and part < parts // 2
            for layer in range(2):
                if not ready:
                    copies[s, part, layer].wait()
            for layer in range(2):
                block = early[layer, :, lanes] if ready else rows[layer, s, :, lanes]
                value = nt(proj_ref[layer, :, lanes], block)
                if part > 0:
                    value = value + acc[layer, :, tokens]
                acc[layer, :, tokens] = value
    far[...] = acc[1 - side_ref[0]]
    near[...] = acc[side_ref[0]]
    copy.wait()
    blocks = held.shape[0] // 2
    for k in range(blocks):
        pair = [held[k].astype(jnp.float32), held[k + blocks].astype(jnp.float32)]
        packed[k] = jnp.concatenate(pair, axis=1).astype(held.dtype)


def project_out(side, rows, proj, queries, early):
    _, seqs, length, width = rows.shape
    rank = proj.shape[1]
    count = queries.shape[0]
    parts = 4 if width % 512 == 0 else 2
    return pl.pallas_call(
        project_out_kernel,
        in_specs=[smem(), hbm(), vmem(), hbm(), vmem()],
        out_specs=[vmem()] * 3,
        out_shape=[
            jax.ShapeDtypeStruct((rank, seqs * length), jnp.float32),
            jax.ShapeDtypeStruct((rank, seqs * length), jnp.float32),
            jax.ShapeDtypeStruct((count // 2, rank, 2 * rank), queries.dtype),
        ],
        scratch_shapes=[
            pltpu.VMEM(rows.shape, rows.dtype),
            pltpu.VMEM((count, rank, rank), queries.dtype),
            pltpu.VMEM((2, rank, seqs * length), jnp.float32),
            pltpu.SemaphoreType.DMA((2, seqs, parts)),
            pltpu.SemaphoreType.DMA,
        ],
        compiler_params=params(40),
        name="project_out",
    )(side, in_hbm(rows), proj, in_hbm(queries), early)


def across(value):
    return lax.ppermute(value, "tensor", [(1, 2), (2, 1)])


def to_owner(near, far):
    return [
        near,
        lax.ppermute(near, "tensor", [(0, 1), (3, 2)]),
        across(far),
        lax.ppermute(far, "tensor", [(0, 2), (3, 1)]),
    ]


def total(pieces):
    value = pieces[0][...]
    for piece in pieces[1:]:
        value = value + piece[...]
    return value


def covariance(value, right):
    none = jnp.zeros_like(value)
    both = [none, value] if right else [value, none]
    return nt(value, jnp.concatenate(both, axis=0), HIGHEST)


def samples_of(x, g, sample_out):
    seqs = sample_out.shape[0]
    length = g.shape[1] // seqs
    for s in range(seqs):
        tokens = slice(s * length, (s + 1) * length)
        sample = nt(x[:, tokens], g[:, tokens], HIGHEST) / length
        sample = sample.astype(jnp.bfloat16).astype(jnp.float32)
        sample_out[s] = jnp.concatenate([sample, sample], axis=1)


def cov_in_kernel(packed_ref, *refs):
    pieces, (packed, x_out, cov_out) = refs[:-3], refs[-3:]
    packed[...] = packed_ref[...]
    x = total(pieces)
    x_out[...] = x
    cov_out[...] = covariance(x, False)


def cov_in(packed, pieces):
    rank, tokens = pieces[0].shape
    return pl.pallas_call(
        cov_in_kernel,
        in_specs=[vmem()] * (1 + len(pieces)),
        out_specs=[vmem()] * 3,
        out_shape=[
            jax.ShapeDtypeStruct(packed.shape, packed.dtype),
            jax.ShapeDtypeStruct((rank, tokens), jnp.float32),
            jax.ShapeDtypeStruct((rank, 2 * rank), jnp.float32),
        ],
        compiler_params=params(16),
        name="cov_in",
    )(packed, *pieces)


def cov_out_kernel(x_ref, cov_ref, *refs):
    pieces, (cov_out, sample_out) = refs[:-2], refs[-2:]
    g = total(pieces)
    cov_out[...] = cov_ref[...] + covariance(g, True)
    samples_of(x_ref[...], g, sample_out)


def cov_out(x, cov, pieces, seqs):
    rank = x.shape[0]
    return pl.pallas_call(
        cov_out_kernel,
        in_specs=[vmem()] * (2 + len(pieces)),
        out_specs=[vmem()] * 2,
        out_shape=[
            jax.ShapeDtypeStruct((rank, 2 * rank), jnp.float32),
            jax.ShapeDtypeStruct((seqs, rank, 2 * rank), jnp.float32),
        ],
        compiler_params=params(16),
        name="cov_out",
    )(x, cov, *pieces)


def scales(steps, spread):
    r = (spread - 1.0) / (spread + 1.0)
    out = []
    for _ in range(steps):
        out.append(2.0 / (2.0 - r * r))
        r = r * r / (2.0 - r * r)
    return out


def damped_inverses(matrices):
    size = matrices[0].shape[0]
    rows = lax.broadcasted_iota(jnp.int32, (size, size), 0)
    cols = lax.broadcasted_iota(jnp.int32, (size, size), 1)
    diagonal = rows == cols
    eye = jnp.where(diagonal, 1.0, 0.0)
    units = [jnp.sum(jnp.where(diagonal, matrix, 0.0)) / size for matrix in matrices]
    damped = [matrix / unit + 0.1 * eye for matrix, unit in zip(matrices, units)]
    low, high = 0.1, size + 0.1
    start = 2.0 / (low + high)
    steps = scales(7, high / low)
    y = [matrix * start for matrix in damped]
    x = [(2.0 * start * steps[0]) * eye - (start * steps[0]) * v for v in y]
    y = [steps[0] * (2.0 * v - nn(v, v, HIGHEST)) for v in y]
    for scale in steps[1:-1]:
        both = [nn(jnp.concatenate(pair, axis=0), pair[1], HIGHEST) for pair in zip(x, y)]
        x = [scale * (2.0 * u - product[:size]) for u, product in zip(x, both)]
        y = [scale * (2.0 * v - product[size:]) for v, product in zip(y, both)]
    x = [steps[-1] * (2.0 * u - nn(u, v, HIGHEST)) for u, v in zip(x, y)]
    rest = [eye - nn(matrix, u, HIGHEST) for matrix, u in zip(damped, x)]
    x = [u + nn(u, r, HIGHEST) for u, r in zip(x, rest)]
    return [u / unit for u, unit in zip(x, units)]


def split(value):
    high = value.astype(jnp.bfloat16)
    rest = value - high.astype(jnp.float32)
    middle = rest.astype(jnp.bfloat16)
    low = (rest - middle.astype(jnp.float32)).astype(jnp.bfloat16)
    return high, middle, low


def score_kernel(tokens, place_ref, own_ref, other_ref, sample_ref, *refs):
    pieces, (out, held, half) = refs[:-3], refs[-3:]
    parts = held.shape[0]
    for k, piece in enumerate(pieces):
        held[place_ref[0] ^ k] = piece[...]
    pair = (own_ref[...] + other_ref[...]) / tokens
    size, both = pair.shape
    left, right = damped_inverses([pair[:, :size], pair[:, size:]])
    samples = [sample_ref[s] for s in range(sample_ref.shape[0])]
    seqs = len(samples)
    blocks = held.shape[1]
    pairs = parts * blocks
    first = jnp.concatenate(split(left), axis=0)
    none = jnp.zeros_like(first)
    first = jnp.concatenate(
        [jnp.concatenate([first, none], axis=1), jnp.concatenate([none, first], axis=1)], axis=0
    )
    none = jnp.zeros_like(right)
    twice = jnp.concatenate(
        [jnp.concatenate([right, none], axis=1), jnp.concatenate([none, right], axis=1)], axis=0
    )
    high, middle, _ = split(twice)
    once = jnp.concatenate([high, middle], axis=1)
    second = jnp.concatenate([once, once], axis=0)

    for part in range(parts // 2):
        for block in range(0, blocks, 2):
            rows = jnp.concatenate(
                [
                    held[part, block],
                    held[part + parts // 2, block],
                    held[part, block + 1],
                    held[part + parts // 2, block + 1],
                ],
                axis=0,
            )
            result = nt(first, rows)
            for k in range(2):
                three = result[3 * size * k : 3 * size * (k + 1)]
                value = three[:size] + three[size : 2 * size] + three[2 * size :]
                high, middle, _ = split(value)
                pair = (2 * part + k) * blocks + block
                lanes = slice(pair * both, (pair + 2) * both)
                half[0, :, lanes] = high
                half[1, :, lanes] = middle
    lines = [[] for _ in range(seqs)]
    for pair in range(pairs):
        lanes = slice(pair * both, (pair + 1) * both)
        rows = jnp.concatenate([half[0, :, lanes], half[1, :, lanes]], axis=1)
        result = nn(rows, second)
        result = (result[:, :both] + result[:, both:]).astype(jnp.bfloat16).astype(jnp.float32)
        for s in range(seqs):
            lines[s].append(jnp.sum(result * samples[s], axis=0, keepdims=True))
    lines = jnp.concatenate([line for part in lines for line in part], axis=0)
    shape = (8, both)
    ends = jnp.where(
        (lax.broadcasted_iota(jnp.int32, shape, 1) < size)
        == (lax.broadcasted_iota(jnp.int32, shape, 0) == 0),
        1.0,
        0.0,
    )
    result = nt(ends, lines, HIGHEST)
    for s in range(seqs):
        for k in range(2):
            out[s : s + 1, k * pairs : (k + 1) * pairs] = result[
                k : k + 1, s * pairs : (s + 1) * pairs
            ]


def score(place, own, other, sample, pieces, tokens):
    blocks, rank, both = pieces[0].shape
    parts = len(pieces)
    pairs = parts * blocks
    seqs = sample.shape[0]
    return pl.pallas_call(
        functools.partial(score_kernel, tokens),
        in_specs=[smem()] + [vmem()] * (3 + len(pieces)),
        out_specs=vmem(),
        out_shape=jax.ShapeDtypeStruct((seqs, 2 * pairs), jnp.float32),
        scratch_shapes=[
            pltpu.VMEM((parts, blocks, rank, both), pieces[0].dtype),
            pltpu.VMEM((2, rank, pairs * both), jnp.bfloat16),
        ],
        compiler_params=params(16),
        name="score",
    )(place, own, other, sample, *pieces)


def swap(value, axis, bit):
    return lax.ppermute(value, axis, [(i, i ^ bit) for i in range(lax.axis_size(axis))])


def local_owned(acts, grads, proj_in, proj_out, queries):
    seqs, length, _ = acts.shape
    parts = lax.axis_size("dp")
    tokens = seqs * length * parts
    column = lax.axis_index("tensor").astype(jnp.int32)
    side = (column >= 2).astype(jnp.int32).reshape(1)
    place = lax.axis_index("dp").astype(jnp.int32).reshape(1)
    x_near, x_far, early = project_in(side, acts, proj_in, grads)
    x_pieces = to_owner(x_near, x_far)
    near, far, packed = project_out(side, grads, proj_out, queries, early)
    pieces = to_owner(near, far)
    packed, x, cov = cov_in(packed, x_pieces)
    query_pieces = [packed] + [swap(packed, "dp", bits) for bits in range(1, parts)]
    cov, sample = cov_out(x, cov, pieces, seqs)
    other = jnp.zeros_like(cov)
    bit = 1
    while bit < parts:
        cov = cov if bit == 1 else cov + other
        other = swap(cov, "dp", bit)
        bit *= 2
    scores = score(place, cov, other, sample, query_pieces, tokens)
    outer = lax.ppermute(scores, "tensor", [(1, 0), (2, 3)])
    outer = outer + lax.ppermute(scores, "tensor", [(2, 0), (1, 3)])
    back = lax.ppermute(outer, "tensor", [(0, 1), (3, 2)])
    return jnp.where((column == 1) | (column == 2), back, outer)


def damp(matrix):
    size = matrix.shape[0]
    shift_by = 0.1 * jnp.trace(matrix) / size
    return matrix + shift_by * jnp.eye(size, dtype=matrix.dtype)


def chol_apply(factor, rhs):
    lower_sol = lax.linalg.triangular_solve(factor, rhs, left_side=True, lower=True)
    return lax.linalg.triangular_solve(
        factor, lower_sol, left_side=True, lower=True, transpose_a=True
    )


def precondition(query, left, right_side):
    count, rank = (query.shape[0], query.shape[1])
    left_fac = jnp.linalg.cholesky(left)
    right_fac = jnp.linalg.cholesky(right_side)
    stacked = jnp.transpose(query, (1, 0, 2)).reshape(rank, count * rank)
    middle = chol_apply(left_fac, stacked).reshape(rank, count, rank)
    turned = jnp.transpose(middle, (2, 1, 0)).reshape(rank, count * rank)
    result = chol_apply(right_fac, turned).reshape(rank, count, rank)
    return jnp.transpose(result, (1, 2, 0))


def diagonal_blocks(whole, rank):
    return jnp.stack([whole[:, 0:rank, 0:rank], whole[:, rank : 2 * rank, rank : 2 * rank]], axis=1)


def local_general(acts, grads, proj_in, proj_out, queries):
    seq_count, length, width_loc = acts.shape
    rank = proj_in.shape[1]
    hidden_loc = grads.shape[3]
    flat = acts.reshape(-1, width_loc)
    xpart = nt(flat, proj_in.reshape(2 * rank, width_loc))
    gpart = jnp.concatenate(
        [nt(grads[layer].reshape(-1, hidden_loc), proj_out[layer]) for layer in range(2)], axis=1
    )
    count = seq_count * length * lax.axis_size("dp")
    xin, gout = lax.psum((xpart, gpart), "tensor")
    in_cov, out_cov = lax.psum((tn(xin, xin, HIGHEST), tn(gout, gout, HIGHEST)), "dp")
    whole = (
        jnp.einsum(
            "sto,sti->soi",
            gout.reshape(seq_count, length, 2 * rank),
            xin.reshape(seq_count, length, 2 * rank),
            precision=HIGHEST,
        )
        / length
    )
    samples = diagonal_blocks(whole, rank)
    in_cov = in_cov / count
    out_cov = out_cov / count
    precond = []
    for layer in range(2):
        low = layer * rank
        damped_in = damp(in_cov[low : low + rank, low : low + rank])
        damped_out = damp(out_cov[low : low + rank, low : low + rank])
        precond.append(precondition(queries[:, layer].astype(jnp.float32), damped_out, damped_in))
    query_count = queries.shape[0]
    query_b = jnp.stack(precond, axis=1).astype(jnp.bfloat16).reshape(query_count, -1)
    sample_b = samples.astype(jnp.bfloat16).reshape(seq_count, -1)
    return nt(sample_b, lax.all_gather(query_b, "dp", axis=0, tiled=True))


def local(acts, grads, proj_in, proj_out, queries):
    parts = lax.axis_size("dp")
    even = parts > 1 and parts & (parts - 1) == 0
    if lax.axis_size("tensor") == 4 and even and queries.shape[0] % 4 == 0:
        return local_owned(acts, grads, proj_in, proj_out, queries)
    return local_general(acts, grads, proj_in, proj_out, queries)


def solution(mesh):
    placed = (
        P(("groups", "dp"), None, "tensor"),
        P(None, ("groups", "dp"), None, "tensor"),
        P(None, None, "tensor"),
        P(None, None, "tensor"),
        P("dp", None, None, None),
    )
    return jax.shard_map(
        local, mesh=mesh, in_specs=placed, out_specs=P(("groups", "dp"), None), check_vma=False
    )
```

```python
import functools

import jax
import jax.numpy as jnp
from jax import lax
from jax.experimental import pallas as pl
from jax.experimental.pallas import tpu as pltpu
from jax.sharding import PartitionSpec as P

HIGHEST = lax.Precision.HIGHEST
MIB = 1024 * 1024


def nt(a, b, precision=None):
    return lax.dot_general(
        a, b, (((1,), (1,)), ((), ())), precision=precision, preferred_element_type=jnp.float32
    )


def tn(a, b, precision=None):
    return lax.dot_general(
        a, b, (((0,), (0,)), ((), ())), precision=precision, preferred_element_type=jnp.float32
    )


def nn(a, b, precision=None):
    return jnp.dot(a, b, precision=precision, preferred_element_type=jnp.float32)


def vmem():
    return pl.BlockSpec(memory_space=pltpu.VMEM)


def smem():
    return pl.BlockSpec(memory_space=pltpu.SMEM)


def hbm():
    return pl.BlockSpec(memory_space=pl.ANY)


def in_hbm(value):
    return pltpu.with_memory_space_constraint(value, pltpu.HBM)


def params(mib):
    return pltpu.CompilerParams(vmem_limit_bytes=mib * MIB)


def project_in_kernel(
    side_ref, rows_hbm, proj_hbm, grads_hbm, near, far, early, rows, proj, acc, sems, proj_sem, early_sem
):
    seqs, length, width = rows.shape
    rank = proj.shape[1]
    proj_copy = pltpu.make_async_copy(proj_hbm, proj, proj_sem)
    proj_copy.start()

    def copy(s):
        return pltpu.make_async_copy(rows_hbm.at[s], rows.at[s], sems.at[s])

    for s in range(seqs):
        copy(s).start()
    early_copy = pltpu.make_async_copy(
        grads_hbm.at[:, 0, :, pl.ds(0, early.shape[2])], early, early_sem
    )
    early_copy.start()
    proj_copy.wait()

    group = 2 - seqs % 2

    @pl.loop(0, seqs // group)
    def _(step):
        for k in range(group):
            copy(step * group + k).wait()
        for k in range(group):
            s = step * group + k
            part = nt(proj[...].reshape(2 * rank, width), rows[s])
            tokens = pl.ds(pl.multiple_of(s * length, length), length)
            acc[0, :, tokens] = part[:rank]
            acc[1, :, tokens] = part[rank:]

    far[...] = acc[1 - side_ref[0]]
    near[...] = acc[side_ref[0]]
    early_copy.wait()


def project_in(side, rows, proj, grads):
    seqs, length, _ = rows.shape
    early = (2, length, grads.shape[3] // 2)
    rank = proj.shape[1]
    return pl.pallas_call(
        project_in_kernel,
        in_specs=[smem(), hbm(), hbm(), hbm()],
        out_specs=[vmem()] * 3,
        out_shape=[
            jax.ShapeDtypeStruct((rank, seqs * length), jnp.float32),
            jax.ShapeDtypeStruct((rank, seqs * length), jnp.float32),
            jax.ShapeDtypeStruct(early, grads.dtype),
        ],
        scratch_shapes=[
            pltpu.VMEM(rows.shape, rows.dtype),
            pltpu.VMEM(proj.shape, proj.dtype),
            pltpu.VMEM((2, rank, seqs * length), jnp.float32),
            pltpu.SemaphoreType.DMA((seqs,)),
            pltpu.SemaphoreType.DMA,
            pltpu.SemaphoreType.DMA,
        ],
        compiler_params=params(16),
        name="project_in",
    )(side, in_hbm(rows), in_hbm(proj), in_hbm(grads))


def project_out_kernel(side_ref, rows_hbm, proj_ref, queries_hbm, early, *refs):
    (near, far, packed), (rows, held, acc, sems, sem) = refs[:3], refs[3:]
    _, seqs, length, width = rows.shape
    parts = sems.shape[2]
    piece = width // parts
    copies = {}
    for s in range(seqs):
        for part in range(parts):
            if s == 0 and part < parts // 2:
                continue
            lanes = pl.ds(part * piece, piece)
            for layer in range(2):
                copies[s, part, layer] = pltpu.make_async_copy(
                    rows_hbm.at[layer, s, :, lanes],
                    rows.at[layer, s, :, lanes],
                    sems.at[layer, s, part],
                )
                copies[s, part, layer].start()
    copy = pltpu.make_async_copy(queries_hbm.at[:, side_ref[0]], held, sem)
    copy.start()
    for s in range(seqs):
        tokens = slice(s * length, (s + 1) * length)
        for part in range(parts):
            lanes = slice(part * piece, (part + 1) * piece)
            ready = s == 0 and part < parts // 2
            for layer in range(2):
                if not ready:
                    copies[s, part, layer].wait()
            for layer in range(2):
                block = early[layer, :, lanes] if ready else rows[layer, s, :, lanes]
                value = nt(proj_ref[layer, :, lanes], block)
                if part > 0:
                    value = value + acc[layer, :, tokens]
                acc[layer, :, tokens] = value
    far[...] = acc[1 - side_ref[0]]
    near[...] = acc[side_ref[0]]
    copy.wait()
    blocks = held.shape[0] // 2
    for k in range(blocks):
        pair = [held[k].astype(jnp.float32), held[k + blocks].astype(jnp.float32)]
        packed[k] = jnp.concatenate(pair, axis=1).astype(held.dtype)


def project_out(side, rows, proj, queries, early):
    _, seqs, length, width = rows.shape
    rank = proj.shape[1]
    count = queries.shape[0]
    parts = 4 if width % 512 == 0 else 2
    return pl.pallas_call(
        project_out_kernel,
        in_specs=[smem(), hbm(), vmem(), hbm(), vmem()],
        out_specs=[vmem()] * 3,
        out_shape=[
            jax.ShapeDtypeStruct((rank, seqs * length), jnp.float32),
            jax.ShapeDtypeStruct((rank, seqs * length), jnp.float32),
            jax.ShapeDtypeStruct((count // 2, rank, 2 * rank), queries.dtype),
        ],
        scratch_shapes=[
            pltpu.VMEM(rows.shape, rows.dtype),
            pltpu.VMEM((count, rank, rank), queries.dtype),
            pltpu.VMEM((2, rank, seqs * length), jnp.float32),
            pltpu.SemaphoreType.DMA((2, seqs, parts)),
            pltpu.SemaphoreType.DMA,
        ],
        compiler_params=params(40),
        name="project_out",
    )(side, in_hbm(rows), proj, in_hbm(queries), early)


def across(value):
    return lax.ppermute(value, "tensor", [(1, 2), (2, 1)])


def to_owner(near, far):
    return [
        near,
        lax.ppermute(near, "tensor", [(0, 1), (3, 2)]),
        across(far),
        lax.ppermute(far, "tensor", [(0, 2), (3, 1)]),
    ]


def total(pieces):
    value = pieces[0][...]
    for piece in pieces[1:]:
        value = value + piece[...]
    return value


def covariance(value, right):
    none = jnp.zeros_like(value)
    both = [none, value] if right else [value, none]
    return nt(value, jnp.concatenate(both, axis=0), HIGHEST)


def samples_of(x, g, sample_out):
    seqs = sample_out.shape[0]
    length = g.shape[1] // seqs
    for s in range(seqs):
        tokens = slice(s * length, (s + 1) * length)
        sample = nt(x[:, tokens], g[:, tokens], HIGHEST) / length
        sample = sample.astype(jnp.bfloat16).astype(jnp.float32)
        sample_out[s] = jnp.concatenate([sample, sample], axis=1)


def cov_in_kernel(packed_ref, *refs):
    pieces, (packed, x_out, cov_out) = refs[:-3], refs[-3:]
    packed[...] = packed_ref[...]
    x = total(pieces)
    x_out[...] = x
    cov_out[...] = covariance(x, False)


def cov_in(packed, pieces):
    rank, tokens = pieces[0].shape
    return pl.pallas_call(
        cov_in_kernel,
        in_specs=[vmem()] * (1 + len(pieces)),
        out_specs=[vmem()] * 3,
        out_shape=[
            jax.ShapeDtypeStruct(packed.shape, packed.dtype),
            jax.ShapeDtypeStruct((rank, tokens), jnp.float32),
            jax.ShapeDtypeStruct((rank, 2 * rank), jnp.float32),
        ],
        compiler_params=params(16),
        name="cov_in",
    )(packed, *pieces)


def cov_out_kernel(x_ref, cov_ref, *refs):
    pieces, (cov_out, sample_out) = refs[:-2], refs[-2:]
    g = total(pieces)
    cov_out[...] = cov_ref[...] + covariance(g, True)
    samples_of(x_ref[...], g, sample_out)


def cov_out(x, cov, pieces, seqs):
    rank = x.shape[0]
    return pl.pallas_call(
        cov_out_kernel,
        in_specs=[vmem()] * (2 + len(pieces)),
        out_specs=[vmem()] * 2,
        out_shape=[
            jax.ShapeDtypeStruct((rank, 2 * rank), jnp.float32),
            jax.ShapeDtypeStruct((seqs, rank, 2 * rank), jnp.float32),
        ],
        compiler_params=params(16),
        name="cov_out",
    )(x, cov, *pieces)


def scales(steps, spread):
    r = (spread - 1.0) / (spread + 1.0)
    out = []
    for _ in range(steps):
        out.append(2.0 / (2.0 - r * r))
        r = r * r / (2.0 - r * r)
    return out


def halves(value):
    high = value.astype(jnp.bfloat16)
    return high, (value - high.astype(jnp.float32)).astype(jnp.bfloat16)


def stacked(value):
    once = jnp.concatenate(halves(value), axis=1)
    return jnp.concatenate([once, once], axis=0)


def product(left, right):
    lanes = right.shape[1]
    both = nn(jnp.concatenate(halves(left), axis=1), stacked(right))
    return both[:, :lanes] + both[:, lanes:]


def damped_inverses(pair):
    size, both = pair.shape
    left = lax.broadcasted_iota(jnp.int32, pair.shape, 1) < size
    whole = jnp.concatenate([jnp.where(left, pair, 0.0), jnp.where(left, 0.0, pair)], axis=0)
    rows = lax.broadcasted_iota(jnp.int32, whole.shape, 0)
    cols = lax.broadcasted_iota(jnp.int32, whole.shape, 1)
    diagonal = rows == cols
    on_diagonal = jnp.where(diagonal, whole, 0.0)
    unit = jnp.where(
        rows < size, jnp.sum(on_diagonal[:size]) / size, jnp.sum(on_diagonal[size:]) / size
    )
    eye = jnp.where(diagonal, 1.0, 0.0)
    matrix = whole / unit + 0.1 * eye
    low, high = 0.1, size + 0.1
    start = 2.0 / (low + high)
    steps = scales(7, high / low)
    y = matrix * start
    x = (2.0 * start * steps[0]) * eye - (start * steps[0]) * y
    y = steps[0] * (2.0 * y - product(y, y))
    for scale in steps[1:-1]:
        turn = product(jnp.concatenate([x, y], axis=0), y)
        x = scale * (2.0 * x - turn[:both])
        y = scale * (2.0 * y - turn[both:])
    x = steps[-1] * (2.0 * x - product(x, y))
    x = x + product(x, eye - product(matrix, x))
    x = x + product(x, eye - nn(matrix, x, HIGHEST))
    return x / unit


def score_kernel(tokens, place_ref, own_ref, other_ref, sample_ref, *refs):
    pieces, (out, held, half) = refs[:-3], refs[-3:]
    parts = held.shape[0]
    for k, piece in enumerate(pieces):
        held[place_ref[0] ^ k] = piece[...]
    pair = (own_ref[...] + other_ref[...]) / tokens
    size, both = pair.shape
    inverses = damped_inverses(pair)
    samples = [sample_ref[s] for s in range(sample_ref.shape[0])]
    seqs = len(samples)
    blocks = held.shape[1]
    pairs = parts * blocks
    first = jnp.concatenate(halves(inverses[:size, :size]), axis=0)
    none = jnp.zeros_like(first)
    first = jnp.concatenate(
        [jnp.concatenate([first, none], axis=1), jnp.concatenate([none, first], axis=1)], axis=0
    )
    right = inverses[size:]
    second = stacked(jnp.concatenate([pltpu.roll(right, size, 1), right], axis=0))
    for part in range(parts // 2):
        for block in range(0, blocks, 2):
            rows = jnp.concatenate(
                [
                    held[part, block],
                    held[part + parts // 2, block],
                    held[part, block + 1],
                    held[part + parts // 2, block + 1],
                ],
                axis=0,
            )
            result = nt(first, rows)
            for k in range(2):
                two = result[both * k : both * (k + 1)]
                high, middle = halves(two[:size] + two[size:])
                pair = (2 * part + k) * blocks + block
                lanes = slice(pair * both, (pair + 2) * both)
                half[0, :, lanes] = high
                half[1, :, lanes] = middle
    lines = [[] for _ in range(seqs)]
    for pair in range(pairs):
        lanes = slice(pair * both, (pair + 1) * both)
        rows = jnp.concatenate([half[0, :, lanes], half[1, :, lanes]], axis=1)
        result = nn(rows, second)
        result = (result[:, :both] + result[:, both:]).astype(jnp.bfloat16).astype(jnp.float32)
        for s in range(seqs):
            lines[s].append(jnp.sum(result * samples[s], axis=0, keepdims=True))
    lines = jnp.concatenate([line for part in lines for line in part], axis=0)
    shape = (8, both)
    ends = jnp.where(
        (lax.broadcasted_iota(jnp.int32, shape, 1) < size)
        == (lax.broadcasted_iota(jnp.int32, shape, 0) == 0),
        1.0,
        0.0,
    )
    result = nt(ends, lines, HIGHEST)
    for s in range(seqs):
        for k in range(2):
            out[s : s + 1, k * pairs : (k + 1) * pairs] = result[
                k : k + 1, s * pairs : (s + 1) * pairs
            ]


def score(place, own, other, sample, pieces, tokens):
    blocks, rank, both = pieces[0].shape
    parts = len(pieces)
    pairs = parts * blocks
    seqs = sample.shape[0]
    return pl.pallas_call(
        functools.partial(score_kernel, tokens),
        in_specs=[smem()] + [vmem()] * (3 + len(pieces)),
        out_specs=vmem(),
        out_shape=jax.ShapeDtypeStruct((seqs, 2 * pairs), jnp.float32),
        scratch_shapes=[
            pltpu.VMEM((parts, blocks, rank, both), pieces[0].dtype),
            pltpu.VMEM((2, rank, pairs * both), jnp.bfloat16),
        ],
        compiler_params=params(16),
        name="score",
    )(place, own, other, sample, *pieces)


def swap(value, axis, bit):
    return lax.ppermute(value, axis, [(i, i ^ bit) for i in range(lax.axis_size(axis))])


def local_owned(acts, grads, proj_in, proj_out, queries):
    seqs, length, _ = acts.shape
    parts = lax.axis_size("dp")
    tokens = seqs * length * parts
    column = lax.axis_index("tensor").astype(jnp.int32)
    side = (column >= 2).astype(jnp.int32).reshape(1)
    place = lax.axis_index("dp").astype(jnp.int32).reshape(1)
    x_near, x_far, early = project_in(side, acts, proj_in, grads)
    x_pieces = to_owner(x_near, x_far)
    near, far, packed = project_out(side, grads, proj_out, queries, early)
    pieces = to_owner(near, far)
    packed, x, cov = cov_in(packed, x_pieces)
    query_pieces = [packed] + [swap(packed, "dp", bits) for bits in range(1, parts)]
    cov, sample = cov_out(x, cov, pieces, seqs)
    other = jnp.zeros_like(cov)
    bit = 1
    while bit < parts:
        cov = cov if bit == 1 else cov + other
        other = swap(cov, "dp", bit)
        bit *= 2
    scores = score(place, cov, other, sample, query_pieces, tokens)
    owner = (column == 1) | (column == 2)
    pieces = [
        across(scores),
        lax.ppermute(scores, "tensor", [(1, 0), (2, 3)]),
        lax.ppermute(scores, "tensor", [(2, 0), (1, 3)]),
    ]
    return jnp.where(owner, scores, 0.0) + pieces[0] + pieces[1] + pieces[2]


def damp(matrix):
    size = matrix.shape[0]
    shift_by = 0.1 * jnp.trace(matrix) / size
    return matrix + shift_by * jnp.eye(size, dtype=matrix.dtype)


def chol_apply(factor, rhs):
    lower_sol = lax.linalg.triangular_solve(factor, rhs, left_side=True, lower=True)
    return lax.linalg.triangular_solve(
        factor, lower_sol, left_side=True, lower=True, transpose_a=True
    )


def precondition(query, left, right_side):
    count, rank = (query.shape[0], query.shape[1])
    left_fac = jnp.linalg.cholesky(left)
    right_fac = jnp.linalg.cholesky(right_side)
    stacked = jnp.transpose(query, (1, 0, 2)).reshape(rank, count * rank)
    middle = chol_apply(left_fac, stacked).reshape(rank, count, rank)
    turned = jnp.transpose(middle, (2, 1, 0)).reshape(rank, count * rank)
    result = chol_apply(right_fac, turned).reshape(rank, count, rank)
    return jnp.transpose(result, (1, 2, 0))


def diagonal_blocks(whole, rank):
    return jnp.stack([whole[:, 0:rank, 0:rank], whole[:, rank : 2 * rank, rank : 2 * rank]], axis=1)


def local_general(acts, grads, proj_in, proj_out, queries):
    seq_count, length, width_loc = acts.shape
    rank = proj_in.shape[1]
    hidden_loc = grads.shape[3]
    flat = acts.reshape(-1, width_loc)
    xpart = nt(flat, proj_in.reshape(2 * rank, width_loc))
    gpart = jnp.concatenate(
        [nt(grads[layer].reshape(-1, hidden_loc), proj_out[layer]) for layer in range(2)], axis=1
    )
    count = seq_count * length * lax.axis_size("dp")
    xin, gout = lax.psum((xpart, gpart), "tensor")
    in_cov, out_cov = lax.psum((tn(xin, xin, HIGHEST), tn(gout, gout, HIGHEST)), "dp")
    whole = (
        jnp.einsum(
            "sto,sti->soi",
            gout.reshape(seq_count, length, 2 * rank),
            xin.reshape(seq_count, length, 2 * rank),
            precision=HIGHEST,
        )
        / length
    )
    samples = diagonal_blocks(whole, rank)
    in_cov = in_cov / count
    out_cov = out_cov / count
    precond = []
    for layer in range(2):
        low = layer * rank
        damped_in = damp(in_cov[low : low + rank, low : low + rank])
        damped_out = damp(out_cov[low : low + rank, low : low + rank])
        precond.append(precondition(queries[:, layer].astype(jnp.float32), damped_out, damped_in))
    query_count = queries.shape[0]
    query_b = jnp.stack(precond, axis=1).astype(jnp.bfloat16).reshape(query_count, -1)
    sample_b = samples.astype(jnp.bfloat16).reshape(seq_count, -1)
    return nt(sample_b, lax.all_gather(query_b, "dp", axis=0, tiled=True))


def local(acts, grads, proj_in, proj_out, queries):
    parts = lax.axis_size("dp")
    even = parts > 1 and parts & (parts - 1) == 0
    if lax.axis_size("tensor") == 4 and even and queries.shape[0] % 4 == 0:
        return local_owned(acts, grads, proj_in, proj_out, queries)
    return local_general(acts, grads, proj_in, proj_out, queries)


def solution(mesh):
    placed = (
        P(("groups", "dp"), None, "tensor"),
        P(None, ("groups", "dp"), None, "tensor"),
        P(None, None, "tensor"),
        P(None, None, "tensor"),
        P("dp", None, None, None),
    )
    return jax.shard_map(
        local, mesh=mesh, in_specs=placed, out_specs=P(("groups", "dp"), None), check_vma=False
    )
```

```python
import functools

import jax
import jax.numpy as jnp
from jax import lax
from jax.experimental import pallas as pl
from jax.experimental.pallas import tpu as pltpu
from jax.sharding import PartitionSpec as P

HIGHEST = lax.Precision.HIGHEST
MIB = 1024 * 1024


def nt(a, b, precision=None):
    return lax.dot_general(
        a, b, (((1,), (1,)), ((), ())), precision=precision, preferred_element_type=jnp.float32
    )


def tn(a, b, precision=None):
    return lax.dot_general(
        a, b, (((0,), (0,)), ((), ())), precision=precision, preferred_element_type=jnp.float32
    )


def nn(a, b, precision=None):
    return jnp.dot(a, b, precision=precision, preferred_element_type=jnp.float32)


def vmem():
    return pl.BlockSpec(memory_space=pltpu.VMEM)


def smem():
    return pl.BlockSpec(memory_space=pltpu.SMEM)


def hbm():
    return pl.BlockSpec(memory_space=pl.ANY)


def in_hbm(value):
    return pltpu.with_memory_space_constraint(value, pltpu.HBM)


def params(mib):
    return pltpu.CompilerParams(vmem_limit_bytes=mib * MIB)


def project_in_kernel(
    parity_ref, rows_hbm, proj_hbm, grads_hbm, first, second, early, rows, proj, acc, sems, proj_sem, early_sem
):
    seqs, length, width = rows.shape
    rank = proj.shape[1]
    proj_copy = pltpu.make_async_copy(proj_hbm, proj, proj_sem)
    proj_copy.start()

    def copy(s):
        return pltpu.make_async_copy(rows_hbm.at[s], rows.at[s], sems.at[s])

    for s in range(seqs):
        copy(s).start()
    early_copy = pltpu.make_async_copy(
        grads_hbm.at[:, 0, :, pl.ds(0, early.shape[2])], early, early_sem
    )
    early_copy.start()
    proj_copy.wait()

    group = 2 - seqs % 2

    @pl.loop(0, seqs // group)
    def _(step):
        for k in range(group):
            copy(step * group + k).wait()
        for k in range(group):
            s = step * group + k
            part = nt(proj[...].reshape(2 * rank, width), rows[s])
            tokens = pl.ds(pl.multiple_of(s * length, length), length)
            acc[0, :, tokens] = part[:rank]
            acc[1, :, tokens] = part[rank:]

    first[...] = acc[parity_ref[0]]
    second[...] = acc[1 - parity_ref[0]]
    early_copy.wait()


def project_in(parity, rows, proj, grads):
    seqs, length, _ = rows.shape
    early = (2, length, grads.shape[3] // 2)
    rank = proj.shape[1]
    return pl.pallas_call(
        project_in_kernel,
        in_specs=[smem(), hbm(), hbm(), hbm()],
        out_specs=[vmem()] * 3,
        out_shape=[
            jax.ShapeDtypeStruct((rank, seqs * length), jnp.float32),
            jax.ShapeDtypeStruct((rank, seqs * length), jnp.float32),
            jax.ShapeDtypeStruct(early, grads.dtype),
        ],
        scratch_shapes=[
            pltpu.VMEM(rows.shape, rows.dtype),
            pltpu.VMEM(proj.shape, proj.dtype),
            pltpu.VMEM((2, rank, seqs * length), jnp.float32),
            pltpu.SemaphoreType.DMA((seqs,)),
            pltpu.SemaphoreType.DMA,
            pltpu.SemaphoreType.DMA,
        ],
        compiler_params=params(16),
        name="project_in",
    )(parity, in_hbm(rows), in_hbm(proj), in_hbm(grads))


def project_out_kernel(parity_ref, side_ref, rows_hbm, proj_ref, queries_hbm, early, *refs):
    (first, second, packed), (rows, held, acc, sems, sem) = refs[:3], refs[3:]
    _, seqs, length, width = rows.shape
    parts = sems.shape[2]
    piece = width // parts
    copies = {}
    for s in range(seqs):
        for part in range(parts):
            if s == 0 and part < parts // 2:
                continue
            lanes = pl.ds(part * piece, piece)
            for layer in range(2):
                copies[s, part, layer] = pltpu.make_async_copy(
                    rows_hbm.at[layer, s, :, lanes],
                    rows.at[layer, s, :, lanes],
                    sems.at[layer, s, part],
                )
                copies[s, part, layer].start()
    copy = pltpu.make_async_copy(queries_hbm.at[:, side_ref[0]], held, sem)
    copy.start()
    for s in range(seqs):
        tokens = slice(s * length, (s + 1) * length)
        for part in range(parts):
            lanes = slice(part * piece, (part + 1) * piece)
            ready = s == 0 and part < parts // 2
            for layer in range(2):
                if not ready:
                    copies[s, part, layer].wait()
            for layer in range(2):
                block = early[layer, :, lanes] if ready else rows[layer, s, :, lanes]
                value = nt(proj_ref[layer, :, lanes], block)
                if part > 0:
                    value = value + acc[layer, :, tokens]
                acc[layer, :, tokens] = value
    first[...] = acc[parity_ref[0]]
    second[...] = acc[1 - parity_ref[0]]
    copy.wait()
    blocks = held.shape[0] // 2
    for k in range(blocks):
        pair = [held[k].astype(jnp.float32), held[k + blocks].astype(jnp.float32)]
        packed[k] = jnp.concatenate(pair, axis=1).astype(held.dtype)


def project_out(parity, side, rows, proj, queries, early):
    _, seqs, length, width = rows.shape
    rank = proj.shape[1]
    count = queries.shape[0]
    parts = 4 if width % 512 == 0 else 2
    return pl.pallas_call(
        project_out_kernel,
        in_specs=[smem(), smem(), hbm(), vmem(), hbm(), vmem()],
        out_specs=[vmem()] * 3,
        out_shape=[
            jax.ShapeDtypeStruct((rank, seqs * length), jnp.float32),
            jax.ShapeDtypeStruct((rank, seqs * length), jnp.float32),
            jax.ShapeDtypeStruct((count // 2, rank, 2 * rank), queries.dtype),
        ],
        scratch_shapes=[
            pltpu.VMEM(rows.shape, rows.dtype),
            pltpu.VMEM((count, rank, rank), queries.dtype),
            pltpu.VMEM((2, rank, seqs * length), jnp.float32),
            pltpu.SemaphoreType.DMA((2, seqs, parts)),
            pltpu.SemaphoreType.DMA,
        ],
        compiler_params=params(40),
        name="project_out",
    )(parity, side, in_hbm(rows), proj, in_hbm(queries), early)


def to_owner(first, second):
    return [
        second,
        lax.ppermute(first, "tensor", [(3, 2), (2, 1)]),
        lax.ppermute(first, "tensor", [(0, 1), (1, 2)]),
        lax.ppermute(second, "tensor", [(0, 2), (3, 1)]),
    ]


def total(pieces):
    value = pieces[0][...]
    for piece in pieces[1:]:
        value = value + piece[...]
    return value


def covariance(value, right):
    none = jnp.zeros_like(value)
    both = [none, value] if right else [value, none]
    return nt(value, jnp.concatenate(both, axis=0), HIGHEST)


def samples_of(x, g, sample_out):
    seqs = sample_out.shape[0]
    length = g.shape[1] // seqs
    for s in range(seqs):
        tokens = slice(s * length, (s + 1) * length)
        sample = nt(x[:, tokens], g[:, tokens], HIGHEST) / length
        sample = sample.astype(jnp.bfloat16).astype(jnp.float32)
        sample_out[s] = jnp.concatenate([sample, sample], axis=1)


def cov_in_kernel(packed_ref, *refs):
    pieces, (packed, x_out, cov_out) = refs[:-3], refs[-3:]
    packed[...] = packed_ref[...]
    x = total(pieces)
    x_out[...] = x
    cov_out[...] = covariance(x, False)


def cov_in(packed, pieces):
    rank, tokens = pieces[0].shape
    return pl.pallas_call(
        cov_in_kernel,
        in_specs=[vmem()] * (1 + len(pieces)),
        out_specs=[vmem()] * 3,
        out_shape=[
            jax.ShapeDtypeStruct(packed.shape, packed.dtype),
            jax.ShapeDtypeStruct((rank, tokens), jnp.float32),
            jax.ShapeDtypeStruct((rank, 2 * rank), jnp.float32),
        ],
        compiler_params=params(16),
        name="cov_in",
    )(packed, *pieces)


def cov_out_kernel(x_ref, cov_ref, *refs):
    pieces, (cov_out, sample_out) = refs[:-2], refs[-2:]
    g = total(pieces)
    cov_out[...] = cov_ref[...] + covariance(g, True)
    samples_of(x_ref[...], g, sample_out)


def cov_out(x, cov, pieces, seqs):
    rank = x.shape[0]
    return pl.pallas_call(
        cov_out_kernel,
        in_specs=[vmem()] * (2 + len(pieces)),
        out_specs=[vmem()] * 2,
        out_shape=[
            jax.ShapeDtypeStruct((rank, 2 * rank), jnp.float32),
            jax.ShapeDtypeStruct((seqs, rank, 2 * rank), jnp.float32),
        ],
        compiler_params=params(16),
        name="cov_out",
    )(x, cov, *pieces)


def scales(steps, spread):
    r = (spread - 1.0) / (spread + 1.0)
    out = []
    for _ in range(steps):
        out.append(2.0 / (2.0 - r * r))
        r = r * r / (2.0 - r * r)
    return out


def halves(value):
    high = value.astype(jnp.bfloat16)
    return high, (value - high.astype(jnp.float32)).astype(jnp.bfloat16)


def stacked(value):
    once = jnp.concatenate(halves(value), axis=1)
    return jnp.concatenate([once, once], axis=0)


def product(left, right):
    lanes = right.shape[1]
    both = nn(jnp.concatenate(halves(left), axis=1), stacked(right))
    return both[:, :lanes] + both[:, lanes:]


def damped_inverses(pair):
    size, both = pair.shape
    left = lax.broadcasted_iota(jnp.int32, pair.shape, 1) < size
    whole = jnp.concatenate([jnp.where(left, pair, 0.0), jnp.where(left, 0.0, pair)], axis=0)
    rows = lax.broadcasted_iota(jnp.int32, whole.shape, 0)
    cols = lax.broadcasted_iota(jnp.int32, whole.shape, 1)
    diagonal = rows == cols
    on_diagonal = jnp.where(diagonal, whole, 0.0)
    unit = jnp.where(
        rows < size, jnp.sum(on_diagonal[:size]) / size, jnp.sum(on_diagonal[size:]) / size
    )
    eye = jnp.where(diagonal, 1.0, 0.0)
    matrix = whole / unit + 0.1 * eye
    low, high = 0.1, size + 0.1
    start = 2.0 / (low + high)
    steps = scales(7, high / low)
    y = matrix * start
    x = (2.0 * start * steps[0]) * eye - (start * steps[0]) * y
    y = steps[0] * (2.0 * y - product(y, y))
    for scale in steps[1:-1]:
        turn = product(jnp.concatenate([x, y], axis=0), y)
        x = scale * (2.0 * x - turn[:both])
        y = scale * (2.0 * y - turn[both:])
    x = steps[-1] * (2.0 * x - product(x, y))
    x = x + product(x, eye - product(matrix, x))
    x = x + product(x, eye - nn(matrix, x, HIGHEST))
    return x / unit


def score_kernel(tokens, place_ref, own_ref, other_ref, sample_ref, *refs):
    pieces, (out, held, half) = refs[:-3], refs[-3:]
    parts = held.shape[0]
    for k, piece in enumerate(pieces):
        held[place_ref[0] ^ k] = piece[...]
    pair = (own_ref[...] + other_ref[...]) / tokens
    size, both = pair.shape
    inverses = damped_inverses(pair)
    samples = [sample_ref[s] for s in range(sample_ref.shape[0])]
    seqs = len(samples)
    blocks = held.shape[1]
    pairs = parts * blocks
    first = jnp.concatenate(halves(inverses[:size, :size]), axis=0)
    none = jnp.zeros_like(first)
    first = jnp.concatenate(
        [jnp.concatenate([first, none], axis=1), jnp.concatenate([none, first], axis=1)], axis=0
    )
    right = inverses[size:]
    second = stacked(jnp.concatenate([pltpu.roll(right, size, 1), right], axis=0))
    for part in range(parts // 2):
        for block in range(0, blocks, 2):
            rows = jnp.concatenate(
                [
                    held[part, block],
                    held[part + parts // 2, block],
                    held[part, block + 1],
                    held[part + parts // 2, block + 1],
                ],
                axis=0,
            )
            result = nt(first, rows)
            for k in range(2):
                two = result[both * k : both * (k + 1)]
                high, middle = halves(two[:size] + two[size:])
                pair = (2 * part + k) * blocks + block
                lanes = slice(pair * both, (pair + 2) * both)
                half[0, :, lanes] = high
                half[1, :, lanes] = middle
    lines = [[] for _ in range(seqs)]
    for pair in range(pairs):
        lanes = slice(pair * both, (pair + 1) * both)
        rows = jnp.concatenate([half[0, :, lanes], half[1, :, lanes]], axis=1)
        result = nn(rows, second)
        result = (result[:, :both] + result[:, both:]).astype(jnp.bfloat16).astype(jnp.float32)
        for s in range(seqs):
            lines[s].append(jnp.sum(result * samples[s], axis=0, keepdims=True))
    lines = jnp.concatenate([line for part in lines for line in part], axis=0)
    shape = (8, both)
    ends = jnp.where(
        (lax.broadcasted_iota(jnp.int32, shape, 1) < size)
        == (lax.broadcasted_iota(jnp.int32, shape, 0) == 0),
        1.0,
        0.0,
    )
    result = nt(ends, lines, HIGHEST)
    for s in range(seqs):
        for k in range(2):
            out[s : s + 1, k * pairs : (k + 1) * pairs] = result[
                k : k + 1, s * pairs : (s + 1) * pairs
            ]


def score(place, own, other, sample, pieces, tokens):
    blocks, rank, both = pieces[0].shape
    parts = len(pieces)
    pairs = parts * blocks
    seqs = sample.shape[0]
    return pl.pallas_call(
        functools.partial(score_kernel, tokens),
        in_specs=[smem()] + [vmem()] * (3 + len(pieces)),
        out_specs=vmem(),
        out_shape=jax.ShapeDtypeStruct((seqs, 2 * pairs), jnp.float32),
        scratch_shapes=[
            pltpu.VMEM((parts, blocks, rank, both), pieces[0].dtype),
            pltpu.VMEM((2, rank, pairs * both), jnp.bfloat16),
        ],
        compiler_params=params(16),
        name="score",
    )(place, own, other, sample, *pieces)


def swap(value, axis, bit):
    return lax.ppermute(value, axis, [(i, i ^ bit) for i in range(lax.axis_size(axis))])


def local_owned(acts, grads, proj_in, proj_out, queries):
    seqs, length, _ = acts.shape
    parts = lax.axis_size("dp")
    tokens = seqs * length * parts
    column = lax.axis_index("tensor").astype(jnp.int32)
    side = (column >= 2).astype(jnp.int32).reshape(1)
    place = lax.axis_index("dp").astype(jnp.int32).reshape(1)
    parity = (column & 1).reshape(1)
    x_first, x_second, early = project_in(parity, acts, proj_in, grads)
    x_pieces = to_owner(x_first, x_second)
    first, second, packed = project_out(parity, side, grads, proj_out, queries, early)
    pieces = to_owner(first, second)
    packed, x, cov = cov_in(packed, x_pieces)
    query_pieces = [packed] + [swap(packed, "dp", bits) for bits in range(1, parts)]
    cov, sample = cov_out(x, cov, pieces, seqs)
    other = jnp.zeros_like(cov)
    bit = 1
    while bit < parts:
        cov = cov if bit == 1 else cov + other
        other = swap(cov, "dp", bit)
        bit *= 2
    scores = score(place, cov, other, sample, query_pieces, tokens)
    owner = (column == 1) | (column == 2)
    pieces = [
        lax.ppermute(scores, "tensor", [(2, 1), (1, 0)]),
        lax.ppermute(scores, "tensor", [(1, 2), (2, 3)]),
        lax.ppermute(scores, "tensor", [(1, 3), (2, 0)]),
    ]
    return jnp.where(owner, scores, 0.0) + pieces[0] + pieces[1] + pieces[2]


def damp(matrix):
    size = matrix.shape[0]
    shift_by = 0.1 * jnp.trace(matrix) / size
    return matrix + shift_by * jnp.eye(size, dtype=matrix.dtype)


def chol_apply(factor, rhs):
    lower_sol = lax.linalg.triangular_solve(factor, rhs, left_side=True, lower=True)
    return lax.linalg.triangular_solve(
        factor, lower_sol, left_side=True, lower=True, transpose_a=True
    )


def precondition(query, left, right_side):
    count, rank = (query.shape[0], query.shape[1])
    left_fac = jnp.linalg.cholesky(left)
    right_fac = jnp.linalg.cholesky(right_side)
    stacked = jnp.transpose(query, (1, 0, 2)).reshape(rank, count * rank)
    middle = chol_apply(left_fac, stacked).reshape(rank, count, rank)
    turned = jnp.transpose(middle, (2, 1, 0)).reshape(rank, count * rank)
    result = chol_apply(right_fac, turned).reshape(rank, count, rank)
    return jnp.transpose(result, (1, 2, 0))


def diagonal_blocks(whole, rank):
    return jnp.stack([whole[:, 0:rank, 0:rank], whole[:, rank : 2 * rank, rank : 2 * rank]], axis=1)


def local_general(acts, grads, proj_in, proj_out, queries):
    seq_count, length, width_loc = acts.shape
    rank = proj_in.shape[1]
    hidden_loc = grads.shape[3]
    flat = acts.reshape(-1, width_loc)
    xpart = nt(flat, proj_in.reshape(2 * rank, width_loc))
    gpart = jnp.concatenate(
        [nt(grads[layer].reshape(-1, hidden_loc), proj_out[layer]) for layer in range(2)], axis=1
    )
    count = seq_count * length * lax.axis_size("dp")
    xin, gout = lax.psum((xpart, gpart), "tensor")
    in_cov, out_cov = lax.psum((tn(xin, xin, HIGHEST), tn(gout, gout, HIGHEST)), "dp")
    whole = (
        jnp.einsum(
            "sto,sti->soi",
            gout.reshape(seq_count, length, 2 * rank),
            xin.reshape(seq_count, length, 2 * rank),
            precision=HIGHEST,
        )
        / length
    )
    samples = diagonal_blocks(whole, rank)
    in_cov = in_cov / count
    out_cov = out_cov / count
    precond = []
    for layer in range(2):
        low = layer * rank
        damped_in = damp(in_cov[low : low + rank, low : low + rank])
        damped_out = damp(out_cov[low : low + rank, low : low + rank])
        precond.append(precondition(queries[:, layer].astype(jnp.float32), damped_out, damped_in))
    query_count = queries.shape[0]
    query_b = jnp.stack(precond, axis=1).astype(jnp.bfloat16).reshape(query_count, -1)
    sample_b = samples.astype(jnp.bfloat16).reshape(seq_count, -1)
    return nt(sample_b, lax.all_gather(query_b, "dp", axis=0, tiled=True))


def local(acts, grads, proj_in, proj_out, queries):
    parts = lax.axis_size("dp")
    even = parts > 1 and parts & (parts - 1) == 0
    if lax.axis_size("tensor") == 4 and even and queries.shape[0] % 4 == 0:
        return local_owned(acts, grads, proj_in, proj_out, queries)
    return local_general(acts, grads, proj_in, proj_out, queries)


def solution(mesh):
    placed = (
        P(("groups", "dp"), None, "tensor"),
        P(None, ("groups", "dp"), None, "tensor"),
        P(None, None, "tensor"),
        P(None, None, "tensor"),
        P("dp", None, None, None),
    )
    return jax.shard_map(
        local, mesh=mesh, in_specs=placed, out_specs=P(("groups", "dp"), None), check_vma=False
    )
```

```python
import functools

import jax
import jax.numpy as jnp
from jax import lax
from jax.experimental import pallas as pl
from jax.experimental.pallas import tpu as pltpu
from jax.sharding import PartitionSpec as P

HIGHEST = lax.Precision.HIGHEST
MIB = 1024 * 1024


def nt(a, b, precision=None):
    return lax.dot_general(
        a, b, (((1,), (1,)), ((), ())), precision=precision, preferred_element_type=jnp.float32
    )


def tn(a, b, precision=None):
    return lax.dot_general(
        a, b, (((0,), (0,)), ((), ())), precision=precision, preferred_element_type=jnp.float32
    )


def nn(a, b, precision=None):
    return jnp.dot(a, b, precision=precision, preferred_element_type=jnp.float32)


def vmem():
    return pl.BlockSpec(memory_space=pltpu.VMEM)


def smem():
    return pl.BlockSpec(memory_space=pltpu.SMEM)


def hbm():
    return pl.BlockSpec(memory_space=pl.ANY)


def in_hbm(value):
    return pltpu.with_memory_space_constraint(value, pltpu.HBM)


def params(mib):
    return pltpu.CompilerParams(vmem_limit_bytes=mib * MIB)


def project_in_kernel(
    side_ref, rows_hbm, proj_hbm, grads_hbm, near, far, again, early, rows, proj, acc, sems, proj_sem, early_sem
):
    seqs, length, width = rows.shape
    rank = proj.shape[1]
    proj_copy = pltpu.make_async_copy(proj_hbm, proj, proj_sem)
    proj_copy.start()

    def copy(s):
        return pltpu.make_async_copy(rows_hbm.at[s], rows.at[s], sems.at[s])

    for s in range(seqs):
        copy(s).start()
    early_copy = pltpu.make_async_copy(
        grads_hbm.at[:, 0, :, pl.ds(0, early.shape[2])], early, early_sem
    )
    early_copy.start()
    proj_copy.wait()

    group = 2 - seqs % 2

    @pl.loop(0, seqs // group)
    def _(step):
        for k in range(group):
            copy(step * group + k).wait()
        for k in range(group):
            s = step * group + k
            part = nt(proj[...].reshape(2 * rank, width), rows[s])
            tokens = pl.ds(pl.multiple_of(s * length, length), length)
            acc[0, :, tokens] = part[:rank]
            acc[1, :, tokens] = part[rank:]

    far[...] = acc[1 - side_ref[0]]
    again[...] = acc[1 - side_ref[0]]
    near[...] = acc[side_ref[0]]
    early_copy.wait()


def project_in(side, rows, proj, grads):
    seqs, length, _ = rows.shape
    early = (2, length, grads.shape[3] // 2)
    rank = proj.shape[1]
    return pl.pallas_call(
        project_in_kernel,
        in_specs=[smem(), hbm(), hbm(), hbm()],
        out_specs=[vmem()] * 4,
        out_shape=[
            jax.ShapeDtypeStruct((rank, seqs * length), jnp.float32),
            jax.ShapeDtypeStruct((rank, seqs * length), jnp.float32),
            jax.ShapeDtypeStruct((rank, seqs * length), jnp.float32),
            jax.ShapeDtypeStruct(early, grads.dtype),
        ],
        scratch_shapes=[
            pltpu.VMEM(rows.shape, rows.dtype),
            pltpu.VMEM(proj.shape, proj.dtype),
            pltpu.VMEM((2, rank, seqs * length), jnp.float32),
            pltpu.SemaphoreType.DMA((seqs,)),
            pltpu.SemaphoreType.DMA,
            pltpu.SemaphoreType.DMA,
        ],
        compiler_params=params(16),
        name="project_in",
    )(side, in_hbm(rows), in_hbm(proj), in_hbm(grads))


def project_out_kernel(side_ref, rows_hbm, proj_ref, queries_hbm, early, *refs):
    (near, far, again, packed), (rows, held, acc, sems, sem) = refs[:4], refs[4:]
    _, seqs, length, width = rows.shape
    parts = sems.shape[2]
    piece = width // parts
    copies = {}
    for s in range(seqs):
        for part in range(parts):
            if s == 0 and part < parts // 2:
                continue
            lanes = pl.ds(part * piece, piece)
            for layer in range(2):
                copies[s, part, layer] = pltpu.make_async_copy(
                    rows_hbm.at[layer, s, :, lanes],
                    rows.at[layer, s, :, lanes],
                    sems.at[layer, s, part],
                )
                copies[s, part, layer].start()
    copy = pltpu.make_async_copy(queries_hbm.at[:, side_ref[0]], held, sem)
    copy.start()
    for s in range(seqs):
        tokens = slice(s * length, (s + 1) * length)
        for part in range(parts):
            lanes = slice(part * piece, (part + 1) * piece)
            ready = s == 0 and part < parts // 2
            for layer in range(2):
                if not ready:
                    copies[s, part, layer].wait()
            for layer in range(2):
                block = early[layer, :, lanes] if ready else rows[layer, s, :, lanes]
                value = nt(proj_ref[layer, :, lanes], block)
                if part > 0:
                    value = value + acc[layer, :, tokens]
                acc[layer, :, tokens] = value
    far[...] = acc[1 - side_ref[0]]
    again[...] = acc[1 - side_ref[0]]
    near[...] = acc[side_ref[0]]
    copy.wait()
    blocks = held.shape[0] // 2
    for k in range(blocks):
        pair = [held[k].astype(jnp.float32), held[k + blocks].astype(jnp.float32)]
        packed[k] = jnp.concatenate(pair, axis=1).astype(held.dtype)


def project_out(side, rows, proj, queries, early):
    _, seqs, length, width = rows.shape
    rank = proj.shape[1]
    count = queries.shape[0]
    parts = 4 if width % 512 == 0 else 2
    return pl.pallas_call(
        project_out_kernel,
        in_specs=[smem(), hbm(), vmem(), hbm(), vmem()],
        out_specs=[vmem()] * 4,
        out_shape=[
            jax.ShapeDtypeStruct((rank, seqs * length), jnp.float32),
            jax.ShapeDtypeStruct((rank, seqs * length), jnp.float32),
            jax.ShapeDtypeStruct((rank, seqs * length), jnp.float32),
            jax.ShapeDtypeStruct((count // 2, rank, 2 * rank), queries.dtype),
        ],
        scratch_shapes=[
            pltpu.VMEM(rows.shape, rows.dtype),
            pltpu.VMEM((count, rank, rank), queries.dtype),
            pltpu.VMEM((2, rank, seqs * length), jnp.float32),
            pltpu.SemaphoreType.DMA((2, seqs, parts)),
            pltpu.SemaphoreType.DMA,
        ],
        compiler_params=params(40),
        name="project_out",
    )(side, in_hbm(rows), proj, in_hbm(queries), early)


def across(value):
    return lax.ppermute(value, "tensor", [(1, 2), (2, 1)])


def to_owner(near, far, again):
    return [
        near,
        lax.ppermute(near, "tensor", [(0, 1), (3, 2)]),
        lax.ppermute(far, "tensor", [(0, 2), (3, 1)]),
        across(again),
    ]


def total(pieces):
    value = pieces[0][...]
    for piece in pieces[1:]:
        value = value + piece[...]
    return value


def covariance(value, right):
    none = jnp.zeros_like(value)
    both = [none, value] if right else [value, none]
    return nt(value, jnp.concatenate(both, axis=0), HIGHEST)


def samples_of(x, g, sample_out):
    seqs = sample_out.shape[0]
    length = g.shape[1] // seqs
    for s in range(seqs):
        tokens = slice(s * length, (s + 1) * length)
        sample = nt(x[:, tokens], g[:, tokens], HIGHEST) / length
        sample = sample.astype(jnp.bfloat16).astype(jnp.float32)
        sample_out[s] = jnp.concatenate([sample, sample], axis=1)


def cov_in_kernel(packed_ref, *refs):
    pieces, (packed, x_out, cov_out) = refs[:-3], refs[-3:]
    packed[...] = packed_ref[...]
    x = total(pieces)
    x_out[...] = x
    cov_out[...] = covariance(x, False)


def cov_in(packed, pieces):
    rank, tokens = pieces[0].shape
    return pl.pallas_call(
        cov_in_kernel,
        in_specs=[vmem()] * (1 + len(pieces)),
        out_specs=[vmem()] * 3,
        out_shape=[
            jax.ShapeDtypeStruct(packed.shape, packed.dtype),
            jax.ShapeDtypeStruct((rank, tokens), jnp.float32),
            jax.ShapeDtypeStruct((rank, 2 * rank), jnp.float32),
        ],
        compiler_params=params(16),
        name="cov_in",
    )(packed, *pieces)


def cov_out_kernel(x_ref, cov_ref, *refs):
    pieces, (cov_out, sample_out) = refs[:-2], refs[-2:]
    g = total(pieces)
    cov_out[...] = cov_ref[...] + covariance(g, True)
    samples_of(x_ref[...], g, sample_out)


def cov_out(x, cov, pieces, seqs):
    rank = x.shape[0]
    return pl.pallas_call(
        cov_out_kernel,
        in_specs=[vmem()] * (2 + len(pieces)),
        out_specs=[vmem()] * 2,
        out_shape=[
            jax.ShapeDtypeStruct((rank, 2 * rank), jnp.float32),
            jax.ShapeDtypeStruct((seqs, rank, 2 * rank), jnp.float32),
        ],
        compiler_params=params(16),
        name="cov_out",
    )(x, cov, *pieces)


def scales(steps, spread):
    r = (spread - 1.0) / (spread + 1.0)
    out = []
    for _ in range(steps):
        out.append(2.0 / (2.0 - r * r))
        r = r * r / (2.0 - r * r)
    return out


def halves(value):
    high = value.astype(jnp.bfloat16)
    return high, (value - high.astype(jnp.float32)).astype(jnp.bfloat16)


def stacked(value):
    once = jnp.concatenate(halves(value), axis=1)
    return jnp.concatenate([once, once], axis=0)


def product(left, right):
    lanes = right.shape[1]
    both = nn(jnp.concatenate(halves(left), axis=1), stacked(right))
    return both[:, :lanes] + both[:, lanes:]


def damped_inverses(pair):
    size, both = pair.shape
    left = lax.broadcasted_iota(jnp.int32, pair.shape, 1) < size
    whole = jnp.concatenate([jnp.where(left, pair, 0.0), jnp.where(left, 0.0, pair)], axis=0)
    rows = lax.broadcasted_iota(jnp.int32, whole.shape, 0)
    cols = lax.broadcasted_iota(jnp.int32, whole.shape, 1)
    diagonal = rows == cols
    on_diagonal = jnp.where(diagonal, whole, 0.0)
    unit = jnp.where(
        rows < size, jnp.sum(on_diagonal[:size]) / size, jnp.sum(on_diagonal[size:]) / size
    )
    eye = jnp.where(diagonal, 1.0, 0.0)
    matrix = whole / unit + 0.1 * eye
    low, high = 0.1, size + 0.1
    start = 2.0 / (low + high)
    steps = scales(7, high / low)
    y = matrix * start
    x = (2.0 * start * steps[0]) * eye - (start * steps[0]) * y
    y = steps[0] * (2.0 * y - product(y, y))
    for scale in steps[1:-1]:
        turn = product(jnp.concatenate([x, y], axis=0), y)
        x = scale * (2.0 * x - turn[:both])
        y = scale * (2.0 * y - turn[both:])
    x = steps[-1] * (2.0 * x - product(x, y))
    x = x + product(x, eye - product(matrix, x))
    x = x + product(x, eye - nn(matrix, x, HIGHEST))
    return x / unit


def score_kernel(tokens, place_ref, own_ref, other_ref, sample_ref, *refs):
    pieces, (out, held, half) = refs[:-3], refs[-3:]
    parts = held.shape[0]
    for k, piece in enumerate(pieces):
        held[place_ref[0] ^ k] = piece[...]
    pair = (own_ref[...] + other_ref[...]) / tokens
    size, both = pair.shape
    inverses = damped_inverses(pair)
    samples = [sample_ref[s] for s in range(sample_ref.shape[0])]
    seqs = len(samples)
    blocks = held.shape[1]
    pairs = parts * blocks
    first = jnp.concatenate(halves(inverses[:size, :size]), axis=0)
    none = jnp.zeros_like(first)
    first = jnp.concatenate(
        [jnp.concatenate([first, none], axis=1), jnp.concatenate([none, first], axis=1)], axis=0
    )
    right = inverses[size:]
    second = stacked(jnp.concatenate([pltpu.roll(right, size, 1), right], axis=0))
    for part in range(parts // 2):
        for block in range(0, blocks, 2):
            rows = jnp.concatenate(
                [
                    held[part, block],
                    held[part + parts // 2, block],
                    held[part, block + 1],
                    held[part + parts // 2, block + 1],
                ],
                axis=0,
            )
            result = nt(first, rows)
            for k in range(2):
                two = result[both * k : both * (k + 1)]
                high, middle = halves(two[:size] + two[size:])
                pair = (2 * part + k) * blocks + block
                lanes = slice(pair * both, (pair + 2) * both)
                half[0, :, lanes] = high
                half[1, :, lanes] = middle
    lines = [[] for _ in range(seqs)]
    for pair in range(pairs):
        lanes = slice(pair * both, (pair + 1) * both)
        rows = jnp.concatenate([half[0, :, lanes], half[1, :, lanes]], axis=1)
        result = nn(rows, second)
        result = (result[:, :both] + result[:, both:]).astype(jnp.bfloat16).astype(jnp.float32)
        for s in range(seqs):
            lines[s].append(jnp.sum(result * samples[s], axis=0, keepdims=True))
    lines = jnp.concatenate([line for part in lines for line in part], axis=0)
    shape = (8, both)
    ends = jnp.where(
        (lax.broadcasted_iota(jnp.int32, shape, 1) < size)
        == (lax.broadcasted_iota(jnp.int32, shape, 0) == 0),
        1.0,
        0.0,
    )
    result = nt(ends, lines, HIGHEST)
    for s in range(seqs):
        for k in range(2):
            out[s : s + 1, k * pairs : (k + 1) * pairs] = result[
                k : k + 1, s * pairs : (s + 1) * pairs
            ]


def score(place, own, other, sample, pieces, tokens):
    blocks, rank, both = pieces[0].shape
    parts = len(pieces)
    pairs = parts * blocks
    seqs = sample.shape[0]
    return pl.pallas_call(
        functools.partial(score_kernel, tokens),
        in_specs=[smem()] + [vmem()] * (3 + len(pieces)),
        out_specs=vmem(),
        out_shape=jax.ShapeDtypeStruct((seqs, 2 * pairs), jnp.float32),
        scratch_shapes=[
            pltpu.VMEM((parts, blocks, rank, both), pieces[0].dtype),
            pltpu.VMEM((2, rank, pairs * both), jnp.bfloat16),
        ],
        compiler_params=params(16),
        name="score",
    )(place, own, other, sample, *pieces)


def swap(value, axis, bit):
    return lax.ppermute(value, axis, [(i, i ^ bit) for i in range(lax.axis_size(axis))])


def owners_swap(value, bits):
    parts = lax.axis_size("dp")
    places = [(t * parts + k, t * parts + (k ^ bits)) for t in (1, 2) for k in range(parts)]
    return lax.ppermute(value, ("tensor", "dp"), places)


def local_owned(acts, grads, proj_in, proj_out, queries):
    seqs, length, _ = acts.shape
    parts = lax.axis_size("dp")
    tokens = seqs * length * parts
    column = lax.axis_index("tensor").astype(jnp.int32)
    side = (column >= 2).astype(jnp.int32).reshape(1)
    place = lax.axis_index("dp").astype(jnp.int32).reshape(1)
    x_near, x_far, x_again, early = project_in(side, acts, proj_in, grads)
    x_pieces = to_owner(x_near, x_far, x_again)
    near, far, again, packed = project_out(side, grads, proj_out, queries, early)
    pieces = to_owner(near, far, again)
    packed, x, cov = cov_in(packed, x_pieces)
    query_pieces = [packed] + [owners_swap(packed, bits) for bits in range(1, parts)]
    cov, sample = cov_out(x, cov, pieces, seqs)
    other = jnp.zeros_like(cov)
    bit = 1
    while bit < parts:
        cov = cov if bit == 1 else cov + other
        other = swap(cov, "dp", bit)
        bit *= 2
    scores = score(place, cov, other, sample, query_pieces, tokens)
    owner = (column == 1) | (column == 2)
    pieces = [
        across(scores),
        lax.ppermute(scores, "tensor", [(1, 0), (2, 3)]),
        lax.ppermute(scores, "tensor", [(2, 0), (1, 3)]),
    ]
    return jnp.where(owner, scores, 0.0) + pieces[0] + pieces[1] + pieces[2]


def damp(matrix):
    size = matrix.shape[0]
    shift_by = 0.1 * jnp.trace(matrix) / size
    return matrix + shift_by * jnp.eye(size, dtype=matrix.dtype)


def chol_apply(factor, rhs):
    lower_sol = lax.linalg.triangular_solve(factor, rhs, left_side=True, lower=True)
    return lax.linalg.triangular_solve(
        factor, lower_sol, left_side=True, lower=True, transpose_a=True
    )


def precondition(query, left, right_side):
    count, rank = (query.shape[0], query.shape[1])
    left_fac = jnp.linalg.cholesky(left)
    right_fac = jnp.linalg.cholesky(right_side)
    stacked = jnp.transpose(query, (1, 0, 2)).reshape(rank, count * rank)
    middle = chol_apply(left_fac, stacked).reshape(rank, count, rank)
    turned = jnp.transpose(middle, (2, 1, 0)).reshape(rank, count * rank)
    result = chol_apply(right_fac, turned).reshape(rank, count, rank)
    return jnp.transpose(result, (1, 2, 0))


def diagonal_blocks(whole, rank):
    return jnp.stack([whole[:, 0:rank, 0:rank], whole[:, rank : 2 * rank, rank : 2 * rank]], axis=1)


def local_general(acts, grads, proj_in, proj_out, queries):
    seq_count, length, width_loc = acts.shape
    rank = proj_in.shape[1]
    hidden_loc = grads.shape[3]
    flat = acts.reshape(-1, width_loc)
    xpart = nt(flat, proj_in.reshape(2 * rank, width_loc))
    gpart = jnp.concatenate(
        [nt(grads[layer].reshape(-1, hidden_loc), proj_out[layer]) for layer in range(2)], axis=1
    )
    count = seq_count * length * lax.axis_size("dp")
    xin, gout = lax.psum((xpart, gpart), "tensor")
    in_cov, out_cov = lax.psum((tn(xin, xin, HIGHEST), tn(gout, gout, HIGHEST)), "dp")
    whole = (
        jnp.einsum(
            "sto,sti->soi",
            gout.reshape(seq_count, length, 2 * rank),
            xin.reshape(seq_count, length, 2 * rank),
            precision=HIGHEST,
        )
        / length
    )
    samples = diagonal_blocks(whole, rank)
    in_cov = in_cov / count
    out_cov = out_cov / count
    precond = []
    for layer in range(2):
        low = layer * rank
        damped_in = damp(in_cov[low : low + rank, low : low + rank])
        damped_out = damp(out_cov[low : low + rank, low : low + rank])
        precond.append(precondition(queries[:, layer].astype(jnp.float32), damped_out, damped_in))
    query_count = queries.shape[0]
    query_b = jnp.stack(precond, axis=1).astype(jnp.bfloat16).reshape(query_count, -1)
    sample_b = samples.astype(jnp.bfloat16).reshape(seq_count, -1)
    return nt(sample_b, lax.all_gather(query_b, "dp", axis=0, tiled=True))


def local(acts, grads, proj_in, proj_out, queries):
    parts = lax.axis_size("dp")
    even = parts > 1 and parts & (parts - 1) == 0
    if lax.axis_size("tensor") == 4 and even and queries.shape[0] % 4 == 0:
        return local_owned(acts, grads, proj_in, proj_out, queries)
    return local_general(acts, grads, proj_in, proj_out, queries)


def solution(mesh):
    placed = (
        P(("groups", "dp"), None, "tensor"),
        P(None, ("groups", "dp"), None, "tensor"),
        P(None, None, "tensor"),
        P(None, None, "tensor"),
        P("dp", None, None, None),
    )
    return jax.shard_map(
        local, mesh=mesh, in_specs=placed, out_specs=P(("groups", "dp"), None), check_vma=False
    )
```

```python
import functools

import jax
import jax.numpy as jnp
from jax import lax
from jax.experimental import pallas as pl
from jax.experimental.pallas import tpu as pltpu
from jax.sharding import PartitionSpec as P

HIGHEST = lax.Precision.HIGHEST
MIB = 1024 * 1024


def nt(a, b, precision=None):
    return lax.dot_general(
        a, b, (((1,), (1,)), ((), ())), precision=precision, preferred_element_type=jnp.float32
    )


def tn(a, b, precision=None):
    return lax.dot_general(
        a, b, (((0,), (0,)), ((), ())), precision=precision, preferred_element_type=jnp.float32
    )


def nn(a, b, precision=None):
    return jnp.dot(a, b, precision=precision, preferred_element_type=jnp.float32)


def vmem():
    return pl.BlockSpec(memory_space=pltpu.VMEM)


def smem():
    return pl.BlockSpec(memory_space=pltpu.SMEM)


def hbm():
    return pl.BlockSpec(memory_space=pl.ANY)


def in_hbm(value):
    return pltpu.with_memory_space_constraint(value, pltpu.HBM)


def params(mib):
    return pltpu.CompilerParams(vmem_limit_bytes=mib * MIB)


def project_in_kernel(
    side_ref, rows_hbm, proj_hbm, grads_hbm, near, far, again, early, rows, proj, acc, sems, proj_sem, early_sem
):
    seqs, length, width = rows.shape
    rank = proj.shape[1]
    proj_copy = pltpu.make_async_copy(proj_hbm, proj, proj_sem)
    proj_copy.start()

    def copy(s):
        return pltpu.make_async_copy(rows_hbm.at[s], rows.at[s], sems.at[s])

    for s in range(seqs):
        copy(s).start()
    early_copy = pltpu.make_async_copy(
        grads_hbm.at[:, 0, :, pl.ds(0, early.shape[2])], early, early_sem
    )
    early_copy.start()
    proj_copy.wait()

    group = 2 - seqs % 2

    @pl.loop(0, seqs // group)
    def _(step):
        for k in range(group):
            copy(step * group + k).wait()
        for k in range(group):
            s = step * group + k
            part = nt(proj[...].reshape(2 * rank, width), rows[s])
            tokens = pl.ds(pl.multiple_of(s * length, length), length)
            acc[0, :, tokens] = part[:rank]
            acc[1, :, tokens] = part[rank:]

    far[...] = acc[1 - side_ref[0]]
    again[...] = acc[1 - side_ref[0]]
    near[...] = acc[side_ref[0]]
    early_copy.wait()


def project_in(side, rows, proj, grads):
    seqs, length, _ = rows.shape
    early = (2, length, grads.shape[3] // 2)
    rank = proj.shape[1]
    return pl.pallas_call(
        project_in_kernel,
        in_specs=[smem(), hbm(), hbm(), hbm()],
        out_specs=[vmem()] * 4,
        out_shape=[
            jax.ShapeDtypeStruct((rank, seqs * length), jnp.float32),
            jax.ShapeDtypeStruct((rank, seqs * length), jnp.float32),
            jax.ShapeDtypeStruct((rank, seqs * length), jnp.float32),
            jax.ShapeDtypeStruct(early, grads.dtype),
        ],
        scratch_shapes=[
            pltpu.VMEM(rows.shape, rows.dtype),
            pltpu.VMEM(proj.shape, proj.dtype),
            pltpu.VMEM((2, rank, seqs * length), jnp.float32),
            pltpu.SemaphoreType.DMA((seqs,)),
            pltpu.SemaphoreType.DMA,
            pltpu.SemaphoreType.DMA,
        ],
        compiler_params=params(16),
        name="project_in",
    )(side, in_hbm(rows), in_hbm(proj), in_hbm(grads))


def project_out_kernel(side_ref, rows_hbm, proj_ref, queries_hbm, early, *refs):
    (near, far, again, packed), (rows, held, acc, sems, sem) = refs[:4], refs[4:]
    _, seqs, length, width = rows.shape
    parts = sems.shape[2]
    piece = width // parts
    copies = {}
    for s in range(seqs):
        for part in range(parts):
            if s == 0 and part < parts // 2:
                continue
            lanes = pl.ds(part * piece, piece)
            for layer in range(2):
                copies[s, part, layer] = pltpu.make_async_copy(
                    rows_hbm.at[layer, s, :, lanes],
                    rows.at[layer, s, :, lanes],
                    sems.at[layer, s, part],
                )
                copies[s, part, layer].start()
    copy = pltpu.make_async_copy(queries_hbm.at[:, side_ref[0]], held, sem)
    copy.start()
    for s in range(seqs):
        tokens = slice(s * length, (s + 1) * length)
        for part in range(parts):
            lanes = slice(part * piece, (part + 1) * piece)
            ready = s == 0 and part < parts // 2
            for layer in range(2):
                if not ready:
                    copies[s, part, layer].wait()
            for layer in range(2):
                block = early[layer, :, lanes] if ready else rows[layer, s, :, lanes]
                value = nt(proj_ref[layer, :, lanes], block)
                if part > 0:
                    value = value + acc[layer, :, tokens]
                acc[layer, :, tokens] = value
    far[...] = acc[1 - side_ref[0]]
    again[...] = acc[1 - side_ref[0]]
    near[...] = acc[side_ref[0]]
    copy.wait()
    blocks = held.shape[0] // 2
    for k in range(blocks):
        pair = [held[k].astype(jnp.float32), held[k + blocks].astype(jnp.float32)]
        packed[k] = jnp.concatenate(pair, axis=1).astype(held.dtype)


def project_out(side, rows, proj, queries, early):
    _, seqs, length, width = rows.shape
    rank = proj.shape[1]
    count = queries.shape[0]
    parts = 4 if width % 512 == 0 else 2
    return pl.pallas_call(
        project_out_kernel,
        in_specs=[smem(), hbm(), vmem(), hbm(), vmem()],
        out_specs=[vmem()] * 4,
        out_shape=[
            jax.ShapeDtypeStruct((rank, seqs * length), jnp.float32),
            jax.ShapeDtypeStruct((rank, seqs * length), jnp.float32),
            jax.ShapeDtypeStruct((rank, seqs * length), jnp.float32),
            jax.ShapeDtypeStruct((count // 2, rank, 2 * rank), queries.dtype),
        ],
        scratch_shapes=[
            pltpu.VMEM(rows.shape, rows.dtype),
            pltpu.VMEM((count, rank, rank), queries.dtype),
            pltpu.VMEM((2, rank, seqs * length), jnp.float32),
            pltpu.SemaphoreType.DMA((2, seqs, parts)),
            pltpu.SemaphoreType.DMA,
        ],
        compiler_params=params(40),
        name="project_out",
    )(side, in_hbm(rows), proj, in_hbm(queries), early)


def across(value):
    return lax.ppermute(value, "tensor", [(1, 2), (2, 1)])


def to_owner(near, far, again):
    return [
        near,
        lax.ppermute(near, "tensor", [(0, 1), (3, 2)]),
        lax.ppermute(far, "tensor", [(0, 2), (3, 1)]),
        across(again),
    ]


def total(pieces):
    value = pieces[0][...]
    for piece in pieces[1:]:
        value = value + piece[...]
    return value


def covariance(value, right):
    none = jnp.zeros_like(value)
    both = [none, value] if right else [value, none]
    return nt(value, jnp.concatenate(both, axis=0), HIGHEST)


def samples_of(x, g, sample_out):
    seqs = sample_out.shape[0]
    length = g.shape[1] // seqs
    for s in range(seqs):
        tokens = slice(s * length, (s + 1) * length)
        sample = nt(x[:, tokens], g[:, tokens], HIGHEST) / length
        sample = sample.astype(jnp.bfloat16).astype(jnp.float32)
        sample_out[s] = jnp.concatenate([sample, sample], axis=1)


def cov_in_kernel(packed_ref, *refs):
    pieces, (packed, x_out, cov_out) = refs[:-3], refs[-3:]
    packed[...] = packed_ref[...]
    x = total(pieces)
    x_out[...] = x
    cov_out[...] = covariance(x, False)


def cov_in(packed, pieces):
    rank, tokens = pieces[0].shape
    return pl.pallas_call(
        cov_in_kernel,
        in_specs=[vmem()] * (1 + len(pieces)),
        out_specs=[vmem()] * 3,
        out_shape=[
            jax.ShapeDtypeStruct(packed.shape, packed.dtype),
            jax.ShapeDtypeStruct((rank, tokens), jnp.float32),
            jax.ShapeDtypeStruct((rank, 2 * rank), jnp.float32),
        ],
        compiler_params=params(16),
        name="cov_in",
    )(packed, *pieces)


def cov_out_kernel(x_ref, cov_ref, *refs):
    pieces, (cov_out, sample_out) = refs[:-2], refs[-2:]
    g = total(pieces)
    cov_out[...] = cov_ref[...] + covariance(g, True)
    samples_of(x_ref[...], g, sample_out)


def cov_out(x, cov, pieces, seqs):
    rank = x.shape[0]
    return pl.pallas_call(
        cov_out_kernel,
        in_specs=[vmem()] * (2 + len(pieces)),
        out_specs=[vmem()] * 2,
        out_shape=[
            jax.ShapeDtypeStruct((rank, 2 * rank), jnp.float32),
            jax.ShapeDtypeStruct((seqs, rank, 2 * rank), jnp.float32),
        ],
        compiler_params=params(16),
        name="cov_out",
    )(x, cov, *pieces)


def scales(steps, spread):
    r = (spread - 1.0) / (spread + 1.0)
    out = []
    for _ in range(steps):
        out.append(2.0 / (2.0 - r * r))
        r = r * r / (2.0 - r * r)
    return out


def halves(value):
    high = value.astype(jnp.bfloat16)
    return high, (value - high.astype(jnp.float32)).astype(jnp.bfloat16)


def stacked(value):
    once = jnp.concatenate(halves(value), axis=1)
    return jnp.concatenate([once, once], axis=0)


def product(left, right):
    lanes = right.shape[1]
    both = nn(jnp.concatenate(halves(left), axis=1), stacked(right))
    return both[:, :lanes] + both[:, lanes:]


def damped_inverses(pair):
    size, both = pair.shape
    left = lax.broadcasted_iota(jnp.int32, pair.shape, 1) < size
    whole = jnp.concatenate([jnp.where(left, pair, 0.0), jnp.where(left, 0.0, pair)], axis=0)
    rows = lax.broadcasted_iota(jnp.int32, whole.shape, 0)
    cols = lax.broadcasted_iota(jnp.int32, whole.shape, 1)
    diagonal = rows == cols
    on_diagonal = jnp.where(diagonal, whole, 0.0)
    unit = jnp.where(
        rows < size, jnp.sum(on_diagonal[:size]) / size, jnp.sum(on_diagonal[size:]) / size
    )
    eye = jnp.where(diagonal, 1.0, 0.0)
    matrix = whole / unit + 0.1 * eye
    low, high = 0.1, size + 0.1
    start = 2.0 / (low + high)
    steps = scales(7, high / low)
    y = matrix * start
    x = (2.0 * start * steps[0]) * eye - (start * steps[0]) * y
    y = steps[0] * (2.0 * y - product(y, y))
    for scale in steps[1:-1]:
        turn = product(jnp.concatenate([x, y], axis=0), y)
        x = scale * (2.0 * x - turn[:both])
        y = scale * (2.0 * y - turn[both:])
    x = steps[-1] * (2.0 * x - product(x, y))
    x = x + product(x, eye - product(matrix, x))
    x = x + product(x, eye - nn(matrix, x, HIGHEST))
    return x / unit


def score_kernel(tokens, place_ref, own_ref, other_ref, sample_ref, *refs):
    pieces, (out, held, half) = refs[:-3], refs[-3:]
    parts = held.shape[0]
    for k, piece in enumerate(pieces):
        held[place_ref[0] ^ k] = piece[...]
    pair = (own_ref[...] + other_ref[...]) / tokens
    size, both = pair.shape
    inverses = damped_inverses(pair)
    samples = [sample_ref[s] for s in range(sample_ref.shape[0])]
    seqs = len(samples)
    blocks = held.shape[1]
    pairs = parts * blocks
    first = jnp.concatenate(halves(inverses[:size, :size]), axis=0)
    none = jnp.zeros_like(first)
    first = jnp.concatenate(
        [jnp.concatenate([first, none], axis=1), jnp.concatenate([none, first], axis=1)], axis=0
    )
    right = inverses[size:]
    second = stacked(jnp.concatenate([pltpu.roll(right, size, 1), right], axis=0))
    for part in range(parts // 2):
        for block in range(0, blocks, 2):
            rows = jnp.concatenate(
                [
                    held[part, block],
                    held[part + parts // 2, block],
                    held[part, block + 1],
                    held[part + parts // 2, block + 1],
                ],
                axis=0,
            )
            result = nt(first, rows)
            for k in range(2):
                two = result[both * k : both * (k + 1)]
                high, middle = halves(two[:size] + two[size:])
                pair = (2 * part + k) * blocks + block
                lanes = slice(pair * both, (pair + 2) * both)
                half[0, :, lanes] = high
                half[1, :, lanes] = middle
    lines = [[] for _ in range(seqs)]
    for pair in range(pairs):
        lanes = slice(pair * both, (pair + 1) * both)
        rows = jnp.concatenate([half[0, :, lanes], half[1, :, lanes]], axis=1)
        result = nn(rows, second)
        result = (result[:, :both] + result[:, both:]).astype(jnp.bfloat16).astype(jnp.float32)
        for s in range(seqs):
            lines[s].append(jnp.sum(result * samples[s], axis=0, keepdims=True))
    lines = jnp.concatenate([line for part in lines for line in part], axis=0)
    shape = (8, both)
    ends = jnp.where(
        (lax.broadcasted_iota(jnp.int32, shape, 1) < size)
        == (lax.broadcasted_iota(jnp.int32, shape, 0) == 0),
        1.0,
        0.0,
    )
    result = nt(ends, lines, HIGHEST)
    for s in range(seqs):
        for k in range(2):
            out[s : s + 1, k * pairs : (k + 1) * pairs] = result[
                k : k + 1, s * pairs : (s + 1) * pairs
            ]


def score(place, own, other, sample, pieces, tokens):
    blocks, rank, both = pieces[0].shape
    parts = len(pieces)
    pairs = parts * blocks
    seqs = sample.shape[0]
    return pl.pallas_call(
        functools.partial(score_kernel, tokens),
        in_specs=[smem()] + [vmem()] * (3 + len(pieces)),
        out_specs=vmem(),
        out_shape=jax.ShapeDtypeStruct((seqs, 2 * pairs), jnp.float32),
        scratch_shapes=[
            pltpu.VMEM((parts, blocks, rank, both), pieces[0].dtype),
            pltpu.VMEM((2, rank, pairs * both), jnp.bfloat16),
        ],
        compiler_params=params(16),
        name="score",
    )(place, own, other, sample, *pieces)


def swap(value, axis, bit):
    return lax.ppermute(value, axis, [(i, i ^ bit) for i in range(lax.axis_size(axis))])


def shift(value, axis, by):
    size = lax.axis_size(axis)
    return lax.ppermute(value, axis, [(i, (i + by) % size) for i in range(size)])


def owners_swap(value, bits):
    parts = lax.axis_size("dp")
    places = [(t * parts + k, t * parts + (k ^ bits)) for t in (1, 2) for k in range(parts)]
    return lax.ppermute(value, ("tensor", "dp"), places)


def local_owned(acts, grads, proj_in, proj_out, queries):
    seqs, length, _ = acts.shape
    parts = lax.axis_size("dp")
    tokens = seqs * length * parts
    column = lax.axis_index("tensor").astype(jnp.int32)
    side = (column >= 2).astype(jnp.int32).reshape(1)
    place = lax.axis_index("dp").astype(jnp.int32).reshape(1)
    x_near, x_far, x_again, early = project_in(side, acts, proj_in, grads)
    x_pieces = to_owner(x_near, x_far, x_again)
    near, far, again, packed = project_out(side, grads, proj_out, queries, early)
    pieces = to_owner(near, far, again)
    packed, x, cov = cov_in(packed, x_pieces)
    query_pieces = [packed] + [owners_swap(packed, bits) for bits in range(1, parts)]
    cov, sample = cov_out(x, cov, pieces, seqs)
    other = jnp.zeros_like(cov)
    bit = 1
    while bit < parts:
        cov = cov if bit == 1 else cov + other
        other = swap(cov, "dp", bit)
        bit *= 2
    scores = score(place, cov, other, sample, query_pieces, tokens)
    above = shift(scores, "tensor", -1)
    opposite = shift(scores, "tensor", 2)
    below = shift(scores, "tensor", 1)
    owner = (column == 1) | (column == 2)
    return jnp.where(owner, scores, opposite) + jnp.where(column >= 2, below, above)


def damp(matrix):
    size = matrix.shape[0]
    shift_by = 0.1 * jnp.trace(matrix) / size
    return matrix + shift_by * jnp.eye(size, dtype=matrix.dtype)


def chol_apply(factor, rhs):
    lower_sol = lax.linalg.triangular_solve(factor, rhs, left_side=True, lower=True)
    return lax.linalg.triangular_solve(
        factor, lower_sol, left_side=True, lower=True, transpose_a=True
    )


def precondition(query, left, right_side):
    count, rank = (query.shape[0], query.shape[1])
    left_fac = jnp.linalg.cholesky(left)
    right_fac = jnp.linalg.cholesky(right_side)
    stacked = jnp.transpose(query, (1, 0, 2)).reshape(rank, count * rank)
    middle = chol_apply(left_fac, stacked).reshape(rank, count, rank)
    turned = jnp.transpose(middle, (2, 1, 0)).reshape(rank, count * rank)
    result = chol_apply(right_fac, turned).reshape(rank, count, rank)
    return jnp.transpose(result, (1, 2, 0))


def diagonal_blocks(whole, rank):
    return jnp.stack([whole[:, 0:rank, 0:rank], whole[:, rank : 2 * rank, rank : 2 * rank]], axis=1)


def local_general(acts, grads, proj_in, proj_out, queries):
    seq_count, length, width_loc = acts.shape
    rank = proj_in.shape[1]
    hidden_loc = grads.shape[3]
    flat = acts.reshape(-1, width_loc)
    xpart = nt(flat, proj_in.reshape(2 * rank, width_loc))
    gpart = jnp.concatenate(
        [nt(grads[layer].reshape(-1, hidden_loc), proj_out[layer]) for layer in range(2)], axis=1
    )
    count = seq_count * length * lax.axis_size("dp")
    xin, gout = lax.psum((xpart, gpart), "tensor")
    in_cov, out_cov = lax.psum((tn(xin, xin, HIGHEST), tn(gout, gout, HIGHEST)), "dp")
    whole = (
        jnp.einsum(
            "sto,sti->soi",
            gout.reshape(seq_count, length, 2 * rank),
            xin.reshape(seq_count, length, 2 * rank),
            precision=HIGHEST,
        )
        / length
    )
    samples = diagonal_blocks(whole, rank)
    in_cov = in_cov / count
    out_cov = out_cov / count
    precond = []
    for layer in range(2):
        low = layer * rank
        damped_in = damp(in_cov[low : low + rank, low : low + rank])
        damped_out = damp(out_cov[low : low + rank, low : low + rank])
        precond.append(precondition(queries[:, layer].astype(jnp.float32), damped_out, damped_in))
    query_count = queries.shape[0]
    query_b = jnp.stack(precond, axis=1).astype(jnp.bfloat16).reshape(query_count, -1)
    sample_b = samples.astype(jnp.bfloat16).reshape(seq_count, -1)
    return nt(sample_b, lax.all_gather(query_b, "dp", axis=0, tiled=True))


def local(acts, grads, proj_in, proj_out, queries):
    parts = lax.axis_size("dp")
    even = parts > 1 and parts & (parts - 1) == 0
    if lax.axis_size("tensor") == 4 and even and queries.shape[0] % 4 == 0:
        return local_owned(acts, grads, proj_in, proj_out, queries)
    return local_general(acts, grads, proj_in, proj_out, queries)


def solution(mesh):
    placed = (
        P(("groups", "dp"), None, "tensor"),
        P(None, ("groups", "dp"), None, "tensor"),
        P(None, None, "tensor"),
        P(None, None, "tensor"),
        P("dp", None, None, None),
    )
    return jax.shard_map(
        local, mesh=mesh, in_specs=placed, out_specs=P(("groups", "dp"), None), check_vma=False
    )
```

```python
import functools

import jax
import jax.numpy as jnp
from jax import lax
from jax.experimental import pallas as pl
from jax.experimental.pallas import tpu as pltpu
from jax.sharding import PartitionSpec as P

HIGHEST = lax.Precision.HIGHEST
MIB = 1024 * 1024


def nt(a, b, precision=None):
    return lax.dot_general(
        a, b, (((1,), (1,)), ((), ())), precision=precision, preferred_element_type=jnp.float32
    )


def tn(a, b, precision=None):
    return lax.dot_general(
        a, b, (((0,), (0,)), ((), ())), precision=precision, preferred_element_type=jnp.float32
    )


def nn(a, b, precision=None):
    return jnp.dot(a, b, precision=precision, preferred_element_type=jnp.float32)


def vmem():
    return pl.BlockSpec(memory_space=pltpu.VMEM)


def smem():
    return pl.BlockSpec(memory_space=pltpu.SMEM)


def hbm():
    return pl.BlockSpec(memory_space=pl.ANY)


def in_hbm(value):
    return pltpu.with_memory_space_constraint(value, pltpu.HBM)


def params(mib):
    return pltpu.CompilerParams(vmem_limit_bytes=mib * MIB)


def project_in_kernel(
    side_ref, rows_hbm, proj_hbm, grads_hbm, near, far, again, early, rows, proj, acc, sems, proj_sem, early_sem
):
    seqs, length, width = rows.shape
    rank = proj.shape[1]
    proj_copy = pltpu.make_async_copy(proj_hbm, proj, proj_sem)
    proj_copy.start()

    def copy(s):
        return pltpu.make_async_copy(rows_hbm.at[s], rows.at[s], sems.at[s])

    for s in range(seqs):
        copy(s).start()
    early_copy = pltpu.make_async_copy(
        grads_hbm.at[:, 0, :, pl.ds(0, early.shape[2])], early, early_sem
    )
    early_copy.start()
    proj_copy.wait()

    group = 2 - seqs % 2

    @pl.loop(0, seqs // group)
    def _(step):
        for k in range(group):
            copy(step * group + k).wait()
        for k in range(group):
            s = step * group + k
            part = nt(proj[...].reshape(2 * rank, width), rows[s])
            tokens = pl.ds(pl.multiple_of(s * length, length), length)
            acc[0, :, tokens] = part[:rank]
            acc[1, :, tokens] = part[rank:]

    far[...] = acc[1 - side_ref[0]]
    again[...] = acc[1 - side_ref[0]]
    near[...] = acc[side_ref[0]]
    early_copy.wait()


def project_in(side, rows, proj, grads):
    seqs, length, _ = rows.shape
    early = (2, length, grads.shape[3] // 2)
    rank = proj.shape[1]
    return pl.pallas_call(
        project_in_kernel,
        in_specs=[smem(), hbm(), hbm(), hbm()],
        out_specs=[vmem()] * 4,
        out_shape=[
            jax.ShapeDtypeStruct((rank, seqs * length), jnp.float32),
            jax.ShapeDtypeStruct((rank, seqs * length), jnp.float32),
            jax.ShapeDtypeStruct((rank, seqs * length), jnp.float32),
            jax.ShapeDtypeStruct(early, grads.dtype),
        ],
        scratch_shapes=[
            pltpu.VMEM(rows.shape, rows.dtype),
            pltpu.VMEM(proj.shape, proj.dtype),
            pltpu.VMEM((2, rank, seqs * length), jnp.float32),
            pltpu.SemaphoreType.DMA((seqs,)),
            pltpu.SemaphoreType.DMA,
            pltpu.SemaphoreType.DMA,
        ],
        compiler_params=params(16),
        name="project_in",
    )(side, in_hbm(rows), in_hbm(proj), in_hbm(grads))


def project_out_kernel(side_ref, rows_hbm, proj_ref, queries_hbm, early, *refs):
    (near, far, again, packed), (rows, held, acc, sems, sem) = refs[:4], refs[4:]
    _, seqs, length, width = rows.shape
    parts = sems.shape[2]
    piece = width // parts
    copies = {}
    for s in range(seqs):
        for part in range(parts):
            if s == 0 and part < parts // 2:
                continue
            lanes = pl.ds(part * piece, piece)
            for layer in range(2):
                copies[s, part, layer] = pltpu.make_async_copy(
                    rows_hbm.at[layer, s, :, lanes],
                    rows.at[layer, s, :, lanes],
                    sems.at[layer, s, part],
                )
                copies[s, part, layer].start()
    copy = pltpu.make_async_copy(queries_hbm.at[:, side_ref[0]], held, sem)
    copy.start()
    for s in range(seqs):
        tokens = slice(s * length, (s + 1) * length)
        for part in range(parts):
            lanes = slice(part * piece, (part + 1) * piece)
            ready = s == 0 and part < parts // 2
            for layer in range(2):
                if not ready:
                    copies[s, part, layer].wait()
            for layer in range(2):
                block = early[layer, :, lanes] if ready else rows[layer, s, :, lanes]
                value = nt(proj_ref[layer, :, lanes], block)
                if part > 0:
                    value = value + acc[layer, :, tokens]
                acc[layer, :, tokens] = value
    far[...] = acc[1 - side_ref[0]]
    again[...] = acc[1 - side_ref[0]]
    near[...] = acc[side_ref[0]]
    copy.wait()
    blocks = held.shape[0] // 2
    for k in range(blocks):
        pair = [held[k].astype(jnp.float32), held[k + blocks].astype(jnp.float32)]
        packed[k] = jnp.concatenate(pair, axis=1).astype(held.dtype)


def project_out(side, rows, proj, queries, early):
    _, seqs, length, width = rows.shape
    rank = proj.shape[1]
    count = queries.shape[0]
    parts = 4 if width % 512 == 0 else 2
    return pl.pallas_call(
        project_out_kernel,
        in_specs=[smem(), hbm(), vmem(), hbm(), vmem()],
        out_specs=[vmem()] * 4,
        out_shape=[
            jax.ShapeDtypeStruct((rank, seqs * length), jnp.float32),
            jax.ShapeDtypeStruct((rank, seqs * length), jnp.float32),
            jax.ShapeDtypeStruct((rank, seqs * length), jnp.float32),
            jax.ShapeDtypeStruct((count // 2, rank, 2 * rank), queries.dtype),
        ],
        scratch_shapes=[
            pltpu.VMEM(rows.shape, rows.dtype),
            pltpu.VMEM((count, rank, rank), queries.dtype),
            pltpu.VMEM((2, rank, seqs * length), jnp.float32),
            pltpu.SemaphoreType.DMA((2, seqs, parts)),
            pltpu.SemaphoreType.DMA,
        ],
        compiler_params=params(40),
        name="project_out",
    )(side, in_hbm(rows), proj, in_hbm(queries), early)


def across(value):
    return lax.ppermute(value, "tensor", [(1, 2), (2, 1)])


def to_owner(near, far, again):
    return [
        near,
        lax.ppermute(near, "tensor", [(0, 1), (3, 2)]),
        lax.ppermute(far, "tensor", [(0, 2), (3, 1)]),
        across(again),
    ]


def total(pieces):
    value = pieces[0][...]
    for piece in pieces[1:]:
        value = value + piece[...]
    return value


def covariance(value, right):
    none = jnp.zeros_like(value)
    both = [none, value] if right else [value, none]
    return nt(value, jnp.concatenate(both, axis=0), HIGHEST)


def samples_of(x, g, sample_out):
    seqs = sample_out.shape[0]
    length = g.shape[1] // seqs
    for s in range(seqs):
        tokens = slice(s * length, (s + 1) * length)
        sample = nt(x[:, tokens], g[:, tokens], HIGHEST) / length
        sample = sample.astype(jnp.bfloat16).astype(jnp.float32)
        sample_out[s] = jnp.concatenate([sample, sample], axis=1)


def cov_in_kernel(packed_ref, *refs):
    pieces, (packed, x_out, cov_out) = refs[:-3], refs[-3:]
    packed[...] = packed_ref[...]
    x = total(pieces)
    x_out[...] = x
    cov_out[...] = covariance(x, False)


def cov_in(packed, pieces):
    rank, tokens = pieces[0].shape
    return pl.pallas_call(
        cov_in_kernel,
        in_specs=[vmem()] * (1 + len(pieces)),
        out_specs=[vmem()] * 3,
        out_shape=[
            jax.ShapeDtypeStruct(packed.shape, packed.dtype),
            jax.ShapeDtypeStruct((rank, tokens), jnp.float32),
            jax.ShapeDtypeStruct((rank, 2 * rank), jnp.float32),
        ],
        compiler_params=params(16),
        name="cov_in",
    )(packed, *pieces)


def cov_out_kernel(x_ref, cov_ref, *refs):
    pieces, (cov_out, sample_out) = refs[:-2], refs[-2:]
    g = total(pieces)
    cov_out[...] = cov_ref[...] + covariance(g, True)
    samples_of(x_ref[...], g, sample_out)


def cov_out(x, cov, pieces, seqs):
    rank = x.shape[0]
    return pl.pallas_call(
        cov_out_kernel,
        in_specs=[vmem()] * (2 + len(pieces)),
        out_specs=[vmem()] * 2,
        out_shape=[
            jax.ShapeDtypeStruct((rank, 2 * rank), jnp.float32),
            jax.ShapeDtypeStruct((seqs, rank, 2 * rank), jnp.float32),
        ],
        compiler_params=params(16),
        name="cov_out",
    )(x, cov, *pieces)


def scales(steps, spread):
    r = (spread - 1.0) / (spread + 1.0)
    out = []
    for _ in range(steps):
        out.append(2.0 / (2.0 - r * r))
        r = r * r / (2.0 - r * r)
    return out


def halves(value):
    high = value.astype(jnp.bfloat16)
    return high, (value - high.astype(jnp.float32)).astype(jnp.bfloat16)


def stacked(value):
    once = jnp.concatenate(halves(value), axis=1)
    return jnp.concatenate([once, once], axis=0)


def product(left, right):
    lanes = right.shape[1]
    both = nn(jnp.concatenate(halves(left), axis=1), stacked(right))
    return both[:, :lanes] + both[:, lanes:]


def damped_inverses(pair):
    size, both = pair.shape
    left = lax.broadcasted_iota(jnp.int32, pair.shape, 1) < size
    whole = jnp.concatenate([jnp.where(left, pair, 0.0), jnp.where(left, 0.0, pair)], axis=0)
    rows = lax.broadcasted_iota(jnp.int32, whole.shape, 0)
    cols = lax.broadcasted_iota(jnp.int32, whole.shape, 1)
    diagonal = rows == cols
    on_diagonal = jnp.where(diagonal, whole, 0.0)
    unit = jnp.where(
        rows < size, jnp.sum(on_diagonal[:size]) / size, jnp.sum(on_diagonal[size:]) / size
    )
    eye = jnp.where(diagonal, 1.0, 0.0)
    matrix = whole / unit + 0.1 * eye
    low, high = 0.1, size + 0.1
    start = 2.0 / (low + high)
    steps = scales(7, high / low)
    y = matrix * start
    x = (2.0 * start * steps[0]) * eye - (start * steps[0]) * y
    y = steps[0] * (2.0 * y - product(y, y))
    for scale in steps[1:-1]:
        turn = product(jnp.concatenate([x, y], axis=0), y)
        x = scale * (2.0 * x - turn[:both])
        y = scale * (2.0 * y - turn[both:])
    x = steps[-1] * (2.0 * x - product(x, y))
    x = x + product(x, eye - product(matrix, x))
    x = x + product(x, eye - nn(matrix, x, HIGHEST))
    return x / unit


def score_kernel(tokens, place_ref, sample_ref, *refs):
    (out, held, half) = refs[-3:]
    parts = held.shape[0]
    covs, pieces = refs[:parts], refs[parts : 2 * parts]
    for k, piece in enumerate(pieces):
        held[place_ref[0] ^ k] = piece[...]
    pair = total(covs) / tokens
    size, both = pair.shape
    inverses = damped_inverses(pair)
    samples = [sample_ref[s] for s in range(sample_ref.shape[0])]
    seqs = len(samples)
    blocks = held.shape[1]
    pairs = parts * blocks
    first = jnp.concatenate(halves(inverses[:size, :size]), axis=0)
    none = jnp.zeros_like(first)
    first = jnp.concatenate(
        [jnp.concatenate([first, none], axis=1), jnp.concatenate([none, first], axis=1)], axis=0
    )
    right = inverses[size:]
    second = stacked(jnp.concatenate([pltpu.roll(right, size, 1), right], axis=0))
    for part in range(parts // 2):
        for block in range(0, blocks, 2):
            rows = jnp.concatenate(
                [
                    held[part, block],
                    held[part + parts // 2, block],
                    held[part, block + 1],
                    held[part + parts // 2, block + 1],
                ],
                axis=0,
            )
            result = nt(first, rows)
            for k in range(2):
                two = result[both * k : both * (k + 1)]
                high, middle = halves(two[:size] + two[size:])
                pair = (2 * part + k) * blocks + block
                lanes = slice(pair * both, (pair + 2) * both)
                half[0, :, lanes] = high
                half[1, :, lanes] = middle
    lines = [[] for _ in range(seqs)]
    for pair in range(pairs):
        lanes = slice(pair * both, (pair + 1) * both)
        rows = jnp.concatenate([half[0, :, lanes], half[1, :, lanes]], axis=1)
        result = nn(rows, second)
        result = (result[:, :both] + result[:, both:]).astype(jnp.bfloat16).astype(jnp.float32)
        for s in range(seqs):
            lines[s].append(jnp.sum(result * samples[s], axis=0, keepdims=True))
    lines = jnp.concatenate([line for part in lines for line in part], axis=0)
    shape = (8, both)
    ends = jnp.where(
        (lax.broadcasted_iota(jnp.int32, shape, 1) < size)
        == (lax.broadcasted_iota(jnp.int32, shape, 0) == 0),
        1.0,
        0.0,
    )
    result = nt(ends, lines, HIGHEST)
    for s in range(seqs):
        for k in range(2):
            out[s : s + 1, k * pairs : (k + 1) * pairs] = result[
                k : k + 1, s * pairs : (s + 1) * pairs
            ]


def score(place, covs, sample, pieces, tokens):
    blocks, rank, both = pieces[0].shape
    parts = len(pieces)
    pairs = parts * blocks
    seqs = sample.shape[0]
    return pl.pallas_call(
        functools.partial(score_kernel, tokens),
        in_specs=[smem(), vmem()] + [vmem()] * (len(covs) + len(pieces)),
        out_specs=vmem(),
        out_shape=jax.ShapeDtypeStruct((seqs, 2 * pairs), jnp.float32),
        scratch_shapes=[
            pltpu.VMEM((parts, blocks, rank, both), pieces[0].dtype),
            pltpu.VMEM((2, rank, pairs * both), jnp.bfloat16),
        ],
        compiler_params=params(16),
        name="score",
    )(place, sample, *covs, *pieces)


def swap(value, axis, bit):
    return lax.ppermute(value, axis, [(i, i ^ bit) for i in range(lax.axis_size(axis))])


def shift(value, axis, by):
    size = lax.axis_size(axis)
    return lax.ppermute(value, axis, [(i, (i + by) % size) for i in range(size)])


def owners_swap(value, bits):
    parts = lax.axis_size("dp")
    places = [(t * parts + k, t * parts + (k ^ bits)) for t in (1, 2) for k in range(parts)]
    return lax.ppermute(value, ("tensor", "dp"), places)


def local_owned(acts, grads, proj_in, proj_out, queries):
    seqs, length, _ = acts.shape
    parts = lax.axis_size("dp")
    tokens = seqs * length * parts
    column = lax.axis_index("tensor").astype(jnp.int32)
    side = (column >= 2).astype(jnp.int32).reshape(1)
    place = lax.axis_index("dp").astype(jnp.int32).reshape(1)
    x_near, x_far, x_again, early = project_in(side, acts, proj_in, grads)
    x_pieces = to_owner(x_near, x_far, x_again)
    near, far, again, packed = project_out(side, grads, proj_out, queries, early)
    pieces = to_owner(near, far, again)
    packed, x, cov = cov_in(packed, x_pieces)
    query_pieces = [packed] + [owners_swap(packed, bits) for bits in range(1, parts)]
    cov, sample = cov_out(x, cov, pieces, seqs)
    covs = [cov] + [swap(cov, "dp", bits) for bits in range(1, parts)]
    scores = score(place, covs, sample, query_pieces, tokens)
    owner = (column == 1) | (column == 2)
    below = shift(scores, "tensor", 1)
    above = shift(scores, "tensor", -1)
    opposite = shift(scores, "tensor", 2)
    return jnp.where(column >= 2, below, above) + jnp.where(owner, scores, opposite)


def damp(matrix):
    size = matrix.shape[0]
    shift_by = 0.1 * jnp.trace(matrix) / size
    return matrix + shift_by * jnp.eye(size, dtype=matrix.dtype)


def chol_apply(factor, rhs):
    lower_sol = lax.linalg.triangular_solve(factor, rhs, left_side=True, lower=True)
    return lax.linalg.triangular_solve(
        factor, lower_sol, left_side=True, lower=True, transpose_a=True
    )


def precondition(query, left, right_side):
    count, rank = (query.shape[0], query.shape[1])
    left_fac = jnp.linalg.cholesky(left)
    right_fac = jnp.linalg.cholesky(right_side)
    stacked = jnp.transpose(query, (1, 0, 2)).reshape(rank, count * rank)
    middle = chol_apply(left_fac, stacked).reshape(rank, count, rank)
    turned = jnp.transpose(middle, (2, 1, 0)).reshape(rank, count * rank)
    result = chol_apply(right_fac, turned).reshape(rank, count, rank)
    return jnp.transpose(result, (1, 2, 0))


def diagonal_blocks(whole, rank):
    return jnp.stack([whole[:, 0:rank, 0:rank], whole[:, rank : 2 * rank, rank : 2 * rank]], axis=1)


def local_general(acts, grads, proj_in, proj_out, queries):
    seq_count, length, width_loc = acts.shape
    rank = proj_in.shape[1]
    hidden_loc = grads.shape[3]
    flat = acts.reshape(-1, width_loc)
    xpart = nt(flat, proj_in.reshape(2 * rank, width_loc))
    gpart = jnp.concatenate(
        [nt(grads[layer].reshape(-1, hidden_loc), proj_out[layer]) for layer in range(2)], axis=1
    )
    count = seq_count * length * lax.axis_size("dp")
    xin, gout = lax.psum((xpart, gpart), "tensor")
    in_cov, out_cov = lax.psum((tn(xin, xin, HIGHEST), tn(gout, gout, HIGHEST)), "dp")
    whole = (
        jnp.einsum(
            "sto,sti->soi",
            gout.reshape(seq_count, length, 2 * rank),
            xin.reshape(seq_count, length, 2 * rank),
            precision=HIGHEST,
        )
        / length
    )
    samples = diagonal_blocks(whole, rank)
    in_cov = in_cov / count
    out_cov = out_cov / count
    precond = []
    for layer in range(2):
        low = layer * rank
        damped_in = damp(in_cov[low : low + rank, low : low + rank])
        damped_out = damp(out_cov[low : low + rank, low : low + rank])
        precond.append(precondition(queries[:, layer].astype(jnp.float32), damped_out, damped_in))
    query_count = queries.shape[0]
    query_b = jnp.stack(precond, axis=1).astype(jnp.bfloat16).reshape(query_count, -1)
    sample_b = samples.astype(jnp.bfloat16).reshape(seq_count, -1)
    return nt(sample_b, lax.all_gather(query_b, "dp", axis=0, tiled=True))


def local(acts, grads, proj_in, proj_out, queries):
    parts = lax.axis_size("dp")
    even = parts > 1 and parts & (parts - 1) == 0
    if lax.axis_size("tensor") == 4 and even and queries.shape[0] % 4 == 0:
        return local_owned(acts, grads, proj_in, proj_out, queries)
    return local_general(acts, grads, proj_in, proj_out, queries)


def solution(mesh):
    placed = (
        P(("groups", "dp"), None, "tensor"),
        P(None, ("groups", "dp"), None, "tensor"),
        P(None, None, "tensor"),
        P(None, None, "tensor"),
        P("dp", None, None, None),
    )
    return jax.shard_map(
        local, mesh=mesh, in_specs=placed, out_specs=P(("groups", "dp"), None), check_vma=False
    )
```

```python
import functools

import jax
import jax.numpy as jnp
from jax import lax
from jax.experimental import pallas as pl
from jax.experimental.pallas import tpu as pltpu
from jax.sharding import PartitionSpec as P

HIGHEST = lax.Precision.HIGHEST
MIB = 1024 * 1024


def nt(a, b, precision=None):
    return lax.dot_general(
        a, b, (((1,), (1,)), ((), ())), precision=precision, preferred_element_type=jnp.float32
    )


def tn(a, b, precision=None):
    return lax.dot_general(
        a, b, (((0,), (0,)), ((), ())), precision=precision, preferred_element_type=jnp.float32
    )


def nn(a, b, precision=None):
    return jnp.dot(a, b, precision=precision, preferred_element_type=jnp.float32)


def vmem():
    return pl.BlockSpec(memory_space=pltpu.VMEM)


def smem():
    return pl.BlockSpec(memory_space=pltpu.SMEM)


def hbm():
    return pl.BlockSpec(memory_space=pl.ANY)


def in_hbm(value):
    return pltpu.with_memory_space_constraint(value, pltpu.HBM)


def params(mib):
    return pltpu.CompilerParams(vmem_limit_bytes=mib * MIB)


def project_in_kernel(
    side_ref, rows_hbm, proj_hbm, grads_hbm, near, far, again, early, rows, proj, acc, sems, proj_sem, early_sem
):
    seqs, length, width = rows.shape
    rank = proj.shape[1]
    proj_copy = pltpu.make_async_copy(proj_hbm, proj, proj_sem)
    proj_copy.start()

    def copy(s):
        return pltpu.make_async_copy(rows_hbm.at[s], rows.at[s], sems.at[s])

    for s in range(seqs):
        copy(s).start()
    early_copy = pltpu.make_async_copy(
        grads_hbm.at[:, 0, :, pl.ds(0, early.shape[2])], early, early_sem
    )
    early_copy.start()
    proj_copy.wait()

    group = 2 - seqs % 2

    @pl.loop(0, seqs // group)
    def _(step):
        for k in range(group):
            copy(step * group + k).wait()
        for k in range(group):
            s = step * group + k
            part = nt(proj[...].reshape(2 * rank, width), rows[s])
            tokens = pl.ds(pl.multiple_of(s * length, length), length)
            acc[0, :, tokens] = part[:rank]
            acc[1, :, tokens] = part[rank:]

    far[...] = acc[1 - side_ref[0]]
    again[...] = acc[1 - side_ref[0]]
    near[...] = acc[side_ref[0]]
    early_copy.wait()


def project_in(side, rows, proj, grads):
    seqs, length, _ = rows.shape
    early = (2, length, grads.shape[3] // 2)
    rank = proj.shape[1]
    return pl.pallas_call(
        project_in_kernel,
        in_specs=[smem(), hbm(), hbm(), hbm()],
        out_specs=[vmem()] * 4,
        out_shape=[
            jax.ShapeDtypeStruct((rank, seqs * length), jnp.float32),
            jax.ShapeDtypeStruct((rank, seqs * length), jnp.float32),
            jax.ShapeDtypeStruct((rank, seqs * length), jnp.float32),
            jax.ShapeDtypeStruct(early, grads.dtype),
        ],
        scratch_shapes=[
            pltpu.VMEM(rows.shape, rows.dtype),
            pltpu.VMEM(proj.shape, proj.dtype),
            pltpu.VMEM((2, rank, seqs * length), jnp.float32),
            pltpu.SemaphoreType.DMA((seqs,)),
            pltpu.SemaphoreType.DMA,
            pltpu.SemaphoreType.DMA,
        ],
        compiler_params=params(16),
        name="project_in",
    )(side, in_hbm(rows), in_hbm(proj), in_hbm(grads))


def project_out_kernel(side_ref, rows_hbm, proj_ref, queries_hbm, early, *refs):
    (near, far, again, packed), (rows, held, acc, sems, sem) = refs[:4], refs[4:]
    _, seqs, length, width = rows.shape
    parts = sems.shape[2]
    piece = width // parts
    copies = {}
    for s in range(seqs):
        for part in range(parts):
            if s == 0 and part < parts // 2:
                continue
            lanes = pl.ds(part * piece, piece)
            for layer in range(2):
                copies[s, part, layer] = pltpu.make_async_copy(
                    rows_hbm.at[layer, s, :, lanes],
                    rows.at[layer, s, :, lanes],
                    sems.at[layer, s, part],
                )
                copies[s, part, layer].start()
    copy = pltpu.make_async_copy(queries_hbm.at[:, side_ref[0]], held, sem)
    copy.start()
    for s in range(seqs):
        tokens = slice(s * length, (s + 1) * length)
        for part in range(parts):
            lanes = slice(part * piece, (part + 1) * piece)
            ready = s == 0 and part < parts // 2
            for layer in range(2):
                if not ready:
                    copies[s, part, layer].wait()
            for layer in range(2):
                block = early[layer, :, lanes] if ready else rows[layer, s, :, lanes]
                value = nt(proj_ref[layer, :, lanes], block)
                if part > 0:
                    value = value + acc[layer, :, tokens]
                acc[layer, :, tokens] = value
    far[...] = acc[1 - side_ref[0]]
    again[...] = acc[1 - side_ref[0]]
    near[...] = acc[side_ref[0]]
    copy.wait()
    blocks = held.shape[0] // 2
    for k in range(blocks):
        pair = [held[k].astype(jnp.float32), held[k + blocks].astype(jnp.float32)]
        packed[k] = jnp.concatenate(pair, axis=1).astype(held.dtype)


def project_out(side, rows, proj, queries, early):
    _, seqs, length, width = rows.shape
    rank = proj.shape[1]
    count = queries.shape[0]
    parts = 4 if width % 512 == 0 else 2
    return pl.pallas_call(
        project_out_kernel,
        in_specs=[smem(), hbm(), vmem(), hbm(), vmem()],
        out_specs=[vmem()] * 4,
        out_shape=[
            jax.ShapeDtypeStruct((rank, seqs * length), jnp.float32),
            jax.ShapeDtypeStruct((rank, seqs * length), jnp.float32),
            jax.ShapeDtypeStruct((rank, seqs * length), jnp.float32),
            jax.ShapeDtypeStruct((count // 2, rank, 2 * rank), queries.dtype),
        ],
        scratch_shapes=[
            pltpu.VMEM(rows.shape, rows.dtype),
            pltpu.VMEM((count, rank, rank), queries.dtype),
            pltpu.VMEM((2, rank, seqs * length), jnp.float32),
            pltpu.SemaphoreType.DMA((2, seqs, parts)),
            pltpu.SemaphoreType.DMA,
        ],
        compiler_params=params(40),
        name="project_out",
    )(side, in_hbm(rows), proj, in_hbm(queries), early)


def across(value):
    return lax.ppermute(value, "tensor", [(1, 2), (2, 1)])


def to_owner(near, far, again):
    return [
        near,
        lax.ppermute(near, "tensor", [(0, 1), (3, 2)]),
        lax.ppermute(far, "tensor", [(0, 2), (3, 1)]),
        across(again),
    ]


def total(pieces):
    value = pieces[0][...]
    for piece in pieces[1:]:
        value = value + piece[...]
    return value


def covariance(value, right):
    none = jnp.zeros_like(value)
    both = [none, value] if right else [value, none]
    return nt(value, jnp.concatenate(both, axis=0), HIGHEST)


def samples_of(x, g, sample_out):
    seqs = sample_out.shape[0]
    length = g.shape[1] // seqs
    for s in range(seqs):
        tokens = slice(s * length, (s + 1) * length)
        sample = nt(x[:, tokens], g[:, tokens], HIGHEST) / length
        sample = sample.astype(jnp.bfloat16).astype(jnp.float32)
        sample_out[s] = jnp.concatenate([sample, sample], axis=1)


def cov_in_kernel(packed_ref, *refs):
    pieces, (packed, x_out, cov_out) = refs[:-3], refs[-3:]
    packed[...] = packed_ref[...]
    x = total(pieces)
    x_out[...] = x
    cov_out[...] = covariance(x, False)


def cov_in(packed, pieces):
    rank, tokens = pieces[0].shape
    return pl.pallas_call(
        cov_in_kernel,
        in_specs=[vmem()] * (1 + len(pieces)),
        out_specs=[vmem()] * 3,
        out_shape=[
            jax.ShapeDtypeStruct(packed.shape, packed.dtype),
            jax.ShapeDtypeStruct((rank, tokens), jnp.float32),
            jax.ShapeDtypeStruct((rank, 2 * rank), jnp.float32),
        ],
        compiler_params=params(16),
        name="cov_in",
    )(packed, *pieces)


def cov_out_kernel(x_ref, cov_ref, *refs):
    pieces, (cov_out, sample_out) = refs[:-2], refs[-2:]
    g = total(pieces)
    cov_out[...] = cov_ref[...] + covariance(g, True)
    samples_of(x_ref[...], g, sample_out)


def cov_out(x, cov, pieces, seqs):
    rank = x.shape[0]
    return pl.pallas_call(
        cov_out_kernel,
        in_specs=[vmem()] * (2 + len(pieces)),
        out_specs=[vmem()] * 2,
        out_shape=[
            jax.ShapeDtypeStruct((rank, 2 * rank), jnp.float32),
            jax.ShapeDtypeStruct((seqs, rank, 2 * rank), jnp.float32),
        ],
        compiler_params=params(16),
        name="cov_out",
    )(x, cov, *pieces)


def scales(steps, spread):
    r = (spread - 1.0) / (spread + 1.0)
    out = []
    for _ in range(steps):
        out.append(2.0 / (2.0 - r * r))
        r = r * r / (2.0 - r * r)
    return out


def halves(value):
    high = value.astype(jnp.bfloat16)
    return high, (value - high.astype(jnp.float32)).astype(jnp.bfloat16)


def stacked(value):
    once = jnp.concatenate(halves(value), axis=1)
    return jnp.concatenate([once, once], axis=0)


def product(left, right):
    lanes = right.shape[1]
    both = nn(jnp.concatenate(halves(left), axis=1), stacked(right))
    return both[:, :lanes] + both[:, lanes:]


def damped_inverses(pair):
    size, both = pair.shape
    left = lax.broadcasted_iota(jnp.int32, pair.shape, 1) < size
    whole = jnp.concatenate([jnp.where(left, pair, 0.0), jnp.where(left, 0.0, pair)], axis=0)
    rows = lax.broadcasted_iota(jnp.int32, whole.shape, 0)
    cols = lax.broadcasted_iota(jnp.int32, whole.shape, 1)
    diagonal = rows == cols
    on_diagonal = jnp.where(diagonal, whole, 0.0)
    unit = jnp.where(
        rows < size, jnp.sum(on_diagonal[:size]) / size, jnp.sum(on_diagonal[size:]) / size
    )
    eye = jnp.where(diagonal, 1.0, 0.0)
    matrix = whole / unit + 0.1 * eye
    low, high = 0.1, size + 0.1
    start = 2.0 / (low + high)
    steps = scales(7, high / low)
    y = matrix * start
    x = (2.0 * start * steps[0]) * eye - (start * steps[0]) * y
    y = steps[0] * (2.0 * y - product(y, y))
    for scale in steps[1:-1]:
        turn = product(jnp.concatenate([x, y], axis=0), y)
        x = scale * (2.0 * x - turn[:both])
        y = scale * (2.0 * y - turn[both:])
    x = steps[-1] * (2.0 * x - product(x, y))
    x = x + product(x, eye - product(matrix, x))
    x = x + product(x, eye - nn(matrix, x, HIGHEST))
    return x / unit


def score_kernel(tokens, place_ref, own_ref, other_ref, sample_ref, *refs):
    pieces, (out, held, half) = refs[:-3], refs[-3:]
    parts = held.shape[0]
    for k, piece in enumerate(pieces):
        held[place_ref[0] ^ k] = piece[...]
    pair = (own_ref[...] + other_ref[...]) / tokens
    size, both = pair.shape
    inverses = damped_inverses(pair)
    samples = [sample_ref[s] for s in range(sample_ref.shape[0])]
    seqs = len(samples)
    blocks = held.shape[1]
    pairs = parts * blocks
    first = jnp.concatenate(halves(inverses[:size, :size]), axis=0)
    none = jnp.zeros_like(first)
    first = jnp.concatenate(
        [jnp.concatenate([first, none], axis=1), jnp.concatenate([none, first], axis=1)], axis=0
    )
    right = inverses[size:]
    second = stacked(jnp.concatenate([pltpu.roll(right, size, 1), right], axis=0))
    for part in range(parts // 2):
        for block in range(0, blocks, 2):
            rows = jnp.concatenate(
                [
                    held[part, block],
                    held[part + parts // 2, block],
                    held[part, block + 1],
                    held[part + parts // 2, block + 1],
                ],
                axis=0,
            )
            result = nt(first, rows)
            for k in range(2):
                two = result[both * k : both * (k + 1)]
                high, middle = halves(two[:size] + two[size:])
                pair = (2 * part + k) * blocks + block
                lanes = slice(pair * both, (pair + 2) * both)
                half[0, :, lanes] = high
                half[1, :, lanes] = middle
    lines = [[] for _ in range(seqs)]
    for pair in range(pairs):
        lanes = slice(pair * both, (pair + 1) * both)
        rows = jnp.concatenate([half[0, :, lanes], half[1, :, lanes]], axis=1)
        result = nn(rows, second)
        result = (result[:, :both] + result[:, both:]).astype(jnp.bfloat16).astype(jnp.float32)
        for s in range(seqs):
            lines[s].append(jnp.sum(result * samples[s], axis=0, keepdims=True))
    lines = jnp.concatenate([line for part in lines for line in part], axis=0)
    shape = (8, both)
    ends = jnp.where(
        (lax.broadcasted_iota(jnp.int32, shape, 1) < size)
        == (lax.broadcasted_iota(jnp.int32, shape, 0) == 0),
        1.0,
        0.0,
    )
    result = nt(ends, lines, HIGHEST)
    for s in range(seqs):
        for k in range(2):
            out[s : s + 1, k * pairs : (k + 1) * pairs] = result[
                k : k + 1, s * pairs : (s + 1) * pairs
            ]


def score(place, own, other, sample, pieces, tokens):
    blocks, rank, both = pieces[0].shape
    parts = len(pieces)
    pairs = parts * blocks
    seqs = sample.shape[0]
    return pl.pallas_call(
        functools.partial(score_kernel, tokens),
        in_specs=[smem()] + [vmem()] * (3 + len(pieces)),
        out_specs=vmem(),
        out_shape=jax.ShapeDtypeStruct((seqs, 2 * pairs), jnp.float32),
        scratch_shapes=[
            pltpu.VMEM((parts, blocks, rank, both), pieces[0].dtype),
            pltpu.VMEM((2, rank, pairs * both), jnp.bfloat16),
        ],
        compiler_params=params(16),
        name="score",
    )(place, own, other, sample, *pieces)


def swap(value, axis, bit):
    return lax.ppermute(value, axis, [(i, i ^ bit) for i in range(lax.axis_size(axis))])


def owners_swap(value, bits):
    parts = lax.axis_size("dp")
    places = [(t * parts + k, t * parts + (k ^ bits)) for t in (1, 2) for k in range(parts)]
    return lax.ppermute(value, ("tensor", "dp"), places)


def local_owned(acts, grads, proj_in, proj_out, queries):
    seqs, length, _ = acts.shape
    parts = lax.axis_size("dp")
    tokens = seqs * length * parts
    column = lax.axis_index("tensor").astype(jnp.int32)
    side = (column >= 2).astype(jnp.int32).reshape(1)
    place = lax.axis_index("dp").astype(jnp.int32).reshape(1)
    x_near, x_far, x_again, early = project_in(side, acts, proj_in, grads)
    x_pieces = to_owner(x_near, x_far, x_again)
    near, far, again, packed = project_out(side, grads, proj_out, queries, early)
    pieces = to_owner(near, far, again)
    packed, x, cov = cov_in(packed, x_pieces)
    query_pieces = [packed] + [owners_swap(packed, bits) for bits in range(1, parts)]
    cov, sample = cov_out(x, cov, pieces, seqs)
    other = jnp.zeros_like(cov)
    bit = 1
    while bit < parts:
        cov = cov if bit == 1 else cov + other
        other = swap(cov, "dp", bit)
        bit *= 2
    scores = score(place, cov, other, sample, query_pieces, tokens)
    owner = (column == 1) | (column == 2)
    one, two, three = (swap(scores, "tensor", bits) for bits in (1, 2, 3))
    return jnp.where(~owner, one, scores) + jnp.where(~owner, two, three)


def damp(matrix):
    size = matrix.shape[0]
    shift_by = 0.1 * jnp.trace(matrix) / size
    return matrix + shift_by * jnp.eye(size, dtype=matrix.dtype)


def chol_apply(factor, rhs):
    lower_sol = lax.linalg.triangular_solve(factor, rhs, left_side=True, lower=True)
    return lax.linalg.triangular_solve(
        factor, lower_sol, left_side=True, lower=True, transpose_a=True
    )


def precondition(query, left, right_side):
    count, rank = (query.shape[0], query.shape[1])
    left_fac = jnp.linalg.cholesky(left)
    right_fac = jnp.linalg.cholesky(right_side)
    stacked = jnp.transpose(query, (1, 0, 2)).reshape(rank, count * rank)
    middle = chol_apply(left_fac, stacked).reshape(rank, count, rank)
    turned = jnp.transpose(middle, (2, 1, 0)).reshape(rank, count * rank)
    result = chol_apply(right_fac, turned).reshape(rank, count, rank)
    return jnp.transpose(result, (1, 2, 0))


def diagonal_blocks(whole, rank):
    return jnp.stack([whole[:, 0:rank, 0:rank], whole[:, rank : 2 * rank, rank : 2 * rank]], axis=1)


def local_general(acts, grads, proj_in, proj_out, queries):
    seq_count, length, width_loc = acts.shape
    rank = proj_in.shape[1]
    hidden_loc = grads.shape[3]
    flat = acts.reshape(-1, width_loc)
    xpart = nt(flat, proj_in.reshape(2 * rank, width_loc))
    gpart = jnp.concatenate(
        [nt(grads[layer].reshape(-1, hidden_loc), proj_out[layer]) for layer in range(2)], axis=1
    )
    count = seq_count * length * lax.axis_size("dp")
    xin, gout = lax.psum((xpart, gpart), "tensor")
    in_cov, out_cov = lax.psum((tn(xin, xin, HIGHEST), tn(gout, gout, HIGHEST)), "dp")
    whole = (
        jnp.einsum(
            "sto,sti->soi",
            gout.reshape(seq_count, length, 2 * rank),
            xin.reshape(seq_count, length, 2 * rank),
            precision=HIGHEST,
        )
        / length
    )
    samples = diagonal_blocks(whole, rank)
    in_cov = in_cov / count
    out_cov = out_cov / count
    precond = []
    for layer in range(2):
        low = layer * rank
        damped_in = damp(in_cov[low : low + rank, low : low + rank])
        damped_out = damp(out_cov[low : low + rank, low : low + rank])
        precond.append(precondition(queries[:, layer].astype(jnp.float32), damped_out, damped_in))
    query_count = queries.shape[0]
    query_b = jnp.stack(precond, axis=1).astype(jnp.bfloat16).reshape(query_count, -1)
    sample_b = samples.astype(jnp.bfloat16).reshape(seq_count, -1)
    return nt(sample_b, lax.all_gather(query_b, "dp", axis=0, tiled=True))


def local(acts, grads, proj_in, proj_out, queries):
    parts = lax.axis_size("dp")
    even = parts > 1 and parts & (parts - 1) == 0
    if lax.axis_size("tensor") == 4 and even and queries.shape[0] % 4 == 0:
        return local_owned(acts, grads, proj_in, proj_out, queries)
    return local_general(acts, grads, proj_in, proj_out, queries)


def solution(mesh):
    placed = (
        P(("groups", "dp"), None, "tensor"),
        P(None, ("groups", "dp"), None, "tensor"),
        P(None, None, "tensor"),
        P(None, None, "tensor"),
        P("dp", None, None, None),
    )
    return jax.shard_map(
        local, mesh=mesh, in_specs=placed, out_specs=P(("groups", "dp"), None), check_vma=False
    )
```

```python
import functools

import jax
import jax.numpy as jnp
from jax import lax
from jax.experimental import pallas as pl
from jax.experimental.pallas import tpu as pltpu
from jax.sharding import PartitionSpec as P

HIGHEST = lax.Precision.HIGHEST
MIB = 1024 * 1024


def nt(a, b, precision=None):
    return lax.dot_general(
        a, b, (((1,), (1,)), ((), ())), precision=precision, preferred_element_type=jnp.float32
    )


def tn(a, b, precision=None):
    return lax.dot_general(
        a, b, (((0,), (0,)), ((), ())), precision=precision, preferred_element_type=jnp.float32
    )


def nn(a, b, precision=None):
    return jnp.dot(a, b, precision=precision, preferred_element_type=jnp.float32)


def vmem():
    return pl.BlockSpec(memory_space=pltpu.VMEM)


def smem():
    return pl.BlockSpec(memory_space=pltpu.SMEM)


def hbm():
    return pl.BlockSpec(memory_space=pl.ANY)


def in_hbm(value):
    return pltpu.with_memory_space_constraint(value, pltpu.HBM)


def params(mib):
    return pltpu.CompilerParams(vmem_limit_bytes=mib * MIB)


def project_in_kernel(
    side_ref, rows_hbm, proj_hbm, grads_hbm, near, far, again, early, rows, proj, acc, sems, proj_sem, early_sem
):
    seqs, length, width = rows.shape
    rank = proj.shape[1]
    proj_copy = pltpu.make_async_copy(proj_hbm, proj, proj_sem)
    proj_copy.start()

    def copy(s):
        return pltpu.make_async_copy(rows_hbm.at[s], rows.at[s], sems.at[s])

    for s in range(seqs):
        copy(s).start()
    early_copy = pltpu.make_async_copy(
        grads_hbm.at[:, 0, :, pl.ds(0, early.shape[2])], early, early_sem
    )
    early_copy.start()
    proj_copy.wait()

    group = 2 - seqs % 2

    @pl.loop(0, seqs // group)
    def _(step):
        for k in range(group):
            copy(step * group + k).wait()
        for k in range(group):
            s = step * group + k
            part = nt(proj[...].reshape(2 * rank, width), rows[s])
            tokens = pl.ds(pl.multiple_of(s * length, length), length)
            acc[0, :, tokens] = part[:rank]
            acc[1, :, tokens] = part[rank:]

    far[...] = acc[1 - side_ref[0]]
    again[...] = acc[1 - side_ref[0]]
    near[...] = acc[side_ref[0]]
    early_copy.wait()


def project_in(side, rows, proj, grads):
    seqs, length, _ = rows.shape
    early = (2, length, grads.shape[3] // 2)
    rank = proj.shape[1]
    return pl.pallas_call(
        project_in_kernel,
        in_specs=[smem(), hbm(), hbm(), hbm()],
        out_specs=[vmem()] * 4,
        out_shape=[
            jax.ShapeDtypeStruct((rank, seqs * length), jnp.float32),
            jax.ShapeDtypeStruct((rank, seqs * length), jnp.float32),
            jax.ShapeDtypeStruct((rank, seqs * length), jnp.float32),
            jax.ShapeDtypeStruct(early, grads.dtype),
        ],
        scratch_shapes=[
            pltpu.VMEM(rows.shape, rows.dtype),
            pltpu.VMEM(proj.shape, proj.dtype),
            pltpu.VMEM((2, rank, seqs * length), jnp.float32),
            pltpu.SemaphoreType.DMA((seqs,)),
            pltpu.SemaphoreType.DMA,
            pltpu.SemaphoreType.DMA,
        ],
        compiler_params=params(16),
        name="project_in",
    )(side, in_hbm(rows), in_hbm(proj), in_hbm(grads))


def project_out_kernel(side_ref, rows_hbm, proj_ref, queries_hbm, early, *refs):
    (near, far, again, packed), (rows, held, acc, sems, sem) = refs[:4], refs[4:]
    _, seqs, length, width = rows.shape
    parts = sems.shape[2]
    piece = width // parts
    copies = {}
    for s in range(seqs):
        for part in range(parts):
            if s == 0 and part < parts // 2:
                continue
            lanes = pl.ds(part * piece, piece)
            for layer in range(2):
                copies[s, part, layer] = pltpu.make_async_copy(
                    rows_hbm.at[layer, s, :, lanes],
                    rows.at[layer, s, :, lanes],
                    sems.at[layer, s, part],
                )
                copies[s, part, layer].start()
    copy = pltpu.make_async_copy(queries_hbm.at[:, side_ref[0]], held, sem)
    copy.start()
    for s in range(seqs):
        tokens = slice(s * length, (s + 1) * length)
        for part in range(parts):
            lanes = slice(part * piece, (part + 1) * piece)
            ready = s == 0 and part < parts // 2
            for layer in range(2):
                if not ready:
                    copies[s, part, layer].wait()
            for layer in range(2):
                block = early[layer, :, lanes] if ready else rows[layer, s, :, lanes]
                value = nt(proj_ref[layer, :, lanes], block)
                if part > 0:
                    value = value + acc[layer, :, tokens]
                acc[layer, :, tokens] = value
    far[...] = acc[1 - side_ref[0]]
    again[...] = acc[1 - side_ref[0]]
    near[...] = acc[side_ref[0]]
    copy.wait()
    blocks = held.shape[0] // 2
    for k in range(blocks):
        pair = [held[k].astype(jnp.float32), held[k + blocks].astype(jnp.float32)]
        packed[k] = jnp.concatenate(pair, axis=1).astype(held.dtype)


def project_out(side, rows, proj, queries, early):
    _, seqs, length, width = rows.shape
    rank = proj.shape[1]
    count = queries.shape[0]
    parts = 4 if width % 512 == 0 else 2
    return pl.pallas_call(
        project_out_kernel,
        in_specs=[smem(), hbm(), vmem(), hbm(), vmem()],
        out_specs=[vmem()] * 4,
        out_shape=[
            jax.ShapeDtypeStruct((rank, seqs * length), jnp.float32),
            jax.ShapeDtypeStruct((rank, seqs * length), jnp.float32),
            jax.ShapeDtypeStruct((rank, seqs * length), jnp.float32),
            jax.ShapeDtypeStruct((count // 2, rank, 2 * rank), queries.dtype),
        ],
        scratch_shapes=[
            pltpu.VMEM(rows.shape, rows.dtype),
            pltpu.VMEM((count, rank, rank), queries.dtype),
            pltpu.VMEM((2, rank, seqs * length), jnp.float32),
            pltpu.SemaphoreType.DMA((2, seqs, parts)),
            pltpu.SemaphoreType.DMA,
        ],
        compiler_params=params(40),
        name="project_out",
    )(side, in_hbm(rows), proj, in_hbm(queries), early)


def across(value):
    return lax.ppermute(value, "tensor", [(1, 2), (2, 1)])


def to_owner(near, far, again):
    return [
        near,
        lax.ppermute(near, "tensor", [(0, 1), (3, 2)]),
        lax.ppermute(far, "tensor", [(0, 2), (3, 1)]),
        across(again),
    ]


def total(pieces):
    value = pieces[0][...]
    for piece in pieces[1:]:
        value = value + piece[...]
    return value


def covariance(value, right):
    none = jnp.zeros_like(value)
    both = [none, value] if right else [value, none]
    return nt(value, jnp.concatenate(both, axis=0), HIGHEST)


def samples_of(x, g, sample_out):
    seqs = sample_out.shape[0]
    length = g.shape[1] // seqs
    for s in range(seqs):
        tokens = slice(s * length, (s + 1) * length)
        sample = nt(x[:, tokens], g[:, tokens], HIGHEST) / length
        sample = sample.astype(jnp.bfloat16).astype(jnp.float32)
        sample_out[s] = jnp.concatenate([sample, sample], axis=1)


def cov_in_kernel(packed_ref, *refs):
    pieces, (packed, x_out, cov_out) = refs[:-3], refs[-3:]
    packed[...] = packed_ref[...]
    x = total(pieces)
    x_out[...] = x
    cov_out[...] = covariance(x, False)


def cov_in(packed, pieces):
    rank, tokens = pieces[0].shape
    return pl.pallas_call(
        cov_in_kernel,
        in_specs=[vmem()] * (1 + len(pieces)),
        out_specs=[vmem()] * 3,
        out_shape=[
            jax.ShapeDtypeStruct(packed.shape, packed.dtype),
            jax.ShapeDtypeStruct((rank, tokens), jnp.float32),
            jax.ShapeDtypeStruct((rank, 2 * rank), jnp.float32),
        ],
        compiler_params=params(16),
        name="cov_in",
    )(packed, *pieces)


def cov_out_kernel(x_ref, cov_ref, *refs):
    pieces, (cov_out, sample_out) = refs[:-2], refs[-2:]
    g = total(pieces)
    cov_out[...] = cov_ref[...] + covariance(g, True)
    samples_of(x_ref[...], g, sample_out)


def cov_out(x, cov, pieces, seqs):
    rank = x.shape[0]
    return pl.pallas_call(
        cov_out_kernel,
        in_specs=[vmem()] * (2 + len(pieces)),
        out_specs=[vmem()] * 2,
        out_shape=[
            jax.ShapeDtypeStruct((rank, 2 * rank), jnp.float32),
            jax.ShapeDtypeStruct((seqs, rank, 2 * rank), jnp.float32),
        ],
        compiler_params=params(16),
        name="cov_out",
    )(x, cov, *pieces)


def scales(steps, spread):
    r = (spread - 1.0) / (spread + 1.0)
    out = []
    for _ in range(steps):
        out.append(2.0 / (2.0 - r * r))
        r = r * r / (2.0 - r * r)
    return out


def halves(value):
    high = value.astype(jnp.bfloat16)
    return high, (value - high.astype(jnp.float32)).astype(jnp.bfloat16)


def stacked(value):
    once = jnp.concatenate(halves(value), axis=1)
    return jnp.concatenate([once, once], axis=0)


def product(left, right):
    lanes = right.shape[1]
    both = nn(jnp.concatenate(halves(left), axis=1), stacked(right))
    return both[:, :lanes] + both[:, lanes:]


def damped_inverses(pair):
    size, both = pair.shape
    left = lax.broadcasted_iota(jnp.int32, pair.shape, 1) < size
    whole = jnp.concatenate([jnp.where(left, pair, 0.0), jnp.where(left, 0.0, pair)], axis=0)
    rows = lax.broadcasted_iota(jnp.int32, whole.shape, 0)
    cols = lax.broadcasted_iota(jnp.int32, whole.shape, 1)
    diagonal = rows == cols
    on_diagonal = jnp.where(diagonal, whole, 0.0)
    unit = jnp.where(
        rows < size, jnp.sum(on_diagonal[:size]) / size, jnp.sum(on_diagonal[size:]) / size
    )
    eye = jnp.where(diagonal, 1.0, 0.0)
    matrix = whole / unit + 0.1 * eye
    low, high = 0.1, size + 0.1
    start = 2.0 / (low + high)
    steps = scales(7, high / low)
    y = matrix * start
    x = (2.0 * start * steps[0]) * eye - (start * steps[0]) * y
    y = steps[0] * (2.0 * y - product(y, y))
    for scale in steps[1:-1]:
        turn = product(jnp.concatenate([x, y], axis=0), y)
        x = scale * (2.0 * x - turn[:both])
        y = scale * (2.0 * y - turn[both:])
    x = steps[-1] * (2.0 * x - product(x, y))
    x = x + product(x, eye - product(matrix, x))
    x = x + product(x, eye - nn(matrix, x, HIGHEST))
    return x / unit


def score_kernel(tokens, place_ref, own_ref, other_ref, sample_ref, *refs):
    pieces, (out, held, half) = refs[:-3], refs[-3:]
    parts = held.shape[0]
    for k, piece in enumerate(pieces):
        held[place_ref[0] ^ k] = piece[...]
    pair = (own_ref[...] + other_ref[...]) / tokens
    size, both = pair.shape
    inverses = damped_inverses(pair)
    samples = [sample_ref[s] for s in range(sample_ref.shape[0])]
    seqs = len(samples)
    blocks = held.shape[1]
    pairs = parts * blocks
    first = jnp.concatenate(halves(inverses[:size, :size]), axis=0)
    none = jnp.zeros_like(first)
    first = jnp.concatenate(
        [jnp.concatenate([first, none], axis=1), jnp.concatenate([none, first], axis=1)], axis=0
    )
    right = inverses[size:]
    second = stacked(jnp.concatenate([pltpu.roll(right, size, 1), right], axis=0))
    for part in range(parts // 2):
        for block in range(0, blocks, 2):
            rows = jnp.concatenate(
                [
                    held[part, block],
                    held[part + parts // 2, block],
                    held[part, block + 1],
                    held[part + parts // 2, block + 1],
                ],
                axis=0,
            )
            result = nt(first, rows)
            for k in range(2):
                two = result[both * k : both * (k + 1)]
                high, middle = halves(two[:size] + two[size:])
                pair = (2 * part + k) * blocks + block
                lanes = slice(pair * both, (pair + 2) * both)
                half[0, :, lanes] = high
                half[1, :, lanes] = middle
    lines = [[] for _ in range(seqs)]
    for pair in range(pairs):
        lanes = slice(pair * both, (pair + 1) * both)
        rows = jnp.concatenate([half[0, :, lanes], half[1, :, lanes]], axis=1)
        result = nn(rows, second)
        result = (result[:, :both] + result[:, both:]).astype(jnp.bfloat16).astype(jnp.float32)
        for s in range(seqs):
            lines[s].append(jnp.sum(result * samples[s], axis=0, keepdims=True))
    lines = jnp.concatenate([line for part in lines for line in part], axis=0)
    shape = (8, both)
    ends = jnp.where(
        (lax.broadcasted_iota(jnp.int32, shape, 1) < size)
        == (lax.broadcasted_iota(jnp.int32, shape, 0) == 0),
        1.0,
        0.0,
    )
    result = nt(ends, lines, HIGHEST)
    for s in range(seqs):
        for k in range(2):
            out[s : s + 1, k * pairs : (k + 1) * pairs] = result[
                k : k + 1, s * pairs : (s + 1) * pairs
            ]


def score(place, own, other, sample, pieces, tokens):
    blocks, rank, both = pieces[0].shape
    parts = len(pieces)
    pairs = parts * blocks
    seqs = sample.shape[0]
    return pl.pallas_call(
        functools.partial(score_kernel, tokens),
        in_specs=[smem()] + [vmem()] * (3 + len(pieces)),
        out_specs=vmem(),
        out_shape=jax.ShapeDtypeStruct((seqs, 2 * pairs), jnp.float32),
        scratch_shapes=[
            pltpu.VMEM((parts, blocks, rank, both), pieces[0].dtype),
            pltpu.VMEM((2, rank, pairs * both), jnp.bfloat16),
        ],
        compiler_params=params(16),
        name="score",
    )(place, own, other, sample, *pieces)


def swap(value, axis, bit):
    return lax.ppermute(value, axis, [(i, i ^ bit) for i in range(lax.axis_size(axis))])


def owners_swap(value, bits):
    parts = lax.axis_size("dp")
    places = [(t * parts + k, t * parts + (k ^ bits)) for t in (1, 2) for k in range(parts)]
    return lax.ppermute(value, ("tensor", "dp"), places)


def local_owned(acts, grads, proj_in, proj_out, queries):
    seqs, length, _ = acts.shape
    parts = lax.axis_size("dp")
    tokens = seqs * length * parts
    column = lax.axis_index("tensor").astype(jnp.int32)
    side = (column >= 2).astype(jnp.int32).reshape(1)
    place = lax.axis_index("dp").astype(jnp.int32).reshape(1)
    x_near, x_far, x_again, early = project_in(side, acts, proj_in, grads)
    x_pieces = to_owner(x_near, x_far, x_again)
    near, far, again, packed = project_out(side, grads, proj_out, queries, early)
    pieces = to_owner(near, far, again)
    packed, x, cov = cov_in(packed, x_pieces)
    query_pieces = [packed] + [owners_swap(packed, bits) for bits in range(1, parts)]
    cov, sample = cov_out(x, cov, pieces, seqs)
    other = jnp.zeros_like(cov)
    bit = 1
    while bit < parts:
        cov = cov if bit == 1 else cov + other
        other = swap(cov, "dp", bit)
        bit *= 2
    scores = score(place, cov, other, sample, query_pieces, tokens)
    owner = (column == 1) | (column == 2)
    one, two, three = (swap(scores, "tensor", bits) for bits in (1, 2, 3))
    return jnp.where(owner, three, one) + jnp.where(owner, scores, two)


def damp(matrix):
    size = matrix.shape[0]
    shift_by = 0.1 * jnp.trace(matrix) / size
    return matrix + shift_by * jnp.eye(size, dtype=matrix.dtype)


def chol_apply(factor, rhs):
    lower_sol = lax.linalg.triangular_solve(factor, rhs, left_side=True, lower=True)
    return lax.linalg.triangular_solve(
        factor, lower_sol, left_side=True, lower=True, transpose_a=True
    )


def precondition(query, left, right_side):
    count, rank = (query.shape[0], query.shape[1])
    left_fac = jnp.linalg.cholesky(left)
    right_fac = jnp.linalg.cholesky(right_side)
    stacked = jnp.transpose(query, (1, 0, 2)).reshape(rank, count * rank)
    middle = chol_apply(left_fac, stacked).reshape(rank, count, rank)
    turned = jnp.transpose(middle, (2, 1, 0)).reshape(rank, count * rank)
    result = chol_apply(right_fac, turned).reshape(rank, count, rank)
    return jnp.transpose(result, (1, 2, 0))


def diagonal_blocks(whole, rank):
    return jnp.stack([whole[:, 0:rank, 0:rank], whole[:, rank : 2 * rank, rank : 2 * rank]], axis=1)


def local_general(acts, grads, proj_in, proj_out, queries):
    seq_count, length, width_loc = acts.shape
    rank = proj_in.shape[1]
    hidden_loc = grads.shape[3]
    flat = acts.reshape(-1, width_loc)
    xpart = nt(flat, proj_in.reshape(2 * rank, width_loc))
    gpart = jnp.concatenate(
        [nt(grads[layer].reshape(-1, hidden_loc), proj_out[layer]) for layer in range(2)], axis=1
    )
    count = seq_count * length * lax.axis_size("dp")
    xin, gout = lax.psum((xpart, gpart), "tensor")
    in_cov, out_cov = lax.psum((tn(xin, xin, HIGHEST), tn(gout, gout, HIGHEST)), "dp")
    whole = (
        jnp.einsum(
            "sto,sti->soi",
            gout.reshape(seq_count, length, 2 * rank),
            xin.reshape(seq_count, length, 2 * rank),
            precision=HIGHEST,
        )
        / length
    )
    samples = diagonal_blocks(whole, rank)
    in_cov = in_cov / count
    out_cov = out_cov / count
    precond = []
    for layer in range(2):
        low = layer * rank
        damped_in = damp(in_cov[low : low + rank, low : low + rank])
        damped_out = damp(out_cov[low : low + rank, low : low + rank])
        precond.append(precondition(queries[:, layer].astype(jnp.float32), damped_out, damped_in))
    query_count = queries.shape[0]
    query_b = jnp.stack(precond, axis=1).astype(jnp.bfloat16).reshape(query_count, -1)
    sample_b = samples.astype(jnp.bfloat16).reshape(seq_count, -1)
    return nt(sample_b, lax.all_gather(query_b, "dp", axis=0, tiled=True))


def local(acts, grads, proj_in, proj_out, queries):
    parts = lax.axis_size("dp")
    even = parts > 1 and parts & (parts - 1) == 0
    if lax.axis_size("tensor") == 4 and even and queries.shape[0] % 4 == 0:
        return local_owned(acts, grads, proj_in, proj_out, queries)
    return local_general(acts, grads, proj_in, proj_out, queries)


def solution(mesh):
    placed = (
        P(("groups", "dp"), None, "tensor"),
        P(None, ("groups", "dp"), None, "tensor"),
        P(None, None, "tensor"),
        P(None, None, "tensor"),
        P("dp", None, None, None),
    )
    return jax.shard_map(
        local, mesh=mesh, in_specs=placed, out_specs=P(("groups", "dp"), None), check_vma=False
    )
```

```python
import functools

import jax
import jax.numpy as jnp
from jax import lax
from jax.experimental import pallas as pl
from jax.experimental.pallas import tpu as pltpu
from jax.sharding import PartitionSpec as P

HIGHEST = lax.Precision.HIGHEST
MIB = 1024 * 1024


def nt(a, b, precision=None):
    return lax.dot_general(
        a, b, (((1,), (1,)), ((), ())), precision=precision, preferred_element_type=jnp.float32
    )


def tn(a, b, precision=None):
    return lax.dot_general(
        a, b, (((0,), (0,)), ((), ())), precision=precision, preferred_element_type=jnp.float32
    )


def nn(a, b, precision=None):
    return jnp.dot(a, b, precision=precision, preferred_element_type=jnp.float32)


def vmem():
    return pl.BlockSpec(memory_space=pltpu.VMEM)


def smem():
    return pl.BlockSpec(memory_space=pltpu.SMEM)


def hbm():
    return pl.BlockSpec(memory_space=pl.ANY)


def in_hbm(value):
    return pltpu.with_memory_space_constraint(value, pltpu.HBM)


def params(mib):
    return pltpu.CompilerParams(vmem_limit_bytes=mib * MIB)


def project_in_kernel(
    side_ref, rows_hbm, proj_hbm, grads_hbm, near, far, again, early, rows, proj, acc, sems, proj_sem, early_sem
):
    seqs, length, width = rows.shape
    rank = proj.shape[1]
    proj_copy = pltpu.make_async_copy(proj_hbm, proj, proj_sem)
    proj_copy.start()

    def copy(s):
        return pltpu.make_async_copy(rows_hbm.at[s], rows.at[s], sems.at[s])

    for s in range(seqs):
        copy(s).start()
    early_copy = pltpu.make_async_copy(
        grads_hbm.at[:, 0, :, pl.ds(0, early.shape[2])], early, early_sem
    )
    early_copy.start()
    proj_copy.wait()

    group = 2 - seqs % 2

    @pl.loop(0, seqs // group)
    def _(step):
        for k in range(group):
            copy(step * group + k).wait()
        for k in range(group):
            s = step * group + k
            part = nt(proj[...].reshape(2 * rank, width), rows[s])
            tokens = pl.ds(pl.multiple_of(s * length, length), length)
            acc[0, :, tokens] = part[:rank]
            acc[1, :, tokens] = part[rank:]

    far[...] = acc[1 - side_ref[0]]
    again[...] = acc[1 - side_ref[0]]
    near[...] = acc[side_ref[0]]
    early_copy.wait()


def project_in(side, rows, proj, grads):
    seqs, length, _ = rows.shape
    early = (2, length, grads.shape[3] // 2)
    rank = proj.shape[1]
    return pl.pallas_call(
        project_in_kernel,
        in_specs=[smem(), hbm(), hbm(), hbm()],
        out_specs=[vmem()] * 4,
        out_shape=[
            jax.ShapeDtypeStruct((rank, seqs * length), jnp.float32),
            jax.ShapeDtypeStruct((rank, seqs * length), jnp.float32),
            jax.ShapeDtypeStruct((rank, seqs * length), jnp.float32),
            jax.ShapeDtypeStruct(early, grads.dtype),
        ],
        scratch_shapes=[
            pltpu.VMEM(rows.shape, rows.dtype),
            pltpu.VMEM(proj.shape, proj.dtype),
            pltpu.VMEM((2, rank, seqs * length), jnp.float32),
            pltpu.SemaphoreType.DMA((seqs,)),
            pltpu.SemaphoreType.DMA,
            pltpu.SemaphoreType.DMA,
        ],
        compiler_params=params(16),
        name="project_in",
    )(side, in_hbm(rows), in_hbm(proj), in_hbm(grads))


def project_out_kernel(side_ref, rows_hbm, proj_ref, queries_hbm, early, *refs):
    (near, far, again, packed), (rows, held, acc, sems, sem) = refs[:4], refs[4:]
    _, seqs, length, width = rows.shape
    parts = sems.shape[2]
    piece = width // parts
    copies = {}
    for s in range(seqs):
        for part in range(parts):
            if s == 0 and part < parts // 2:
                continue
            lanes = pl.ds(part * piece, piece)
            for layer in range(2):
                copies[s, part, layer] = pltpu.make_async_copy(
                    rows_hbm.at[layer, s, :, lanes],
                    rows.at[layer, s, :, lanes],
                    sems.at[layer, s, part],
                )
                copies[s, part, layer].start()
    copy = pltpu.make_async_copy(queries_hbm.at[:, side_ref[0]], held, sem)
    copy.start()
    for s in range(seqs):
        tokens = slice(s * length, (s + 1) * length)
        for part in range(parts):
            lanes = slice(part * piece, (part + 1) * piece)
            ready = s == 0 and part < parts // 2
            for layer in range(2):
                if not ready:
                    copies[s, part, layer].wait()
            for layer in range(2):
                block = early[layer, :, lanes] if ready else rows[layer, s, :, lanes]
                value = nt(proj_ref[layer, :, lanes], block)
                if part > 0:
                    value = value + acc[layer, :, tokens]
                acc[layer, :, tokens] = value
    far[...] = acc[1 - side_ref[0]]
    again[...] = acc[1 - side_ref[0]]
    near[...] = acc[side_ref[0]]
    copy.wait()
    blocks = held.shape[0] // 2
    for k in range(blocks):
        pair = [held[k].astype(jnp.float32), held[k + blocks].astype(jnp.float32)]
        packed[k] = jnp.concatenate(pair, axis=1).astype(held.dtype)


def project_out(side, rows, proj, queries, early):
    _, seqs, length, width = rows.shape
    rank = proj.shape[1]
    count = queries.shape[0]
    parts = 4 if width % 512 == 0 else 2
    return pl.pallas_call(
        project_out_kernel,
        in_specs=[smem(), hbm(), vmem(), hbm(), vmem()],
        out_specs=[vmem()] * 4,
        out_shape=[
            jax.ShapeDtypeStruct((rank, seqs * length), jnp.float32),
            jax.ShapeDtypeStruct((rank, seqs * length), jnp.float32),
            jax.ShapeDtypeStruct((rank, seqs * length), jnp.float32),
            jax.ShapeDtypeStruct((count // 2, rank, 2 * rank), queries.dtype),
        ],
        scratch_shapes=[
            pltpu.VMEM(rows.shape, rows.dtype),
            pltpu.VMEM((count, rank, rank), queries.dtype),
            pltpu.VMEM((2, rank, seqs * length), jnp.float32),
            pltpu.SemaphoreType.DMA((2, seqs, parts)),
            pltpu.SemaphoreType.DMA,
        ],
        compiler_params=params(40),
        name="project_out",
    )(side, in_hbm(rows), proj, in_hbm(queries), early)


def across(value):
    return lax.ppermute(value, "tensor", [(1, 2), (2, 1)])


def to_owner(near, far, again):
    return [
        near,
        lax.ppermute(near, "tensor", [(0, 1), (3, 2), (1, 0), (2, 3)]),
        lax.ppermute(far, "tensor", [(0, 2), (3, 1), (1, 0), (2, 3)]),
        across(again),
    ]


def total(pieces):
    value = pieces[0][...]
    for piece in pieces[1:]:
        value = value + piece[...]
    return value


def covariance(value, right):
    none = jnp.zeros_like(value)
    both = [none, value] if right else [value, none]
    return nt(value, jnp.concatenate(both, axis=0), HIGHEST)


def samples_of(x, g, sample_out):
    seqs = sample_out.shape[0]
    length = g.shape[1] // seqs
    for s in range(seqs):
        tokens = slice(s * length, (s + 1) * length)
        sample = nt(x[:, tokens], g[:, tokens], HIGHEST) / length
        sample = sample.astype(jnp.bfloat16).astype(jnp.float32)
        sample_out[s] = jnp.concatenate([sample, sample], axis=1)


def cov_in_kernel(packed_ref, *refs):
    pieces, (packed, x_out, cov_out) = refs[:-3], refs[-3:]
    packed[...] = packed_ref[...]
    x = total(pieces)
    x_out[...] = x
    cov_out[...] = covariance(x, False)


def cov_in(packed, pieces):
    rank, tokens = pieces[0].shape
    return pl.pallas_call(
        cov_in_kernel,
        in_specs=[vmem()] * (1 + len(pieces)),
        out_specs=[vmem()] * 3,
        out_shape=[
            jax.ShapeDtypeStruct(packed.shape, packed.dtype),
            jax.ShapeDtypeStruct((rank, tokens), jnp.float32),
            jax.ShapeDtypeStruct((rank, 2 * rank), jnp.float32),
        ],
        compiler_params=params(16),
        name="cov_in",
    )(packed, *pieces)


def cov_out_kernel(x_ref, cov_ref, *refs):
    pieces, (cov_out, sample_out) = refs[:-2], refs[-2:]
    g = total(pieces)
    cov_out[...] = cov_ref[...] + covariance(g, True)
    samples_of(x_ref[...], g, sample_out)


def cov_out(x, cov, pieces, seqs):
    rank = x.shape[0]
    return pl.pallas_call(
        cov_out_kernel,
        in_specs=[vmem()] * (2 + len(pieces)),
        out_specs=[vmem()] * 2,
        out_shape=[
            jax.ShapeDtypeStruct((rank, 2 * rank), jnp.float32),
            jax.ShapeDtypeStruct((seqs, rank, 2 * rank), jnp.float32),
        ],
        compiler_params=params(16),
        name="cov_out",
    )(x, cov, *pieces)


def scales(steps, spread):
    r = (spread - 1.0) / (spread + 1.0)
    out = []
    for _ in range(steps):
        out.append(2.0 / (2.0 - r * r))
        r = r * r / (2.0 - r * r)
    return out


def halves(value):
    high = value.astype(jnp.bfloat16)
    return high, (value - high.astype(jnp.float32)).astype(jnp.bfloat16)


def stacked(value):
    once = jnp.concatenate(halves(value), axis=1)
    return jnp.concatenate([once, once], axis=0)


def product(left, right):
    lanes = right.shape[1]
    both = nn(jnp.concatenate(halves(left), axis=1), stacked(right))
    return both[:, :lanes] + both[:, lanes:]


def damped_inverses(pair):
    size, both = pair.shape
    left = lax.broadcasted_iota(jnp.int32, pair.shape, 1) < size
    whole = jnp.concatenate([jnp.where(left, pair, 0.0), jnp.where(left, 0.0, pair)], axis=0)
    rows = lax.broadcasted_iota(jnp.int32, whole.shape, 0)
    cols = lax.broadcasted_iota(jnp.int32, whole.shape, 1)
    diagonal = rows == cols
    on_diagonal = jnp.where(diagonal, whole, 0.0)
    unit = jnp.where(
        rows < size, jnp.sum(on_diagonal[:size]) / size, jnp.sum(on_diagonal[size:]) / size
    )
    eye = jnp.where(diagonal, 1.0, 0.0)
    matrix = whole / unit + 0.1 * eye
    low, high = 0.1, size + 0.1
    start = 2.0 / (low + high)
    steps = scales(7, high / low)
    y = matrix * start
    x = (2.0 * start * steps[0]) * eye - (start * steps[0]) * y
    y = steps[0] * (2.0 * y - product(y, y))
    for scale in steps[1:-1]:
        turn = product(jnp.concatenate([x, y], axis=0), y)
        x = scale * (2.0 * x - turn[:both])
        y = scale * (2.0 * y - turn[both:])
    x = steps[-1] * (2.0 * x - product(x, y))
    x = x + product(x, eye - product(matrix, x))
    x = x + product(x, eye - nn(matrix, x, HIGHEST))
    return x / unit


def score_kernel(tokens, place_ref, own_ref, other_ref, sample_ref, *refs):
    pieces, (out, held, half) = refs[:-3], refs[-3:]
    parts = held.shape[0]
    for k, piece in enumerate(pieces):
        held[place_ref[0] ^ k] = piece[...]
    pair = (own_ref[...] + other_ref[...]) / tokens
    size, both = pair.shape
    inverses = damped_inverses(pair)
    samples = [sample_ref[s] for s in range(sample_ref.shape[0])]
    seqs = len(samples)
    blocks = held.shape[1]
    pairs = parts * blocks
    first = jnp.concatenate(halves(inverses[:size, :size]), axis=0)
    none = jnp.zeros_like(first)
    first = jnp.concatenate(
        [jnp.concatenate([first, none], axis=1), jnp.concatenate([none, first], axis=1)], axis=0
    )
    right = inverses[size:]
    second = stacked(jnp.concatenate([pltpu.roll(right, size, 1), right], axis=0))
    for part in range(parts // 2):
        for block in range(0, blocks, 2):
            rows = jnp.concatenate(
                [
                    held[part, block],
                    held[part + parts // 2, block],
                    held[part, block + 1],
                    held[part + parts // 2, block + 1],
                ],
                axis=0,
            )
            result = nt(first, rows)
            for k in range(2):
                two = result[both * k : both * (k + 1)]
                high, middle = halves(two[:size] + two[size:])
                pair = (2 * part + k) * blocks + block
                lanes = slice(pair * both, (pair + 2) * both)
                half[0, :, lanes] = high
                half[1, :, lanes] = middle
    lines = [[] for _ in range(seqs)]
    for pair in range(pairs):
        lanes = slice(pair * both, (pair + 1) * both)
        rows = jnp.concatenate([half[0, :, lanes], half[1, :, lanes]], axis=1)
        result = nn(rows, second)
        result = (result[:, :both] + result[:, both:]).astype(jnp.bfloat16).astype(jnp.float32)
        for s in range(seqs):
            lines[s].append(jnp.sum(result * samples[s], axis=0, keepdims=True))
    lines = jnp.concatenate([line for part in lines for line in part], axis=0)
    shape = (8, both)
    ends = jnp.where(
        (lax.broadcasted_iota(jnp.int32, shape, 1) < size)
        == (lax.broadcasted_iota(jnp.int32, shape, 0) == 0),
        1.0,
        0.0,
    )
    result = nt(ends, lines, HIGHEST)
    for s in range(seqs):
        for k in range(2):
            out[s : s + 1, k * pairs : (k + 1) * pairs] = result[
                k : k + 1, s * pairs : (s + 1) * pairs
            ]


def score(place, own, other, sample, pieces, tokens):
    blocks, rank, both = pieces[0].shape
    parts = len(pieces)
    pairs = parts * blocks
    seqs = sample.shape[0]
    return pl.pallas_call(
        functools.partial(score_kernel, tokens),
        in_specs=[smem()] + [vmem()] * (3 + len(pieces)),
        out_specs=vmem(),
        out_shape=jax.ShapeDtypeStruct((seqs, 2 * pairs), jnp.float32),
        scratch_shapes=[
            pltpu.VMEM((parts, blocks, rank, both), pieces[0].dtype),
            pltpu.VMEM((2, rank, pairs * both), jnp.bfloat16),
        ],
        compiler_params=params(16),
        name="score",
    )(place, own, other, sample, *pieces)


def swap(value, axis, bit):
    return lax.ppermute(value, axis, [(i, i ^ bit) for i in range(lax.axis_size(axis))])


def shift(value, axis, by):
    size = lax.axis_size(axis)
    return lax.ppermute(value, axis, [(i, (i + by) % size) for i in range(size)])


def owners_swap(value, bits):
    parts = lax.axis_size("dp")
    places = [(t * parts + k, t * parts + (k ^ bits)) for t in (1, 2) for k in range(parts)]
    return lax.ppermute(value, ("tensor", "dp"), places)


def local_owned(acts, grads, proj_in, proj_out, queries):
    seqs, length, _ = acts.shape
    parts = lax.axis_size("dp")
    tokens = seqs * length * parts
    column = lax.axis_index("tensor").astype(jnp.int32)
    side = (column >= 2).astype(jnp.int32).reshape(1)
    place = lax.axis_index("dp").astype(jnp.int32).reshape(1)
    x_near, x_far, x_again, early = project_in(side, acts, proj_in, grads)
    x_pieces = to_owner(x_near, x_far, x_again)
    near, far, again, packed = project_out(side, grads, proj_out, queries, early)
    pieces = to_owner(near, far, again)
    packed, x, cov = cov_in(packed, x_pieces)
    query_pieces = [packed] + [owners_swap(packed, bits) for bits in range(1, parts)]
    cov, sample = cov_out(x, cov, pieces, seqs)
    other = jnp.zeros_like(cov)
    bit = 1
    while bit < parts:
        cov = cov if bit == 1 else cov + other
        other = swap(cov, "dp", bit)
        bit *= 2
    scores = score(place, cov, other, sample, query_pieces, tokens)
    above = shift(scores, "tensor", -1)
    opposite = shift(scores, "tensor", 2)
    below = shift(scores, "tensor", 1)
    owner = (column == 1) | (column == 2)
    return jnp.where(owner, scores, opposite) + jnp.where(column >= 2, below, above)


def damp(matrix):
    size = matrix.shape[0]
    shift_by = 0.1 * jnp.trace(matrix) / size
    return matrix + shift_by * jnp.eye(size, dtype=matrix.dtype)


def chol_apply(factor, rhs):
    lower_sol = lax.linalg.triangular_solve(factor, rhs, left_side=True, lower=True)
    return lax.linalg.triangular_solve(
        factor, lower_sol, left_side=True, lower=True, transpose_a=True
    )


def precondition(query, left, right_side):
    count, rank = (query.shape[0], query.shape[1])
    left_fac = jnp.linalg.cholesky(left)
    right_fac = jnp.linalg.cholesky(right_side)
    stacked = jnp.transpose(query, (1, 0, 2)).reshape(rank, count * rank)
    middle = chol_apply(left_fac, stacked).reshape(rank, count, rank)
    turned = jnp.transpose(middle, (2, 1, 0)).reshape(rank, count * rank)
    result = chol_apply(right_fac, turned).reshape(rank, count, rank)
    return jnp.transpose(result, (1, 2, 0))


def diagonal_blocks(whole, rank):
    return jnp.stack([whole[:, 0:rank, 0:rank], whole[:, rank : 2 * rank, rank : 2 * rank]], axis=1)


def local_general(acts, grads, proj_in, proj_out, queries):
    seq_count, length, width_loc = acts.shape
    rank = proj_in.shape[1]
    hidden_loc = grads.shape[3]
    flat = acts.reshape(-1, width_loc)
    xpart = nt(flat, proj_in.reshape(2 * rank, width_loc))
    gpart = jnp.concatenate(
        [nt(grads[layer].reshape(-1, hidden_loc), proj_out[layer]) for layer in range(2)], axis=1
    )
    count = seq_count * length * lax.axis_size("dp")
    xin, gout = lax.psum((xpart, gpart), "tensor")
    in_cov, out_cov = lax.psum((tn(xin, xin, HIGHEST), tn(gout, gout, HIGHEST)), "dp")
    whole = (
        jnp.einsum(
            "sto,sti->soi",
            gout.reshape(seq_count, length, 2 * rank),
            xin.reshape(seq_count, length, 2 * rank),
            precision=HIGHEST,
        )
        / length
    )
    samples = diagonal_blocks(whole, rank)
    in_cov = in_cov / count
    out_cov = out_cov / count
    precond = []
    for layer in range(2):
        low = layer * rank
        damped_in = damp(in_cov[low : low + rank, low : low + rank])
        damped_out = damp(out_cov[low : low + rank, low : low + rank])
        precond.append(precondition(queries[:, layer].astype(jnp.float32), damped_out, damped_in))
    query_count = queries.shape[0]
    query_b = jnp.stack(precond, axis=1).astype(jnp.bfloat16).reshape(query_count, -1)
    sample_b = samples.astype(jnp.bfloat16).reshape(seq_count, -1)
    return nt(sample_b, lax.all_gather(query_b, "dp", axis=0, tiled=True))


def local(acts, grads, proj_in, proj_out, queries):
    parts = lax.axis_size("dp")
    even = parts > 1 and parts & (parts - 1) == 0
    if lax.axis_size("tensor") == 4 and even and queries.shape[0] % 4 == 0:
        return local_owned(acts, grads, proj_in, proj_out, queries)
    return local_general(acts, grads, proj_in, proj_out, queries)


def solution(mesh):
    placed = (
        P(("groups", "dp"), None, "tensor"),
        P(None, ("groups", "dp"), None, "tensor"),
        P(None, None, "tensor"),
        P(None, None, "tensor"),
        P("dp", None, None, None),
    )
    return jax.shard_map(
        local, mesh=mesh, in_specs=placed, out_specs=P(("groups", "dp"), None), check_vma=False
    )
```

```python
import functools

import jax
import jax.numpy as jnp
from jax import lax
from jax.experimental import pallas as pl
from jax.experimental.pallas import tpu as pltpu
from jax.sharding import PartitionSpec as P

HIGHEST = lax.Precision.HIGHEST
MIB = 1024 * 1024


def nt(a, b, precision=None):
    return lax.dot_general(
        a, b, (((1,), (1,)), ((), ())), precision=precision, preferred_element_type=jnp.float32
    )


def tn(a, b, precision=None):
    return lax.dot_general(
        a, b, (((0,), (0,)), ((), ())), precision=precision, preferred_element_type=jnp.float32
    )


def nn(a, b, precision=None):
    return jnp.dot(a, b, precision=precision, preferred_element_type=jnp.float32)


def vmem():
    return pl.BlockSpec(memory_space=pltpu.VMEM)


def smem():
    return pl.BlockSpec(memory_space=pltpu.SMEM)


def hbm():
    return pl.BlockSpec(memory_space=pl.ANY)


def in_hbm(value):
    return pltpu.with_memory_space_constraint(value, pltpu.HBM)


def params(mib):
    return pltpu.CompilerParams(vmem_limit_bytes=mib * MIB)


def project_in_kernel(
    side_ref, rows_hbm, proj_hbm, grads_hbm, near, far, again, early, rows, proj, acc, sems, proj_sem, early_sem
):
    seqs, length, width = rows.shape
    rank = proj.shape[1]
    proj_copy = pltpu.make_async_copy(proj_hbm, proj, proj_sem)
    proj_copy.start()

    def copy(s):
        return pltpu.make_async_copy(rows_hbm.at[s], rows.at[s], sems.at[s])

    for s in range(seqs):
        copy(s).start()
    early_copy = pltpu.make_async_copy(
        grads_hbm.at[:, 0, :, pl.ds(0, early.shape[2])], early, early_sem
    )
    early_copy.start()
    proj_copy.wait()

    group = 2 - seqs % 2

    @pl.loop(0, seqs // group)
    def _(step):
        for k in range(group):
            copy(step * group + k).wait()
        for k in range(group):
            s = step * group + k
            part = nt(proj[...].reshape(2 * rank, width), rows[s])
            tokens = pl.ds(pl.multiple_of(s * length, length), length)
            acc[0, :, tokens] = part[:rank]
            acc[1, :, tokens] = part[rank:]

    far[...] = acc[1 - side_ref[0]]
    again[...] = acc[1 - side_ref[0]]
    near[...] = acc[side_ref[0]]
    early_copy.wait()


def project_in(side, rows, proj, grads):
    seqs, length, _ = rows.shape
    early = (2, length, grads.shape[3] // 2)
    rank = proj.shape[1]
    return pl.pallas_call(
        project_in_kernel,
        in_specs=[smem(), hbm(), hbm(), hbm()],
        out_specs=[vmem()] * 4,
        out_shape=[
            jax.ShapeDtypeStruct((rank, seqs * length), jnp.float32),
            jax.ShapeDtypeStruct((rank, seqs * length), jnp.float32),
            jax.ShapeDtypeStruct((rank, seqs * length), jnp.float32),
            jax.ShapeDtypeStruct(early, grads.dtype),
        ],
        scratch_shapes=[
            pltpu.VMEM(rows.shape, rows.dtype),
            pltpu.VMEM(proj.shape, proj.dtype),
            pltpu.VMEM((2, rank, seqs * length), jnp.float32),
            pltpu.SemaphoreType.DMA((seqs,)),
            pltpu.SemaphoreType.DMA,
            pltpu.SemaphoreType.DMA,
        ],
        compiler_params=params(16),
        name="project_in",
    )(side, in_hbm(rows), in_hbm(proj), in_hbm(grads))


def project_out_kernel(side_ref, rows_hbm, proj_ref, queries_hbm, early, *refs):
    (near, far, again, packed), (rows, held, acc, sems, sem) = refs[:4], refs[4:]
    _, seqs, length, width = rows.shape
    parts = sems.shape[2]
    piece = width // parts
    copies = {}
    for s in range(seqs):
        for part in range(parts):
            if s == 0 and part < parts // 2:
                continue
            lanes = pl.ds(part * piece, piece)
            for layer in range(2):
                copies[s, part, layer] = pltpu.make_async_copy(
                    rows_hbm.at[layer, s, :, lanes],
                    rows.at[layer, s, :, lanes],
                    sems.at[layer, s, part],
                )
                copies[s, part, layer].start()
    copy = pltpu.make_async_copy(queries_hbm.at[:, side_ref[0]], held, sem)
    copy.start()
    for s in range(seqs):
        tokens = slice(s * length, (s + 1) * length)
        for part in range(parts):
            lanes = slice(part * piece, (part + 1) * piece)
            ready = s == 0 and part < parts // 2
            for layer in range(2):
                if not ready:
                    copies[s, part, layer].wait()
            for layer in range(2):
                block = early[layer, :, lanes] if ready else rows[layer, s, :, lanes]
                value = nt(proj_ref[layer, :, lanes], block)
                if part > 0:
                    value = value + acc[layer, :, tokens]
                acc[layer, :, tokens] = value
    far[...] = acc[1 - side_ref[0]]
    again[...] = acc[1 - side_ref[0]]
    near[...] = acc[side_ref[0]]
    copy.wait()
    blocks = held.shape[0] // 2
    for k in range(blocks):
        pair = [held[k].astype(jnp.float32), held[k + blocks].astype(jnp.float32)]
        packed[k] = jnp.concatenate(pair, axis=1).astype(held.dtype)


def project_out(side, rows, proj, queries, early):
    _, seqs, length, width = rows.shape
    rank = proj.shape[1]
    count = queries.shape[0]
    parts = 4 if width % 512 == 0 else 2
    return pl.pallas_call(
        project_out_kernel,
        in_specs=[smem(), hbm(), vmem(), hbm(), vmem()],
        out_specs=[vmem()] * 4,
        out_shape=[
            jax.ShapeDtypeStruct((rank, seqs * length), jnp.float32),
            jax.ShapeDtypeStruct((rank, seqs * length), jnp.float32),
            jax.ShapeDtypeStruct((rank, seqs * length), jnp.float32),
            jax.ShapeDtypeStruct((count // 2, rank, 2 * rank), queries.dtype),
        ],
        scratch_shapes=[
            pltpu.VMEM(rows.shape, rows.dtype),
            pltpu.VMEM((count, rank, rank), queries.dtype),
            pltpu.VMEM((2, rank, seqs * length), jnp.float32),
            pltpu.SemaphoreType.DMA((2, seqs, parts)),
            pltpu.SemaphoreType.DMA,
        ],
        compiler_params=params(40),
        name="project_out",
    )(side, in_hbm(rows), proj, in_hbm(queries), early)


def across(value):
    return lax.ppermute(value, "tensor", [(1, 2), (2, 1)])


def to_owner(near, far, again):
    return [
        near,
        lax.ppermute(near, "tensor", [(0, 1), (3, 2), (1, 0), (2, 3)]),
        lax.ppermute(far, "tensor", [(0, 2), (3, 1), (1, 0), (2, 3)]),
        across(again),
    ]


def total(pieces):
    value = pieces[0][...]
    for piece in pieces[1:]:
        value = value + piece[...]
    return value


def covariance(value, right):
    none = jnp.zeros_like(value)
    both = [none, value] if right else [value, none]
    return nt(value, jnp.concatenate(both, axis=0), HIGHEST)


def samples_of(x, g, sample_out):
    seqs = sample_out.shape[0]
    length = g.shape[1] // seqs
    for s in range(seqs):
        tokens = slice(s * length, (s + 1) * length)
        sample = nt(x[:, tokens], g[:, tokens], HIGHEST) / length
        sample = sample.astype(jnp.bfloat16).astype(jnp.float32)
        sample_out[s] = jnp.concatenate([sample, sample], axis=1)


def cov_in_kernel(packed_ref, *refs):
    pieces, (packed, x_out, cov_out) = refs[:-3], refs[-3:]
    packed[...] = packed_ref[...]
    x = total(pieces)
    x_out[...] = x
    cov_out[...] = covariance(x, False)


def cov_in(packed, pieces):
    rank, tokens = pieces[0].shape
    return pl.pallas_call(
        cov_in_kernel,
        in_specs=[vmem()] * (1 + len(pieces)),
        out_specs=[vmem()] * 3,
        out_shape=[
            jax.ShapeDtypeStruct(packed.shape, packed.dtype),
            jax.ShapeDtypeStruct((rank, tokens), jnp.float32),
            jax.ShapeDtypeStruct((rank, 2 * rank), jnp.float32),
        ],
        compiler_params=params(16),
        name="cov_in",
    )(packed, *pieces)


def cov_out_kernel(x_ref, cov_ref, *refs):
    pieces, (cov_out, sample_out) = refs[:-2], refs[-2:]
    g = total(pieces)
    cov_out[...] = cov_ref[...] + covariance(g, True)
    samples_of(x_ref[...], g, sample_out)


def cov_out(x, cov, pieces, seqs):
    rank = x.shape[0]
    return pl.pallas_call(
        cov_out_kernel,
        in_specs=[vmem()] * (2 + len(pieces)),
        out_specs=[vmem()] * 2,
        out_shape=[
            jax.ShapeDtypeStruct((rank, 2 * rank), jnp.float32),
            jax.ShapeDtypeStruct((seqs, rank, 2 * rank), jnp.float32),
        ],
        compiler_params=params(16),
        name="cov_out",
    )(x, cov, *pieces)


def scales(steps, spread):
    r = (spread - 1.0) / (spread + 1.0)
    out = []
    for _ in range(steps):
        out.append(2.0 / (2.0 - r * r))
        r = r * r / (2.0 - r * r)
    return out


def halves(value):
    high = value.astype(jnp.bfloat16)
    return high, (value - high.astype(jnp.float32)).astype(jnp.bfloat16)


def stacked(value):
    once = jnp.concatenate(halves(value), axis=1)
    return jnp.concatenate([once, once], axis=0)


def product(left, right):
    lanes = right.shape[1]
    both = nn(jnp.concatenate(halves(left), axis=1), stacked(right))
    return both[:, :lanes] + both[:, lanes:]


def damped_inverses(pair):
    size, both = pair.shape
    left = lax.broadcasted_iota(jnp.int32, pair.shape, 1) < size
    whole = jnp.concatenate([jnp.where(left, pair, 0.0), jnp.where(left, 0.0, pair)], axis=0)
    rows = lax.broadcasted_iota(jnp.int32, whole.shape, 0)
    cols = lax.broadcasted_iota(jnp.int32, whole.shape, 1)
    diagonal = rows == cols
    on_diagonal = jnp.where(diagonal, whole, 0.0)
    unit = jnp.where(
        rows < size, jnp.sum(on_diagonal[:size]) / size, jnp.sum(on_diagonal[size:]) / size
    )
    eye = jnp.where(diagonal, 1.0, 0.0)
    matrix = whole / unit + 0.1 * eye
    low, high = 0.1, size + 0.1
    start = 2.0 / (low + high)
    steps = scales(7, high / low)
    y = matrix * start
    x = (2.0 * start * steps[0]) * eye - (start * steps[0]) * y
    y = steps[0] * (2.0 * y - product(y, y))
    for scale in steps[1:-1]:
        turn = product(jnp.concatenate([x, y], axis=0), y)
        x = scale * (2.0 * x - turn[:both])
        y = scale * (2.0 * y - turn[both:])
    x = steps[-1] * (2.0 * x - product(x, y))
    x = x + product(x, eye - product(matrix, x))
    x = x + product(x, eye - nn(matrix, x, HIGHEST))
    return x / unit


def score_kernel(tokens, place_ref, own_ref, other_ref, sample_ref, *refs):
    pieces, (out, held, half) = refs[:-3], refs[-3:]
    parts = held.shape[0]
    for k, piece in enumerate(pieces):
        held[place_ref[0] ^ k] = piece[...]
    pair = (own_ref[...] + other_ref[...]) / tokens
    size, both = pair.shape
    inverses = damped_inverses(pair)
    samples = [sample_ref[s] for s in range(sample_ref.shape[0])]
    seqs = len(samples)
    blocks = held.shape[1]
    pairs = parts * blocks
    first = jnp.concatenate(halves(inverses[:size, :size]), axis=0)
    none = jnp.zeros_like(first)
    first = jnp.concatenate(
        [jnp.concatenate([first, none], axis=1), jnp.concatenate([none, first], axis=1)], axis=0
    )
    right = inverses[size:]
    second = stacked(jnp.concatenate([pltpu.roll(right, size, 1), right], axis=0))
    for part in range(parts // 2):
        for block in range(0, blocks, 2):
            rows = jnp.concatenate(
                [
                    held[part, block],
                    held[part + parts // 2, block],
                    held[part, block + 1],
                    held[part + parts // 2, block + 1],
                ],
                axis=0,
            )
            result = nt(first, rows)
            for k in range(2):
                two = result[both * k : both * (k + 1)]
                high, middle = halves(two[:size] + two[size:])
                pair = (2 * part + k) * blocks + block
                lanes = slice(pair * both, (pair + 2) * both)
                half[0, :, lanes] = high
                half[1, :, lanes] = middle
    lines = [[] for _ in range(seqs)]
    for pair in range(pairs):
        lanes = slice(pair * both, (pair + 1) * both)
        rows = jnp.concatenate([half[0, :, lanes], half[1, :, lanes]], axis=1)
        result = nn(rows, second)
        result = (result[:, :both] + result[:, both:]).astype(jnp.bfloat16).astype(jnp.float32)
        for s in range(seqs):
            lines[s].append(jnp.sum(result * samples[s], axis=0, keepdims=True))
    lines = jnp.concatenate([line for part in lines for line in part], axis=0)
    shape = (8, both)
    ends = jnp.where(
        (lax.broadcasted_iota(jnp.int32, shape, 1) < size)
        == (lax.broadcasted_iota(jnp.int32, shape, 0) == 0),
        1.0,
        0.0,
    )
    result = nt(ends, lines, HIGHEST)
    for s in range(seqs):
        for k in range(2):
            out[s : s + 1, k * pairs : (k + 1) * pairs] = result[
                k : k + 1, s * pairs : (s + 1) * pairs
            ]


def score(place, own, other, sample, pieces, tokens):
    blocks, rank, both = pieces[0].shape
    parts = len(pieces)
    pairs = parts * blocks
    seqs = sample.shape[0]
    return pl.pallas_call(
        functools.partial(score_kernel, tokens),
        in_specs=[smem()] + [vmem()] * (3 + len(pieces)),
        out_specs=vmem(),
        out_shape=jax.ShapeDtypeStruct((seqs, 2 * pairs), jnp.float32),
        scratch_shapes=[
            pltpu.VMEM((parts, blocks, rank, both), pieces[0].dtype),
            pltpu.VMEM((2, rank, pairs * both), jnp.bfloat16),
        ],
        compiler_params=params(16),
        name="score",
    )(place, own, other, sample, *pieces)


def swap(value, axis, bit):
    return lax.ppermute(value, axis, [(i, i ^ bit) for i in range(lax.axis_size(axis))])


def shift(value, axis, by):
    size = lax.axis_size(axis)
    return lax.ppermute(value, axis, [(i, (i + by) % size) for i in range(size)])


def local_owned(acts, grads, proj_in, proj_out, queries):
    seqs, length, _ = acts.shape
    parts = lax.axis_size("dp")
    tokens = seqs * length * parts
    column = lax.axis_index("tensor").astype(jnp.int32)
    side = (column >= 2).astype(jnp.int32).reshape(1)
    place = lax.axis_index("dp").astype(jnp.int32).reshape(1)
    x_near, x_far, x_again, early = project_in(side, acts, proj_in, grads)
    x_pieces = to_owner(x_near, x_far, x_again)
    near, far, again, packed = project_out(side, grads, proj_out, queries, early)
    pieces = to_owner(near, far, again)
    packed, x, cov = cov_in(packed, x_pieces)
    query_pieces = [packed] + [swap(packed, "dp", bits) for bits in range(1, parts)]
    cov, sample = cov_out(x, cov, pieces, seqs)
    other = jnp.zeros_like(cov)
    bit = 1
    while bit < parts:
        cov = cov if bit == 1 else cov + other
        other = swap(cov, "dp", bit)
        bit *= 2
    scores = score(place, cov, other, sample, query_pieces, tokens)
    above = shift(scores, "tensor", -1)
    opposite = shift(scores, "tensor", 2)
    below = shift(scores, "tensor", 1)
    owner = (column == 1) | (column == 2)
    return jnp.where(owner, scores, opposite) + jnp.where(column >= 2, below, above)


def damp(matrix):
    size = matrix.shape[0]
    shift_by = 0.1 * jnp.trace(matrix) / size
    return matrix + shift_by * jnp.eye(size, dtype=matrix.dtype)


def chol_apply(factor, rhs):
    lower_sol = lax.linalg.triangular_solve(factor, rhs, left_side=True, lower=True)
    return lax.linalg.triangular_solve(
        factor, lower_sol, left_side=True, lower=True, transpose_a=True
    )


def precondition(query, left, right_side):
    count, rank = (query.shape[0], query.shape[1])
    left_fac = jnp.linalg.cholesky(left)
    right_fac = jnp.linalg.cholesky(right_side)
    stacked = jnp.transpose(query, (1, 0, 2)).reshape(rank, count * rank)
    middle = chol_apply(left_fac, stacked).reshape(rank, count, rank)
    turned = jnp.transpose(middle, (2, 1, 0)).reshape(rank, count * rank)
    result = chol_apply(right_fac, turned).reshape(rank, count, rank)
    return jnp.transpose(result, (1, 2, 0))


def diagonal_blocks(whole, rank):
    return jnp.stack([whole[:, 0:rank, 0:rank], whole[:, rank : 2 * rank, rank : 2 * rank]], axis=1)


def local_general(acts, grads, proj_in, proj_out, queries):
    seq_count, length, width_loc = acts.shape
    rank = proj_in.shape[1]
    hidden_loc = grads.shape[3]
    flat = acts.reshape(-1, width_loc)
    xpart = nt(flat, proj_in.reshape(2 * rank, width_loc))
    gpart = jnp.concatenate(
        [nt(grads[layer].reshape(-1, hidden_loc), proj_out[layer]) for layer in range(2)], axis=1
    )
    count = seq_count * length * lax.axis_size("dp")
    xin, gout = lax.psum((xpart, gpart), "tensor")
    in_cov, out_cov = lax.psum((tn(xin, xin, HIGHEST), tn(gout, gout, HIGHEST)), "dp")
    whole = (
        jnp.einsum(
            "sto,sti->soi",
            gout.reshape(seq_count, length, 2 * rank),
            xin.reshape(seq_count, length, 2 * rank),
            precision=HIGHEST,
        )
        / length
    )
    samples = diagonal_blocks(whole, rank)
    in_cov = in_cov / count
    out_cov = out_cov / count
    precond = []
    for layer in range(2):
        low = layer * rank
        damped_in = damp(in_cov[low : low + rank, low : low + rank])
        damped_out = damp(out_cov[low : low + rank, low : low + rank])
        precond.append(precondition(queries[:, layer].astype(jnp.float32), damped_out, damped_in))
    query_count = queries.shape[0]
    query_b = jnp.stack(precond, axis=1).astype(jnp.bfloat16).reshape(query_count, -1)
    sample_b = samples.astype(jnp.bfloat16).reshape(seq_count, -1)
    return nt(sample_b, lax.all_gather(query_b, "dp", axis=0, tiled=True))


def local(acts, grads, proj_in, proj_out, queries):
    parts = lax.axis_size("dp")
    even = parts > 1 and parts & (parts - 1) == 0
    if lax.axis_size("tensor") == 4 and even and queries.shape[0] % 4 == 0:
        return local_owned(acts, grads, proj_in, proj_out, queries)
    return local_general(acts, grads, proj_in, proj_out, queries)


def solution(mesh):
    placed = (
        P(("groups", "dp"), None, "tensor"),
        P(None, ("groups", "dp"), None, "tensor"),
        P(None, None, "tensor"),
        P(None, None, "tensor"),
        P("dp", None, None, None),
    )
    return jax.shard_map(
        local, mesh=mesh, in_specs=placed, out_specs=P(("groups", "dp"), None), check_vma=False
    )
```
